512 devices in a mesh: dp: 32 (over z, x), proto: 16 (over y, core).
Axes of the slice: x: 4, y: 8, z: 8, core: 2. Of those that a mesh axis runs over, the one named last changes fastest.
Arguments:
- student_patches: bfloat16 [512, 256, 256], P(('dp', 'proto')), may hold values from -9 to 9
- teacher_patches: bfloat16 [512, 256, 256], P(('dp', 'proto')), may hold values from -9 to 9
- mask_order: int32 [512, 256], P(('dp', 'proto')), may hold values from 0 to 255, each once within a row
- counts: int32 [32, 16], P('dp', 'proto'), may hold values from 1 to 72, 384 in all within a row
- student_protos: bfloat16 [256, 65536], P(None, 'proto'), may hold values from -0.375 to 0.375
- teacher_protos: bfloat16 [256, 65536], P(None, 'proto'), may hold values from -0.375 to 0.375
Outputs:
- student_grad: bfloat16 [512, 256, 256], P(('dp', 'proto'))
- image_loss: float32 [32, 16], P('dp', 'proto')
The draws below stay inside these ranges and needn't reach their ends.
Inputs may be any that keep to these rules, and one draw needn't show every extreme that they name: Each dp index's 16 counts sum to 384, and the largest of them is 72. `mask_order`: each image's row names every patch once; its first counts entries are that image's masked patches.
All inputs are finite; a program needn't handle non-finite values. No bound on the sum of `counts` on one device may be relied on, other than what follows from the above.
Results may differ from the reference program's by a relative error of at most 0.02.
Values may be sent and summed in bfloat16 or wider, within the bound.
No kernel may reach another device: no remote copies, remote signals or barrier semaphores. Data moves between devices by JAX's collectives and lax.ppermute only.
A program may use at most 64 MiB of HBM per device.

```python
import math
import jax
import jax.numpy as jnp
import numpy as np
from jax import lax

PATCHES = 256
BOT = 256
PROTOS = 65536
MASK_DEV = 24
ITERS = 3
MOST = 72
IMAGES = 512
N_DP = 32
N_PROTO = 16


def draw_student_patches(key, part):
    key = jax.random.fold_in(key, 11)
    return jnp.clip(jax.random.normal(key, (IMAGES, PATCHES, BOT), jnp.float32), -6.0, 6.0).astype(jnp.bfloat16)


def draw_teacher_patches(key, part):
    key = jax.random.fold_in(key, 23)
    return jnp.clip(jax.random.normal(key, (IMAGES, PATCHES, BOT), jnp.float32), -6.0, 6.0).astype(jnp.bfloat16)


def block_levels(stream_key, extent, shards, least, high):
    loudness = 1.0
    for position, blocks in shards:
        draws = jax.random.uniform(jax.random.fold_in(jax.random.fold_in(stream_key, 6), position), (blocks,), jnp.float32, least / len(shards), high / len(shards))
        loudness = loudness * jnp.repeat(jnp.exp(draws), extent[position] // blocks).reshape((-1,) + (1,) * (len(extent) - 1 - position))
    return loudness


def length_profile(amount, total, reach, slope):
    portions = [(1 << 20) // math.isqrt(rank ** slope) + 1 for rank in range(2, amount + 1)]
    rest, given = total - reach - (amount - 1), [1] * (amount - 1)
    while rest > 0:
        candidates = [i for i in range(amount - 1) if given[i] < reach]
        whole, remaining = sum([portions[i] for i in candidates]), rest
        for i in candidates:
            addition = min(reach - given[i], max(1, remaining * portions[i] // whole), rest)
            given[i] = given[i] + addition
            rest = rest - addition
    return np.array([reach] + given)


def ragged(stream_key, amount, total, limit, lean):
    if amount == 2:
        one = jax.random.randint(stream_key, (), max(1, total - limit), min(limit, total - 1) + 1)
        return jnp.stack([one, total - one])
    sizes = jnp.asarray(length_profile(amount, total, limit, lean), jnp.int32)
    couples = (amount - 1) // 2
    donor, receiver = sizes[1:1 + 2 * couples:2], sizes[2:2 + 2 * couples:2]
    slack = jnp.minimum(donor - 1, limit - receiver)
    passed = jax.random.randint(jax.random.fold_in(stream_key, 1), (couples,), 0, 1 << 20) % (slack + 1)
    sizes = sizes.at[1:1 + 2 * couples:2].set(donor - passed).at[2:2 + 2 * couples:2].set(receiver + passed)
    return sizes[jax.random.permutation(jax.random.fold_in(stream_key, 2), amount)]


def bell_draw(rng, extent, width, most, pieces=(), kind=jnp.bfloat16):
    entries = jax.random.normal(rng, extent, jnp.float32) * width
    if len(pieces) > 0:
        entries = block_levels(rng, extent, pieces, -0.22, 0.18) * entries
    return jnp.clip(entries, min=-most, max=most).astype(kind)


def setup_inputs(seed: int = 0) -> dict:
    key_list = jax.random.split(jax.random.key(seed), 7)
    return {
        "student_patches": draw_student_patches(jax.random.fold_in(key_list[6], 71), 0),
        "teacher_patches": draw_teacher_patches(jax.random.fold_in(key_list[6], 71), 0),
        "mask_order": jax.vmap(lambda own: jax.random.permutation(own, PATCHES))(jax.random.split(key_list[2], IMAGES)).reshape((IMAGES, PATCHES)).astype(jnp.int32),
        "counts": jax.vmap(lambda own: ragged(own, N_PROTO, MASK_DEV * N_PROTO, MOST, 2))(jax.random.split(key_list[3], N_DP)).reshape((N_DP, N_PROTO)).astype(jnp.int32),
        "student_protos": bell_draw(key_list[4], (BOT, PROTOS), BOT ** -0.5, 0.375, ((1, 16),)),
        "teacher_protos": bell_draw(key_list[5], (BOT, PROTOS), BOT ** -0.5, 0.375, ((1, 16),)),
    }


teach_temp = 0.07
stud_temp = 0.1


def compact_group(group_sizes, group_order):
    group_ends = jnp.cumsum(group_sizes).astype(jnp.int32)
    group_starts = group_ends - group_sizes
    row_index = jnp.arange(MASK_DEV * N_PROTO, dtype=jnp.int32)
    holder = jnp.sum((row_index[:, None] >= group_ends[None, :]).astype(jnp.int32), axis=1)
    within = row_index - group_starts[holder]
    return holder, group_order[holder, within]


def reference(student_patches, teacher_patches, mask_order, counts, student_protos, teacher_protos):
    orders = mask_order.reshape(N_DP, N_PROTO, PATCHES)
    holders, patch_ids = jax.vmap(compact_group)(counts, orders)
    image_of_row = (jnp.arange(N_DP, dtype=jnp.int32)[:, None] * N_PROTO + holders).astype(jnp.int32)
    student_rows = student_patches[image_of_row, patch_ids]
    teacher_rows = teacher_patches[image_of_row, patch_ids]
    groups = jnp.arange(N_DP, dtype=jnp.int32)

    def teacher_logits(group):
        return jnp.dot(teacher_rows[group], teacher_protos, preferred_element_type=jnp.float32) / teach_temp

    def merge_columns(carry, values):
        highest, totals = carry
        newest = jnp.maximum(highest, jnp.max(values, axis=0))
        totals = totals * jnp.exp(highest - newest) + jnp.sum(jnp.exp(values - newest[None, :]), axis=0)
        return (newest, totals)

    start_stats = (jnp.full((PROTOS,), -1e30, jnp.float32), jnp.zeros((PROTOS,), jnp.float32))

    def first_pass(carry, group):
        return merge_columns(carry, teacher_logits(group)), None

    (highest, totals), unused = lax.scan(first_pass, start_stats, groups)
    col_potential = -(highest + jnp.log(totals))

    for sweep in range(ITERS - 1):
        def later_pass(carry, group, col_now=col_potential):
            logits = teacher_logits(group)
            row_now = -jax.nn.logsumexp(logits + col_now[None, :], axis=1)
            return merge_columns(carry, logits + row_now[:, None]), None

        (highest, totals), unused = lax.scan(later_pass, start_stats, groups)
        col_potential = -(highest + jnp.log(totals))

    def finish(group):
        shifted = teacher_logits(group) + col_potential[None, :]
        row_potential = -jax.nn.logsumexp(shifted, axis=1)
        target = jnp.exp(shifted + row_potential[:, None])
        student_logits = jnp.dot(student_rows[group], student_protos, preferred_element_type=jnp.float32) / stud_temp
        student_lse = jax.nn.logsumexp(student_logits, axis=1)
        cross = student_lse - jnp.sum(target * student_logits, axis=1)
        difference = ((jnp.exp(student_logits - student_lse[:, None]) - target) / stud_temp).astype(jnp.bfloat16)
        row_grad = jnp.dot(difference, student_protos.T, preferred_element_type=jnp.float32).astype(jnp.bfloat16)
        member = holders[group][:, None] == jnp.arange(N_PROTO, dtype=jnp.int32)[None, :]
        losses = jnp.sum(jnp.where(member, cross[:, None], 0.0), axis=0) / counts[group].astype(jnp.float32)
        return row_grad, losses

    row_grads, image_loss = lax.map(finish, groups)
    student_grad = jnp.zeros((IMAGES, PATCHES, BOT), jnp.bfloat16).at[image_of_row, patch_ids].set(row_grads)
    return student_grad, image_loss
```

```python
import jax
import jax.numpy as jnp
from jax import lax
from jax.sharding import PartitionSpec as P

MASK_DEV = 24
MOST = 72
TEACH = 1.0 / 0.07
STUD = 1.0 / 0.1
F32 = jnp.float32
BF16 = jnp.bfloat16


def lse(values, axis):
    high = jnp.max(values, axis=axis, keepdims=True)
    return jnp.squeeze(high, axis) + jnp.log(jnp.sum(jnp.exp(values - high), axis=axis))


def share(values, axis):
    peers = lax.axis_size(axis)
    return lax.all_to_all(jnp.broadcast_to(values[None], (peers,) + values.shape), axis, 0, 0, tiled=True)


def body(student_patches, teacher_patches, mask_order, counts, student_protos, teacher_protos):
    width = lax.axis_size("proto")
    own_index = lax.axis_index("proto")
    row_total = MASK_DEV * width
    own_count = counts[0, 0]
    order = mask_order[0, :MOST]
    picked_teacher = teacher_patches[0][order]
    picked_student = student_patches[0][order]
    tail = jnp.broadcast_to(own_count.astype(BF16), (8, picked_teacher.shape[1]))
    gathered = lax.all_gather(jnp.concatenate([picked_teacher, tail], axis=0), "proto", axis=0, tiled=False)
    padded = jnp.pad(picked_student, ((0, 64), (0, 0)))
    gathered_student = lax.all_gather(padded, "proto", axis=0, tiled=False)[:, :MOST].reshape(width * MOST, -1)
    sizes = gathered[:, MOST, 0].astype(jnp.int32)
    ends = jnp.cumsum(sizes)
    starts = ends - sizes
    peers = jnp.arange(width, dtype=jnp.int32)
    own_start = jnp.sum(jnp.where(peers == own_index, starts, 0))
    row_index = jnp.arange(row_total, dtype=jnp.int32)
    holder = jnp.sum((row_index[:, None] >= ends[None, :]).astype(jnp.int32), axis=1)
    member = holder[:, None] == peers[None, :]
    within = row_index - jnp.sum(jnp.where(member, starts[None, :], 0), axis=1)
    teacher_rows = gathered[:, :MOST].reshape(width * MOST, -1)[holder * MOST + within]
    student_rows = gathered_student[holder * MOST + within]
    slots = jnp.clip(starts[:, None] + jnp.arange(MOST, dtype=jnp.int32)[None, :], 0, row_total - 1).reshape(-1)

    logits = jnp.dot(teacher_rows, teacher_protos, preferred_element_type=F32) * TEACH
    col = -lse(share(lse(logits, 0), "dp"), 0)

    stud = jnp.dot(student_rows, student_protos, preferred_element_type=F32) * STUD
    stud_high = jnp.max(stud, axis=1)
    stud_exp = jnp.exp(stud - stud_high[:, None])
    stud_lse = stud_high + jnp.log(jnp.sum(stud_exp, axis=1))
    stud_sum = lax.dot_general(stud_exp.astype(BF16), student_protos, (((1,), (1,)), ((), ())), preferred_element_type=F32)

    shifted = logits + col[None, :]
    high = jnp.max(shifted, axis=1)
    exact = jnp.exp(shifted - high[:, None])
    kernel = exact.astype(BF16)
    own_lse = high + jnp.log(jnp.sum(exact, axis=1))
    both = share(jnp.concatenate([own_lse.reshape(-1, 128), stud_lse.reshape(-1, 128)], axis=0), "proto")
    both = lse(both, 0).reshape(2, row_total)
    row_lse, student_lse = both[0], both[1]
    row_scale = jnp.exp(high - row_lse)

    stud_part = (stud_sum * jnp.exp(stud_high - student_lse)[:, None]).astype(BF16)
    stud_back = lax.psum_scatter(stud_part[slots], "proto", scatter_dimension=0, tiled=True)

    def columns(row_scale):
        sums = jnp.sum(kernel.astype(F32) * row_scale[:, None], axis=0)
        return 1.0 / jnp.sum(share(sums.astype(BF16), "dp").astype(F32), axis=0)

    col_scale = columns(row_scale)
    row_sums = row_scale * jnp.sum(kernel.astype(F32) * col_scale[None, :], axis=1)
    row_scale = row_scale / jnp.sum(share(row_sums.reshape(-1, 128), "proto"), axis=0).reshape(-1)
    col_scale = columns(row_scale)
    weights = (kernel.astype(F32) * col_scale[None, :]).astype(BF16)
    teach_sum = lax.dot_general(weights, student_protos, (((1,), (1,)), ((), ())), preferred_element_type=F32)
    total = row_scale * jnp.sum(weights.astype(F32), axis=1)
    teach_part = (teach_sum * row_scale[:, None]).astype(BF16)[slots].reshape(width, MOST, -1)
    total_slots = total[slots].reshape(width, MOST)
    total_high = total_slots.astype(BF16)
    total_low = (total_slots - total_high.astype(F32)).astype(BF16)
    wide = jnp.pad(jnp.stack([total_high, total_low], axis=1), ((0, 0), (0, 6), (0, teach_part.shape[2] - MOST)))
    back = lax.all_to_all(jnp.concatenate([teach_part, wide], axis=1), "proto", 0, 0, tiled=True)
    back = jnp.sum(back.astype(F32), axis=0)
    row_norm = back[MOST, :MOST] + back[MOST + 1, :MOST]
    slot = jnp.arange(MOST, dtype=jnp.int32)
    used = slot < own_count
    mean_proto = back[:MOST] / jnp.where(used, row_norm, 1.0)[:, None]
    own_lse_rows = student_lse[jnp.clip(own_start + slot, 0, row_total - 1)]
    cross = own_lse_rows - STUD * jnp.sum(picked_student.astype(F32) * mean_proto, axis=1)
    own_loss = jnp.sum(jnp.where(used, cross, 0.0)) / own_count.astype(F32)
    own_rows = jnp.where(used[:, None], STUD * (stud_back.astype(F32) - mean_proto), 0.0)
    student_grad = (
        jnp.zeros((student_patches.shape[1], student_patches.shape[2]), BF16).at[order].set(own_rows.astype(BF16))
    )
    return (student_grad[None], own_loss.reshape(1, 1))


def solution(mesh):
    placed = (
        P(("dp", "proto"), None, None),
        P(("dp", "proto"), None, None),
        P(("dp", "proto"), None),
        P("dp", "proto"),
        P(None, "proto"),
        P(None, "proto"),
    )
    return jax.shard_map(
        body,
        mesh=mesh,
        in_specs=placed,
        out_specs=(P(("dp", "proto"), None, None), P("dp", "proto")),
        check_vma=False,
    )
```

```python
import functools

import jax
import jax.numpy as jnp
from jax import lax
from jax.experimental import pallas as pl
from jax.experimental.pallas import tpu as pltpu
from jax.sharding import PartitionSpec as P

MASK_DEV = 24
MOST = 72
SLOT = 80
TEACH = 1.0 / 0.07
STUD = 1.0 / 0.1
F32 = jnp.float32
BF16 = jnp.bfloat16
LANES = 128
BLOCK = 1024
LIMIT = 40 << 20
VMEM = pl.BlockSpec(memory_space=pltpu.VMEM)
SMEM = pl.BlockSpec(memory_space=pltpu.SMEM)


def call(kernel, out_shape, *args, grid=None, in_specs=None, out_specs=None, scratch=(), flops=0, moved=0):
    out_shape = [jax.ShapeDtypeStruct(s, d) for s, d in out_shape]
    extra = {} if grid is None else {"grid": grid}
    return pl.pallas_call(
        kernel,
        out_shape=out_shape,
        in_specs=[VMEM] * len(args) if in_specs is None else in_specs,
        out_specs=[VMEM] * len(out_shape) if out_specs is None else out_specs,
        scratch_shapes=list(scratch),
        compiler_params=pltpu.CompilerParams(vmem_limit_bytes=LIMIT),
        cost_estimate=pl.CostEstimate(flops=flops, bytes_accessed=moved, transcendentals=0),
        **extra,
    )(*args)


def iota(shape, dim):
    return lax.broadcasted_iota(jnp.int32, shape, dim)


def eye():
    return iota((LANES, LANES), 0) == iota((LANES, LANES), 1)


def to_lanes(column):
    parts = []
    for b in range(column.shape[0] // LANES):
        part = jnp.broadcast_to(column[b * LANES : (b + 1) * LANES], (LANES, LANES))
        parts.append(jnp.sum(jnp.where(eye(), part, 0.0), axis=0, keepdims=True))
    return jnp.concatenate(parts, axis=0)


def to_column(lanes):
    parts = []
    for b in range(lanes.shape[0]):
        part = jnp.broadcast_to(lanes[b : b + 1], (LANES, LANES))
        parts.append(jnp.sum(jnp.where(eye(), part, 0.0), axis=1, keepdims=True))
    return jnp.concatenate(parts, axis=0)


def pick_kernel(teacher_ref, student_ref, order_ref, count_ref, teacher_out, student_out):
    patches, width = teacher_ref.shape
    order = jnp.broadcast_to(order_ref[:, :LANES], (patches, LANES))
    chosen = (iota((patches, LANES), 0) == order).astype(BF16)
    dims = (((0,), (0,)), ((), ()))
    picked = lax.dot_general(chosen, teacher_ref[...], dims, preferred_element_type=F32)
    count = jnp.full((SLOT - MOST, width), count_ref[0, 0], jnp.int32).astype(F32)
    teacher_out[...] = jnp.concatenate([picked[:MOST], count], axis=0).astype(BF16)
    picked = lax.dot_general(chosen, student_ref[...], dims, preferred_element_type=F32)
    student_out[...] = picked.astype(BF16)


def compact(gathered, starts, counts, rows):
    total = gathered.shape[0]
    images = starts.shape[0]
    slots = total // images
    lane, image = iota((images, total), 1), iota((images, total), 0)
    within = lane - image * slots
    member = jnp.logical_and(within >= 0, within < slots)
    used = jnp.logical_and(member, within.astype(F32) < counts[:, :1])
    row = jnp.sum(jnp.where(used, starts[:, :1] + within.astype(F32) + 1.0, 0.0), axis=0, keepdims=True) - 1.0
    chosen = (iota((rows, total), 0).astype(F32) == row).astype(BF16)
    return jnp.dot(chosen, gathered, preferred_element_type=F32).astype(BF16)


def spread(starts, counts, slots, rows):
    images = starts.shape[0]
    shape = (images, slots, rows)
    within = iota(shape, 1)
    row = (iota(shape, 2) - within).astype(F32) - starts[:, :1].reshape(images, 1, 1)
    used = jnp.logical_and(row == 0.0, within.astype(F32) < counts[:, :1].reshape(images, 1, 1))
    return used.astype(F32).astype(BF16).reshape(images * slots, rows)


def column_kernel(gathered_ref, protos_ref, share_ref, rows_ref, places_ref):
    images = gathered_ref.shape[0]
    rows = rows_ref.shape[0]

    @pl.when(pl.program_id(0) == 0)
    def _():
        counts = gathered_ref[:, MOST:MOST + 8, :LANES].astype(F32)[:, 0]
        before = (iota((images, images), 1) < iota((images, images), 0)).astype(BF16)
        starts = jnp.dot(before, counts.astype(BF16), preferred_element_type=F32)
        places_ref[0] = starts
        places_ref[1] = counts
        flat = gathered_ref[...].reshape(images * SLOT, gathered_ref.shape[2])
        rows_ref[...] = compact(flat, starts, counts, rows)

    logits = jnp.dot(rows_ref[...], protos_ref[...], preferred_element_type=F32) * TEACH
    high = jnp.max(logits, axis=0, keepdims=True)
    total = jnp.sum(jnp.exp(logits - high), axis=0, keepdims=True)
    share_ref[...] = jnp.broadcast_to(high + jnp.log(total), share_ref.shape)


def row_kernel(shares_ref, rows_ref, protos_ref, student_lse_ref, matrix_ref, high_ref, share_ref, sums):
    step = pl.program_id(0)
    shares = shares_ref[...]
    top = jnp.max(shares, axis=0, keepdims=True)
    column = top + jnp.log(jnp.sum(jnp.exp(shares - top), axis=0, keepdims=True))
    logits = jnp.dot(rows_ref[...], protos_ref[...], preferred_element_type=F32) * TEACH
    shifted = logits - column
    high = jnp.max(shifted, axis=1, keepdims=True)
    exact = jnp.exp(shifted - high)
    matrix_ref[...] = exact.astype(BF16)
    high_ref[step] = high
    sums[step] = jnp.sum(exact, axis=1, keepdims=True)

    @pl.when(step == pl.num_programs(0) - 1)
    def _():
        highs = high_ref[...]
        top = jnp.max(highs, axis=0)
        total = jnp.sum(jnp.exp(highs - top[None]) * sums[...], axis=0)
        own = to_lanes(top + jnp.log(total))
        peers, depth = share_ref.shape[0], share_ref.shape[1]
        chunk = jnp.concatenate([own, student_lse_ref[...], jnp.zeros((depth - 2 * own.shape[0], LANES), F32)], axis=0)
        share_ref[...] = jnp.broadcast_to(chunk[None], share_ref.shape)


def merged(shares):
    top = jnp.max(shares, axis=0)
    return top + jnp.log(jnp.sum(jnp.exp(shares - top[None]), axis=0))


def column_sums(matrix_ref, scale, share_ref):
    sums = jnp.sum(matrix_ref[...].astype(F32) * scale, axis=0, keepdims=True)
    share_ref[...] = jnp.broadcast_to(sums, share_ref.shape).astype(share_ref.dtype)


def first_column_kernel(shares_ref, high_ref, matrix_ref, share_ref, scale_ref, student_lse_ref):
    step = pl.program_id(0)
    lines = student_lse_ref.shape[0]

    @pl.when(step == 0)
    def _():
        both = merged(shares_ref[...][:, : 2 * lines])
        student_lse_ref[...] = both[lines:]
        scale_ref[...] = jnp.exp(high_ref[...] - to_column(both[:lines])[None])

    column_sums(matrix_ref, scale_ref[step], share_ref)


def later_column_kernel(shares_ref, scale_in_ref, matrix_ref, share_ref, scale_ref):
    step = pl.program_id(0)

    @pl.when(step == 0)
    def _():
        lines = scale_ref.shape[1] // LANES
        total = to_column(jnp.sum(shares_ref[...][:, :lines], axis=0))
        scale_ref[...] = scale_in_ref[...] / total[None]

    column_sums(matrix_ref, scale_ref[step], share_ref)


def later_row_kernel(shares_ref, scale_ref, matrix_ref, share_ref, sums):
    step = pl.program_id(0)
    inverse = 1.0 / jnp.sum(shares_ref[...].astype(F32), axis=0, keepdims=True)
    part = scale_ref[step] * jnp.sum(matrix_ref[...].astype(F32) * inverse, axis=1, keepdims=True)

    @pl.when(step == 0)
    def _():
        sums[...] = part

    @pl.when(step > 0)
    def _():
        sums[...] += part

    @pl.when(step == pl.num_programs(0) - 1)
    def _():
        own = to_lanes(sums[...])
        chunk = jnp.concatenate([own, jnp.zeros((share_ref.shape[1] - own.shape[0], LANES), F32)], axis=0)
        share_ref[...] = jnp.broadcast_to(chunk[None], share_ref.shape)


def target_kernel(shares_ref, scale_ref, matrix_ref, protos_ref, places_ref, out_ref, sums, total):
    step = pl.program_id(0)
    scale = scale_ref[step]
    inverse = 1.0 / jnp.sum(shares_ref[...].astype(F32), axis=0, keepdims=True)
    weights = matrix_ref[...].astype(F32) * inverse
    narrow = weights.astype(BF16)
    part = scale * lax.dot_general(narrow, protos_ref[...], (((1,), (1,)), ((), ())), preferred_element_type=F32)
    mass = scale * jnp.sum(narrow.astype(F32), axis=1, keepdims=True)

    @pl.when(step == 0)
    def _():
        sums[...] = part
        total[...] = mass

    @pl.when(step > 0)
    def _():
        sums[...] += part
        total[...] += mass

    @pl.when(step == pl.num_programs(0) - 1)
    def _():
        rows, width = sums.shape
        mass_high = jnp.broadcast_to(total[...], (rows, LANES)).astype(BF16)
        mass_low = (jnp.broadcast_to(total[...], (rows, LANES)) - mass_high.astype(F32)).astype(BF16)
        sent = jnp.concatenate([sums[...].astype(BF16), mass_high, mass_low], axis=1)
        images = out_ref.shape[0]
        chosen = spread(places_ref[0], places_ref[1], SLOT, rows)
        packed = jnp.dot(chosen, sent, preferred_element_type=F32).reshape(images, SLOT, width + 2 * LANES)
        same = iota((1, SLOT, LANES), 1) == iota((1, SLOT, LANES), 2)
        high = jnp.sum(jnp.where(same, packed[:, :, width : width + LANES], 0.0), axis=1, keepdims=True)
        low = jnp.sum(jnp.where(same, packed[:, :, width + LANES :], 0.0), axis=1, keepdims=True)
        filler = jnp.zeros((images, 1, width - LANES), F32)
        out_ref[:, :MOST] = packed[:, :MOST, :width].astype(BF16)
        numbers = jnp.concatenate(
            [
                jnp.concatenate([high, filler], axis=2),
                jnp.concatenate([low, filler], axis=2),
                jnp.zeros((images, SLOT - MOST - 2, width), F32),
            ],
            axis=1,
        )
        out_ref[:, MOST:] = numbers.astype(BF16)


def student_kernel(gathered_ref, places_ref, protos_ref, sums_ref, high_ref, lse_ref, rows_ref, total):
    step = pl.program_id(0)
    rows = rows_ref.shape[0]

    @pl.when(step == 0)
    def _():
        images, slots, width = gathered_ref.shape
        flat = gathered_ref[...].reshape(images * slots, width)
        rows_ref[...] = compact(flat, places_ref[0], places_ref[1], rows)
        high_ref[...] = jnp.full(high_ref.shape, -1e30, F32)
        total[...] = jnp.zeros(total.shape, F32)
        sums_ref[...] = jnp.zeros(sums_ref.shape, F32)

    protos = protos_ref[...]
    logits = jnp.dot(rows_ref[...], protos, preferred_element_type=F32) * STUD
    before = high_ref[...]
    high = jnp.maximum(before, jnp.max(logits, axis=1, keepdims=True))
    shrink = jnp.exp(before - high)
    exact = jnp.exp(logits - high)
    total[...] = total[...] * shrink + jnp.sum(exact, axis=1, keepdims=True)
    part = lax.dot_general(exact.astype(BF16), protos, (((1,), (1,)), ((), ())), preferred_element_type=F32)
    sums_ref[...] = sums_ref[...] * shrink + part
    high_ref[...] = high

    @pl.when(step == pl.num_programs(0) - 1)
    def _():
        lse_ref[...] = to_lanes(high_ref[...] + jnp.log(total[...]))


def student_pack_kernel(sums_ref, high_ref, lse_ref, places_ref, out_ref):
    rows = sums_ref.shape[0]
    images = places_ref.shape[1]
    sent = (sums_ref[...] * jnp.exp(high_ref[...] - to_column(lse_ref[...]))).astype(BF16)
    chosen = spread(places_ref[0], places_ref[1], out_ref.shape[0] // images, rows)
    out_ref[...] = jnp.dot(chosen, sent, preferred_element_type=F32).astype(BF16)


def finish_kernel(back_ref, student_ref, picked_ref, lse_ref, places_ref, order_ref, index_ref, grad_ref, loss_ref):
    patches, width = grad_ref.shape
    lines = lse_ref.shape[0]
    back = jnp.sum(back_ref[...].astype(F32), axis=0)
    images = places_ref.shape[1]
    own = iota((images, LANES), 0) == index_ref[0, 0]
    start = jnp.sum(jnp.where(own, places_ref[0], 0.0), axis=0, keepdims=True)
    count = jnp.sum(jnp.where(own, places_ref[1], 0.0), axis=0, keepdims=True)
    mass = to_column((back[MOST : MOST + 1] + back[MOST + 1 : MOST + 2])[:, :LANES])[:MOST]
    used = iota((MOST, 1), 0).astype(F32) < count[:, :1]
    mean = back[:MOST] / jnp.where(used, mass, 1.0)
    lse_row = jnp.concatenate([lse_ref[b : b + 1] for b in range(lines)], axis=1)
    shape = (MOST, lines * LANES)
    here = (iota(shape, 1) - iota(shape, 0)).astype(F32) == start[:, :1]
    own_lse = jnp.sum(jnp.where(here, lse_row, 0.0), axis=1, keepdims=True)
    cross = own_lse - STUD * jnp.sum(picked_ref[:MOST].astype(F32) * mean, axis=1, keepdims=True)
    cross = jnp.sum(jnp.where(used, cross, 0.0), axis=0, keepdims=True)
    loss_ref[...] = cross / count[:, :1]
    rows = jnp.where(used, STUD * (student_ref[...].astype(F32) - mean), 0.0)
    rows = jnp.concatenate([rows, jnp.zeros((LANES - MOST, width), F32)], axis=0).astype(BF16)
    order = jnp.broadcast_to(order_ref[:, :LANES], (patches, LANES))
    chosen = (iota((patches, LANES), 0) == order).astype(BF16)
    grad_ref[...] = jnp.dot(chosen, rows, preferred_element_type=F32).astype(BF16)


def body(student_patches, teacher_patches, mask_order, counts, student_protos, teacher_protos):
    width = lax.axis_size("proto")
    groups = lax.axis_size("dp")
    rows = MASK_DEV * width
    lines = rows // LANES
    patches, bot = student_patches.shape[1:]
    protos = student_protos.shape[1]
    steps = protos // BLOCK
    depth = 8
    index = lax.axis_index("proto").astype(jnp.int32).reshape(1, 1)
    over = functools.partial(lax.all_to_all, split_axis=0, concat_axis=0, tiled=True)
    wide = pl.BlockSpec((bot, BLOCK), lambda k: (0, k))
    peer = pl.BlockSpec((groups, BLOCK), lambda k: (0, k))
    square = pl.BlockSpec((rows, BLOCK), lambda k: (0, k))
    grid = (steps,)
    dot = 2 * rows * protos * bot
    column = pltpu.VMEM((rows, 1), F32)

    teacher_sent, student_sent = call(
        pick_kernel,
        [((SLOT, bot), BF16), ((LANES, bot), BF16)],
        teacher_patches[0],
        student_patches[0],
        mask_order,
        counts,
        in_specs=[VMEM, VMEM, VMEM, SMEM],
        moved=4 * patches * bot,
    )
    gathered_student = lax.all_gather(student_sent, "proto", axis=0, tiled=False)
    gathered = lax.all_gather(teacher_sent, "proto", axis=0, tiled=False)
    share, teacher_rows, places = call(
        column_kernel,
        [((groups, protos), F32), ((rows, bot), BF16), ((2, width, LANES), F32)],
        gathered,
        teacher_protos,
        grid=grid,
        in_specs=[VMEM, wide],
        out_specs=[peer, VMEM, VMEM],
        flops=dot,
        moved=2 * bot * protos,
    )
    shares = over(share, "dp")
    student_sum, student_high, student_lse = call(
        student_kernel,
        [((rows, bot), F32), ((rows, 1), F32), ((lines, LANES), F32)],
        gathered_student,
        places,
        student_protos,
        grid=grid,
        in_specs=[VMEM, VMEM, wide],
        scratch=[pltpu.VMEM((rows, bot), BF16), column],
        flops=2 * dot,
        moved=2 * bot * protos,
    )
    matrix, high, share = call(
        row_kernel,
        [((rows, protos), BF16), ((steps, rows, 1), F32), ((width, depth, LANES), F32)],
        shares,
        teacher_rows,
        teacher_protos,
        student_lse,
        grid=grid,
        in_specs=[peer, VMEM, wide, VMEM],
        out_specs=[square, VMEM, VMEM],
        scratch=[pltpu.VMEM((steps, rows, 1), F32)],
        flops=dot,
        moved=2 * bot * protos + 2 * rows * protos,
    )
    shares = over(share, "proto")
    share, scale, student_lse = call(
        first_column_kernel,
        [((groups, protos), BF16), ((steps, rows, 1), F32), ((lines, LANES), F32)],
        shares,
        high,
        matrix,
        grid=grid,
        in_specs=[VMEM, VMEM, square],
        out_specs=[peer, VMEM, VMEM],
        moved=2 * rows * protos,
    )
    student_part = call(
        student_pack_kernel,
        [((width * MOST, bot), BF16)],
        student_sum,
        student_high,
        student_lse,
        places,
        flops=2 * width * MOST * rows * bot,
    )[0]
    student_back = lax.psum_scatter(student_part, "proto", scatter_dimension=0, tiled=True)
    shares = over(share, "dp")
    share = call(
        later_row_kernel,
        [((width, depth, LANES), F32)],
        shares,
        scale,
        matrix,
        grid=grid,
        in_specs=[peer, VMEM, square],
        scratch=[column],
        moved=2 * rows * protos,
    )[0]
    shares = over(share, "proto")
    share, scale = call(
        later_column_kernel,
        [((groups, protos), BF16), ((steps, rows, 1), F32)],
        shares,
        scale,
        matrix,
        grid=grid,
        in_specs=[VMEM, VMEM, square],
        out_specs=[peer, VMEM],
        moved=2 * rows * protos,
    )
    shares = over(share, "dp")
    sent = call(
        target_kernel,
        [((width, SLOT, bot), BF16)],
        shares,
        scale,
        matrix,
        student_protos,
        places,
        grid=grid,
        in_specs=[peer, VMEM, square, wide, VMEM],
        scratch=[pltpu.VMEM((rows, bot), F32), column],
        flops=dot,
        moved=2 * rows * protos,
    )[0]
    back = over(sent, "proto")
    student_grad, image_loss = call(
        finish_kernel,
        [((patches, bot), BF16), ((1, 1), F32)],
        back,
        student_back,
        student_sent,
        student_lse,
        places,
        mask_order,
        index,
        in_specs=[VMEM, VMEM, VMEM, VMEM, VMEM, VMEM, SMEM],
        moved=2 * patches * bot,
    )
    return (student_grad[None], image_loss)


def solution(mesh):
    placed = (
        P(("dp", "proto"), None, None),
        P(("dp", "proto"), None, None),
        P(("dp", "proto"), None),
        P("dp", "proto"),
        P(None, "proto"),
        P(None, "proto"),
    )
    return jax.shard_map(
        body,
        mesh=mesh,
        in_specs=placed,
        out_specs=(P(("dp", "proto"), None, None), P("dp", "proto")),
        check_vma=False,
    )
```

```python
import functools

import jax
import jax.numpy as jnp
from jax import lax
from jax.experimental import pallas as pl
from jax.experimental.pallas import tpu as pltpu
from jax.sharding import PartitionSpec as P

MASK_DEV = 24
MOST = 72
SLOT = 80
TEACH = 1.0 / 0.07
STUD = 1.0 / 0.1
F32 = jnp.float32
BF16 = jnp.bfloat16
LANES = 128
BLOCK = 2048
LIMIT = 20 << 20
VMEM = pl.BlockSpec(memory_space=pltpu.VMEM)
SMEM = pl.BlockSpec(memory_space=pltpu.SMEM)


def call(kernel, out_shape, *args, grid=None, in_specs=None, out_specs=None, scratch=(), flops=0, moved=0):
    out_shape = [jax.ShapeDtypeStruct(s, d) for s, d in out_shape]
    extra = {} if grid is None else {"grid": grid}
    return pl.pallas_call(
        kernel,
        out_shape=out_shape,
        in_specs=[VMEM] * len(args) if in_specs is None else in_specs,
        out_specs=[VMEM] * len(out_shape) if out_specs is None else out_specs,
        scratch_shapes=list(scratch),
        compiler_params=pltpu.CompilerParams(vmem_limit_bytes=LIMIT),
        cost_estimate=pl.CostEstimate(flops=flops, bytes_accessed=moved, transcendentals=0),
        **extra,
    )(*args)


def iota(shape, dim):
    return lax.broadcasted_iota(jnp.int32, shape, dim)


def eye():
    return iota((LANES, LANES), 0) == iota((LANES, LANES), 1)


def to_lanes(column):
    parts = []
    for b in range(column.shape[0] // LANES):
        part = jnp.broadcast_to(column[b * LANES : (b + 1) * LANES], (LANES, LANES))
        parts.append(jnp.sum(jnp.where(eye(), part, 0.0), axis=0, keepdims=True))
    return jnp.concatenate(parts, axis=0)


def to_column(lanes):
    parts = []
    for b in range(lanes.shape[0]):
        part = jnp.broadcast_to(lanes[b : b + 1], (LANES, LANES))
        parts.append(jnp.sum(jnp.where(eye(), part, 0.0), axis=1, keepdims=True))
    return jnp.concatenate(parts, axis=0)


def to_lines(row):
    return jnp.concatenate([row[:, b * LANES : (b + 1) * LANES] for b in range(row.shape[1] // LANES)], axis=0)


def to_row(lines):
    return jnp.concatenate([lines[b : b + 1] for b in range(lines.shape[0])], axis=1)


def merged(shares):
    top = jnp.max(shares, axis=0)
    return top + jnp.log(jnp.sum(jnp.exp(shares - top[None]), axis=0))


def pick_kernel(teacher_ref, student_ref, order_ref, count_ref, teacher_out, student_out):
    patches, width = teacher_ref.shape
    order = jnp.broadcast_to(order_ref[:, :LANES], (patches, LANES))
    chosen = (iota((patches, LANES), 0) == order).astype(BF16)
    dims = (((0,), (0,)), ((), ()))
    picked = lax.dot_general(chosen, teacher_ref[...], dims, preferred_element_type=F32)
    count = jnp.full((SLOT - MOST, width), count_ref[0, 0], jnp.int32).astype(F32)
    teacher_out[...] = jnp.concatenate([picked[:MOST], count], axis=0).astype(BF16)
    picked = lax.dot_general(chosen, student_ref[...], dims, preferred_element_type=F32)
    student_out[...] = picked.astype(BF16)


def compact(gathered, starts, counts, rows):
    total = gathered.shape[0]
    images = starts.shape[0]
    slots = total // images
    lane, image = iota((images, total), 1), iota((images, total), 0)
    within = lane - image * slots
    member = jnp.logical_and(within >= 0, within < slots)
    used = jnp.logical_and(member, within.astype(F32) < counts[:, :1])
    row = jnp.sum(jnp.where(used, starts[:, :1] + within.astype(F32) + 1.0, 0.0), axis=0, keepdims=True) - 1.0
    chosen = (iota((rows, total), 0).astype(F32) == row).astype(BF16)
    return jnp.dot(chosen, gathered, preferred_element_type=F32).astype(BF16)


def spread(starts, counts, slots, rows):
    images = starts.shape[0]
    shape = (images, slots, rows)
    within = iota(shape, 1)
    row = (iota(shape, 2) - within).astype(F32) - starts[:, :1].reshape(images, 1, 1)
    used = jnp.logical_and(row == 0.0, within.astype(F32) < counts[:, :1].reshape(images, 1, 1))
    return used.astype(F32).astype(BF16).reshape(images * slots, rows)


def column_kernel(gathered_ref, protos_ref, share_ref, rows_ref, places_ref):
    images = gathered_ref.shape[0]
    rows = rows_ref.shape[0]

    @pl.when(pl.program_id(0) == 0)
    def _():
        counts = gathered_ref[:, MOST:MOST + 8, :LANES].astype(F32)[:, 0]
        before = (iota((images, images), 1) < iota((images, images), 0)).astype(BF16)
        starts = jnp.dot(before, counts.astype(BF16), preferred_element_type=F32)
        places_ref[0] = starts
        places_ref[1] = counts
        flat = gathered_ref[...].reshape(images * SLOT, gathered_ref.shape[2])
        rows_ref[...] = compact(flat, starts, counts, rows)

    logits = jnp.dot(rows_ref[...], protos_ref[...], preferred_element_type=F32) * TEACH
    high = jnp.max(logits, axis=0, keepdims=True)
    total = jnp.sum(jnp.exp(logits - high), axis=0, keepdims=True)
    share_ref[...] = jnp.broadcast_to(to_lines(high + jnp.log(total))[None], share_ref.shape)


def row_kernel(shares_ref, rows_ref, protos_ref, student_lse_ref, matrix_ref, high_ref, share_ref, sums):
    step = pl.program_id(0)
    column = to_row(merged(shares_ref[...]))
    logits = jnp.dot(rows_ref[...], protos_ref[...], preferred_element_type=F32) * TEACH
    shifted = logits - column
    high = jnp.max(shifted, axis=1, keepdims=True)
    exact = jnp.exp(shifted - high)
    matrix_ref[...] = exact.astype(BF16)
    high_ref[step] = high
    sums[step] = jnp.sum(exact, axis=1, keepdims=True)

    @pl.when(step == pl.num_programs(0) - 1)
    def _():
        highs = high_ref[...]
        top = jnp.max(highs, axis=0)
        total = jnp.sum(jnp.exp(highs - top[None]) * sums[...], axis=0)
        own = to_lanes(top + jnp.log(total))
        peers, depth = share_ref.shape[0], share_ref.shape[1]
        chunk = jnp.concatenate([own, student_lse_ref[...], jnp.zeros((depth - 2 * own.shape[0], LANES), F32)], axis=0)
        share_ref[...] = jnp.broadcast_to(chunk[None], share_ref.shape)


def column_sums(matrix_ref, scale, share_ref):
    sums = jnp.sum(matrix_ref[...].astype(F32) * scale, axis=0, keepdims=True)
    share_ref[...] = jnp.broadcast_to(to_lines(sums)[None], share_ref.shape).astype(share_ref.dtype)


def first_column_kernel(shares_ref, high_ref, matrix_ref, share_ref, scale_ref, student_lse_ref):
    step = pl.program_id(0)
    lines = student_lse_ref.shape[0]

    @pl.when(step == 0)
    def _():
        both = merged(shares_ref[...][:, : 2 * lines])
        student_lse_ref[...] = both[lines:]
        scale_ref[...] = jnp.exp(high_ref[...] - to_column(both[:lines])[None])

    column_sums(matrix_ref, scale_ref[step], share_ref)


def later_column_kernel(shares_ref, scale_in_ref, matrix_ref, share_ref, scale_ref):
    step = pl.program_id(0)

    @pl.when(step == 0)
    def _():
        lines = scale_ref.shape[1] // LANES
        total = to_column(jnp.sum(shares_ref[...][:, :lines], axis=0))
        scale_ref[...] = scale_in_ref[...] / total[None]

    column_sums(matrix_ref, scale_ref[step], share_ref)


def later_row_kernel(shares_ref, scale_ref, matrix_ref, share_ref, sums):
    step = pl.program_id(0)
    inverse = to_row(1.0 / jnp.sum(shares_ref[...].astype(F32), axis=0))
    part = scale_ref[step] * jnp.sum(matrix_ref[...].astype(F32) * inverse, axis=1, keepdims=True)

    @pl.when(step == 0)
    def _():
        sums[...] = part

    @pl.when(step > 0)
    def _():
        sums[...] += part

    @pl.when(step == pl.num_programs(0) - 1)
    def _():
        own = to_lanes(sums[...])
        chunk = jnp.concatenate([own, jnp.zeros((share_ref.shape[1] - own.shape[0], LANES), F32)], axis=0)
        share_ref[...] = jnp.broadcast_to(chunk[None], share_ref.shape)


def target_kernel(shares_ref, scale_ref, matrix_ref, protos_ref, places_ref, out_ref, sums, total):
    step = pl.program_id(0)
    scale = scale_ref[step]
    inverse = to_row(1.0 / jnp.sum(shares_ref[...].astype(F32), axis=0))
    weights = matrix_ref[...].astype(F32) * inverse
    narrow = weights.astype(BF16)
    part = scale * lax.dot_general(narrow, protos_ref[...], (((1,), (1,)), ((), ())), preferred_element_type=F32)
    mass = scale * jnp.sum(narrow.astype(F32), axis=1, keepdims=True)

    @pl.when(step == 0)
    def _():
        sums[...] = part
        total[...] = mass

    @pl.when(step > 0)
    def _():
        sums[...] += part
        total[...] += mass

    @pl.when(step == pl.num_programs(0) - 1)
    def _():
        rows, width = sums.shape
        mass_high = jnp.broadcast_to(total[...], (rows, LANES)).astype(BF16)
        mass_low = (jnp.broadcast_to(total[...], (rows, LANES)) - mass_high.astype(F32)).astype(BF16)
        sent = jnp.concatenate([sums[...].astype(BF16), mass_high, mass_low], axis=1)
        images = out_ref.shape[0]
        chosen = spread(places_ref[0], places_ref[1], SLOT, rows)
        packed = jnp.dot(chosen, sent, preferred_element_type=F32).reshape(images, SLOT, width + 2 * LANES)
        same = iota((1, SLOT, LANES), 1) == iota((1, SLOT, LANES), 2)
        high = jnp.sum(jnp.where(same, packed[:, :, width : width + LANES], 0.0), axis=1, keepdims=True)
        low = jnp.sum(jnp.where(same, packed[:, :, width + LANES :], 0.0), axis=1, keepdims=True)
        filler = jnp.zeros((images, 1, width - LANES), F32)
        out_ref[:, :MOST] = packed[:, :MOST, :width].astype(BF16)
        numbers = jnp.concatenate(
            [
                jnp.concatenate([high, filler], axis=2),
                jnp.concatenate([low, filler], axis=2),
                jnp.zeros((images, SLOT - MOST - 2, width), F32),
            ],
            axis=1,
        )
        out_ref[:, MOST:] = numbers.astype(BF16)


def student_kernel(gathered_ref, places_ref, protos_ref, sums_ref, high_ref, lse_ref, rows_ref, total):
    step = pl.program_id(0)
    rows = rows_ref.shape[0]

    @pl.when(step == 0)
    def _():
        images, slots, width = gathered_ref.shape
        flat = gathered_ref[...].reshape(images * slots, width)
        rows_ref[...] = compact(flat, places_ref[0], places_ref[1], rows)
        high_ref[...] = jnp.full(high_ref.shape, -1e30, F32)
        total[...] = jnp.zeros(total.shape, F32)
        sums_ref[...] = jnp.zeros(sums_ref.shape, F32)

    protos = protos_ref[...]
    logits = jnp.dot(rows_ref[...], protos, preferred_element_type=F32) * STUD
    before = high_ref[...]
    high = jnp.maximum(before, jnp.max(logits, axis=1, keepdims=True))
    shrink = jnp.exp(before - high)
    exact = jnp.exp(logits - high)
    total[...] = total[...] * shrink + jnp.sum(exact, axis=1, keepdims=True)
    part = lax.dot_general(exact.astype(BF16), protos, (((1,), (1,)), ((), ())), preferred_element_type=F32)
    sums_ref[...] = sums_ref[...] * shrink + part
    high_ref[...] = high

    @pl.when(step == pl.num_programs(0) - 1)
    def _():
        lse_ref[...] = to_lanes(high_ref[...] + jnp.log(total[...]))


def student_pack_kernel(sums_ref, high_ref, lse_ref, places_ref, out_ref):
    rows = sums_ref.shape[0]
    images = places_ref.shape[1]
    sent = (sums_ref[...] * jnp.exp(high_ref[...] - to_column(lse_ref[...]))).astype(BF16)
    chosen = spread(places_ref[0], places_ref[1], out_ref.shape[0] // images, rows)
    out_ref[...] = jnp.dot(chosen, sent, preferred_element_type=F32).astype(BF16)


def finish_kernel(back_ref, student_ref, picked_ref, lse_ref, places_ref, order_ref, index_ref, grad_ref, loss_ref):
    patches, width = grad_ref.shape
    lines = lse_ref.shape[0]
    back = jnp.sum(back_ref[...].astype(F32), axis=0)
    images = places_ref.shape[1]
    own = iota((images, LANES), 0) == index_ref[0, 0]
    start = jnp.sum(jnp.where(own, places_ref[0], 0.0), axis=0, keepdims=True)
    count = jnp.sum(jnp.where(own, places_ref[1], 0.0), axis=0, keepdims=True)
    mass = to_column((back[MOST : MOST + 1] + back[MOST + 1 : MOST + 2])[:, :LANES])[:MOST]
    used = iota((MOST, 1), 0).astype(F32) < count[:, :1]
    mean = back[:MOST] / jnp.where(used, mass, 1.0)
    lse_row = to_row(lse_ref[...])
    shape = (MOST, lines * LANES)
    here = (iota(shape, 1) - iota(shape, 0)).astype(F32) == start[:, :1]
    own_lse = jnp.sum(jnp.where(here, lse_row, 0.0), axis=1, keepdims=True)
    cross = own_lse - STUD * jnp.sum(picked_ref[:MOST].astype(F32) * mean, axis=1, keepdims=True)
    cross = jnp.sum(jnp.where(used, cross, 0.0), axis=0, keepdims=True)
    loss_ref[...] = cross / count[:, :1]
    rows = jnp.where(used, STUD * (student_ref[...].astype(F32) - mean), 0.0)
    rows = jnp.concatenate([rows, jnp.zeros((LANES - MOST, width), F32)], axis=0).astype(BF16)
    order = jnp.broadcast_to(order_ref[:, :LANES], (patches, LANES))
    chosen = (iota((patches, LANES), 0) == order).astype(BF16)
    grad_ref[...] = jnp.dot(chosen, rows, preferred_element_type=F32).astype(BF16)


def body(student_patches, teacher_patches, mask_order, counts, student_protos, teacher_protos):
    width = lax.axis_size("proto")
    groups = lax.axis_size("dp")
    rows = MASK_DEV * width
    lines = rows // LANES
    patches, bot = student_patches.shape[1:]
    protos = student_protos.shape[1]
    steps = protos // BLOCK
    depth = 8
    index = lax.axis_index("proto").astype(jnp.int32).reshape(1, 1)
    over = functools.partial(lax.all_to_all, split_axis=0, concat_axis=0, tiled=True)
    wide = pl.BlockSpec((bot, BLOCK), lambda k: (0, k))
    peer = pl.BlockSpec((groups, BLOCK // LANES, LANES), lambda k: (0, k, 0))
    square = pl.BlockSpec((rows, BLOCK), lambda k: (0, k))
    grid = (steps,)
    dot = 2 * rows * protos * bot
    column = pltpu.VMEM((rows, 1), F32)

    teacher_sent, student_sent = call(
        pick_kernel,
        [((SLOT, bot), BF16), ((LANES, bot), BF16)],
        teacher_patches[0],
        student_patches[0],
        mask_order,
        counts,
        in_specs=[VMEM, VMEM, VMEM, SMEM],
        moved=4 * patches * bot,
    )
    gathered_student = lax.all_gather(student_sent, "proto", axis=0, tiled=False)
    gathered = lax.all_gather(teacher_sent, "proto", axis=0, tiled=False)
    share, teacher_rows, places = call(
        column_kernel,
        [((groups, protos // LANES, LANES), F32), ((rows, bot), BF16), ((2, width, LANES), F32)],
        gathered,
        teacher_protos,
        grid=grid,
        in_specs=[VMEM, wide],
        out_specs=[peer, VMEM, VMEM],
        flops=dot,
        moved=2 * bot * protos,
    )
    shares = over(share, "dp")
    student_sum, student_high, student_lse = call(
        student_kernel,
        [((rows, bot), F32), ((rows, 1), F32), ((lines, LANES), F32)],
        gathered_student,
        places,
        student_protos,
        grid=grid,
        in_specs=[VMEM, VMEM, wide],
        scratch=[pltpu.VMEM((rows, bot), BF16), column],
        flops=2 * dot,
        moved=2 * bot * protos,
    )
    matrix, high, share = call(
        row_kernel,
        [((rows, protos), BF16), ((steps, rows, 1), F32), ((width, depth, LANES), F32)],
        shares,
        teacher_rows,
        teacher_protos,
        student_lse,
        grid=grid,
        in_specs=[peer, VMEM, wide, VMEM],
        out_specs=[square, VMEM, VMEM],
        scratch=[pltpu.VMEM((steps, rows, 1), F32)],
        flops=dot,
        moved=2 * bot * protos + 2 * rows * protos,
    )
    shares = over(share, "proto")
    share, scale, student_lse = call(
        first_column_kernel,
        [((groups, protos // LANES, LANES), BF16), ((steps, rows, 1), F32), ((lines, LANES), F32)],
        shares,
        high,
        matrix,
        grid=grid,
        in_specs=[VMEM, VMEM, square],
        out_specs=[peer, VMEM, VMEM],
        moved=2 * rows * protos,
    )
    student_part = call(
        student_pack_kernel,
        [((width * MOST, bot), BF16)],
        student_sum,
        student_high,
        student_lse,
        places,
        flops=2 * width * MOST * rows * bot,
    )[0]
    shares, student_part = lax.optimization_barrier((over(share, "dp"), student_part))
    student_back = lax.psum_scatter(student_part, "proto", scatter_dimension=0, tiled=True)
    share = call(
        later_row_kernel,
        [((width, depth, LANES), F32)],
        shares,
        scale,
        matrix,
        grid=grid,
        in_specs=[peer, VMEM, square],
        scratch=[column],
        moved=2 * rows * protos,
    )[0]
    shares = over(share, "proto")
    share, scale = call(
        later_column_kernel,
        [((groups, protos // LANES, LANES), BF16), ((steps, rows, 1), F32)],
        shares,
        scale,
        matrix,
        grid=grid,
        in_specs=[VMEM, VMEM, square],
        out_specs=[peer, VMEM],
        moved=2 * rows * protos,
    )
    shares = over(share, "dp")
    sent = call(
        target_kernel,
        [((width, SLOT, bot), BF16)],
        shares,
        scale,
        matrix,
        student_protos,
        places,
        grid=grid,
        in_specs=[peer, VMEM, square, wide, VMEM],
        scratch=[pltpu.VMEM((rows, bot), F32), column],
        flops=dot,
        moved=2 * rows * protos,
    )[0]
    back = over(sent, "proto")
    student_grad, image_loss = call(
        finish_kernel,
        [((patches, bot), BF16), ((1, 1), F32)],
        back,
        student_back,
        student_sent,
        student_lse,
        places,
        mask_order,
        index,
        in_specs=[VMEM, VMEM, VMEM, VMEM, VMEM, VMEM, SMEM],
        moved=2 * patches * bot,
    )
    return (student_grad[None], image_loss)


def solution(mesh):
    placed = (
        P(("dp", "proto"), None, None),
        P(("dp", "proto"), None, None),
        P(("dp", "proto"), None),
        P("dp", "proto"),
        P(None, "proto"),
        P(None, "proto"),
    )
    return jax.shard_map(
        body,
        mesh=mesh,
        in_specs=placed,
        out_specs=(P(("dp", "proto"), None, None), P("dp", "proto")),
        check_vma=False,
    )
```

```python
import functools

import jax
import jax.numpy as jnp
from jax import lax
from jax.experimental import pallas as pl
from jax.experimental.pallas import tpu as pltpu
from jax.sharding import PartitionSpec as P

MASK_DEV = 24
MOST = 72
SLOT = 80
TEACH = 1.0 / 0.07
STUD = 1.0 / 0.1
F32 = jnp.float32
BF16 = jnp.bfloat16
LANES = 128
BLOCK = 2048
LIMIT = 20 << 20
VMEM = pl.BlockSpec(memory_space=pltpu.VMEM)
SMEM = pl.BlockSpec(memory_space=pltpu.SMEM)


def call(kernel, out_shape, *args, grid=None, in_specs=None, out_specs=None, scratch=(), flops=0, moved=0):
    out_shape = [jax.ShapeDtypeStruct(s, d) for s, d in out_shape]
    extra = {} if grid is None else {"grid": grid}
    return pl.pallas_call(
        kernel,
        out_shape=out_shape,
        in_specs=[VMEM] * len(args) if in_specs is None else in_specs,
        out_specs=[VMEM] * len(out_shape) if out_specs is None else out_specs,
        scratch_shapes=list(scratch),
        compiler_params=pltpu.CompilerParams(vmem_limit_bytes=LIMIT),
        cost_estimate=pl.CostEstimate(flops=flops, bytes_accessed=moved, transcendentals=0),
        **extra,
    )(*args)


def iota(shape, dim):
    return lax.broadcasted_iota(jnp.int32, shape, dim)


def eye():
    return iota((LANES, LANES), 0) == iota((LANES, LANES), 1)


def to_lanes(column):
    parts = []
    for b in range(column.shape[0] // LANES):
        part = jnp.broadcast_to(column[b * LANES : (b + 1) * LANES], (LANES, LANES))
        parts.append(jnp.sum(jnp.where(eye(), part, 0.0), axis=0, keepdims=True))
    return jnp.concatenate(parts, axis=0)


def to_column(lanes):
    parts = []
    for b in range(lanes.shape[0]):
        part = jnp.broadcast_to(lanes[b : b + 1], (LANES, LANES))
        parts.append(jnp.sum(jnp.where(eye(), part, 0.0), axis=1, keepdims=True))
    return jnp.concatenate(parts, axis=0)


def to_lines(row):
    return jnp.concatenate([row[:, b * LANES : (b + 1) * LANES] for b in range(row.shape[1] // LANES)], axis=0)


def to_row(lines):
    return jnp.concatenate([lines[b : b + 1] for b in range(lines.shape[0])], axis=1)


def merged(shares):
    top = jnp.max(shares, axis=0)
    return top + jnp.log(jnp.sum(jnp.exp(shares - top[None]), axis=0))


def pick_kernel(teacher_ref, student_ref, order_ref, count_ref, teacher_out, student_out):
    patches, width = teacher_ref.shape
    order = jnp.broadcast_to(order_ref[:, :LANES], (patches, LANES))
    chosen = (iota((patches, LANES), 0) == order).astype(BF16)
    dims = (((0,), (0,)), ((), ()))
    picked = lax.dot_general(chosen, teacher_ref[...], dims, preferred_element_type=F32)
    count = jnp.full((SLOT - MOST, width), count_ref[0, 0], jnp.int32).astype(F32)
    teacher_out[...] = jnp.concatenate([picked[:MOST], count], axis=0).astype(BF16)
    picked = lax.dot_general(chosen, student_ref[...], dims, preferred_element_type=F32)
    student_out[...] = picked.astype(BF16)


def compact(gathered, starts, counts, rows):
    total = gathered.shape[0]
    images = starts.shape[0]
    slots = total // images
    lane, image = iota((images, total), 1), iota((images, total), 0)
    within = lane - image * slots
    member = jnp.logical_and(within >= 0, within < slots)
    used = jnp.logical_and(member, within.astype(F32) < counts[:, :1])
    row = jnp.sum(jnp.where(used, starts[:, :1] + within.astype(F32) + 1.0, 0.0), axis=0, keepdims=True) - 1.0
    chosen = (iota((rows, total), 0).astype(F32) == row).astype(BF16)
    return jnp.dot(chosen, gathered, preferred_element_type=F32).astype(BF16)


def spread(starts, counts, slots, rows):
    images = starts.shape[0]
    shape = (images, slots, rows)
    within = iota(shape, 1)
    row = (iota(shape, 2) - within).astype(F32) - starts[:, :1].reshape(images, 1, 1)
    used = jnp.logical_and(row == 0.0, within.astype(F32) < counts[:, :1].reshape(images, 1, 1))
    return used.astype(F32).astype(BF16).reshape(images * slots, rows)


def column_kernel(gathered_ref, index_ref, protos_ref, share_ref, rows_ref, places_ref):
    images = gathered_ref.shape[0]
    rows = rows_ref.shape[0]

    @pl.when(pl.program_id(0) == 0)
    def _():
        counts = gathered_ref[:, MOST:MOST + 8, :LANES].astype(F32)[:, 0]
        before = (iota((images, images), 1) < iota((images, images), 0)).astype(BF16)
        starts = jnp.dot(before, counts.astype(BF16), preferred_element_type=F32)
        half, core = images // 2, index_ref[0, 0] % 2
        place = iota((images, images), 0)
        image = jnp.where(place < half, 2 * place + core, 2 * (place - half) + 1 - core)
        other = iota((images, images), 1)
        places_ref[0] = jnp.dot((other < image).astype(BF16), counts.astype(BF16), preferred_element_type=F32)
        places_ref[1] = jnp.dot((other == image).astype(BF16), counts.astype(BF16), preferred_element_type=F32)
        places_ref[2] = starts
        places_ref[3] = counts
        flat = gathered_ref[...].reshape(images * SLOT, gathered_ref.shape[2])
        rows_ref[...] = compact(flat, starts, counts, rows)

    logits = jnp.dot(rows_ref[...], protos_ref[...], preferred_element_type=F32) * TEACH
    high = jnp.max(logits, axis=0, keepdims=True)
    total = jnp.sum(jnp.exp(logits - high), axis=0, keepdims=True)
    share_ref[...] = jnp.broadcast_to(to_lines(high + jnp.log(total))[None], share_ref.shape)


def fill_share(share_ref, lines):
    blank = jnp.zeros((share_ref.shape[1] - lines.shape[0], LANES), F32)
    share_ref[...] = jnp.broadcast_to(jnp.concatenate([lines, blank], axis=0)[None], share_ref.shape)


def row_kernel(shares_ref, rows_ref, protos_ref, matrix_ref, high_ref, share_ref, sums):
    step = pl.program_id(0)
    column = to_row(merged(shares_ref[...]))
    logits = jnp.dot(rows_ref[...], protos_ref[...], preferred_element_type=F32) * TEACH
    shifted = logits - column
    high = jnp.max(shifted, axis=1, keepdims=True)
    exact = jnp.exp(shifted - high)
    matrix_ref[...] = exact.astype(BF16)
    high_ref[step] = high
    sums[step] = jnp.sum(exact, axis=1, keepdims=True)

    @pl.when(step == pl.num_programs(0) - 1)
    def _():
        highs = high_ref[...]
        top = jnp.max(highs, axis=0)
        total = jnp.sum(jnp.exp(highs - top[None]) * sums[...], axis=0)
        fill_share(share_ref, to_lanes(top + jnp.log(total)))


def column_sums(matrix_ref, scale, share_ref):
    sums = jnp.sum(matrix_ref[...].astype(F32) * scale, axis=0, keepdims=True)
    share_ref[...] = jnp.broadcast_to(to_lines(sums)[None], share_ref.shape).astype(share_ref.dtype)


def first_column_kernel(shares_ref, high_ref, matrix_ref, share_ref, scale_ref):
    step = pl.program_id(0)

    @pl.when(step == 0)
    def _():
        lines = scale_ref.shape[1] // LANES
        row_lse = merged(shares_ref[...][:, :lines])
        scale_ref[...] = jnp.exp(high_ref[...] - to_column(row_lse)[None])

    column_sums(matrix_ref, scale_ref[step], share_ref)


def later_column_kernel(shares_ref, scale_in_ref, matrix_ref, share_ref, scale_ref):
    step = pl.program_id(0)

    @pl.when(step == 0)
    def _():
        lines = scale_ref.shape[1] // LANES
        total = to_column(jnp.sum(shares_ref[...][:, :lines], axis=0))
        scale_ref[...] = scale_in_ref[...] / total[None]

    column_sums(matrix_ref, scale_ref[step], share_ref)


def later_row_kernel(shares_ref, scale_ref, matrix_ref, share_ref, sums):
    step = pl.program_id(0)
    inverse = to_row(1.0 / jnp.sum(shares_ref[...].astype(F32), axis=0))
    part = scale_ref[step] * jnp.sum(matrix_ref[...].astype(F32) * inverse, axis=1, keepdims=True)

    @pl.when(step == 0)
    def _():
        sums[...] = part

    @pl.when(step > 0)
    def _():
        sums[...] += part

    @pl.when(step == pl.num_programs(0) - 1)
    def _():
        fill_share(share_ref, to_lanes(sums[...]))


def split(values, parts):
    out = []
    for _ in range(parts):
        part = values.astype(BF16)
        out.append(part)
        values = values - part.astype(F32)
    return out


def pack(sums, numbers, parts, starts, counts):
    rows, width = sums.shape
    images = starts.shape[0]
    wide = jnp.broadcast_to(numbers, (rows, LANES))
    sent = jnp.concatenate([sums.astype(BF16)] + split(wide, parts), axis=1)
    chosen = spread(starts, counts, SLOT, rows)
    packed = jnp.dot(chosen, sent, preferred_element_type=F32).reshape(images, SLOT, width + parts * LANES)
    same = iota((1, SLOT, LANES), 1) == iota((1, SLOT, LANES), 2)
    tail = []
    for k in range(parts):
        part = packed[:, :, width + k * LANES : width + (k + 1) * LANES]
        tail.append(jnp.sum(jnp.where(same, part, 0.0), axis=1, keepdims=True))
    return packed[:, :MOST, :width].astype(BF16), join(tail, width)


def join(tail, width):
    images = tail[0].shape[0]
    filler = jnp.zeros((images, 1, width - LANES), F32)
    rows = [jnp.concatenate([part.astype(F32), filler], axis=2) for part in tail]
    rows.append(jnp.zeros((images, SLOT - MOST - len(tail), width), F32))
    return jnp.concatenate(rows, axis=1).astype(BF16)


def numbers_of(chunk, parts):
    tail = chunk[:, MOST:SLOT, :LANES].astype(F32)
    return sum(tail[:, k] for k in range(parts))


def put(own_ref, other_ref, rows, tail):
    half = own_ref.shape[0]
    own_ref[:, :MOST], own_ref[:, MOST:] = rows[:half], tail[:half]
    other_ref[:, :MOST], other_ref[:, MOST:] = rows[half:], tail[half:]


def slots_of(lanes):
    images = lanes.shape[0]
    same = iota((1, MOST, LANES), 1) == iota((1, MOST, LANES), 2)
    return jnp.sum(jnp.where(same, lanes.reshape(images, 1, LANES), 0.0), axis=2, keepdims=True)


def target_kernel(shares_ref, scale_ref, matrix_ref, protos_ref, places_ref, own_ref, other_ref, sums, total):
    step = pl.program_id(0)
    scale = scale_ref[step]
    inverse = to_row(1.0 / jnp.sum(shares_ref[...].astype(F32), axis=0))
    weights = matrix_ref[...].astype(F32) * inverse
    narrow = weights.astype(BF16)
    part = scale * lax.dot_general(narrow, protos_ref[...], (((1,), (1,)), ((), ())), preferred_element_type=F32)
    mass = scale * jnp.sum(narrow.astype(F32), axis=1, keepdims=True)

    @pl.when(step == 0)
    def _():
        sums[...] = part
        total[...] = mass

    @pl.when(step > 0)
    def _():
        sums[...] += part
        total[...] += mass

    @pl.when(step == pl.num_programs(0) - 1)
    def _():
        put(own_ref, other_ref, *pack(sums[...], total[...], 2, places_ref[0], places_ref[1]))


def target_merge_kernel(own_ref, came_ref, student_ref, out_ref):
    width = own_ref.shape[2]
    out_ref[:, :MOST] = (own_ref[:, :MOST].astype(F32) + came_ref[:, :MOST].astype(F32)).astype(BF16)
    total = numbers_of(own_ref, 2) + numbers_of(came_ref, 2)
    out_ref[:, MOST:SLOT] = join([part[:, None] for part in split(total, 2)], width)
    out_ref[:, SLOT:] = student_ref[...]


def student_kernel(gathered_ref, places_ref, protos_ref, own_ref, other_ref, rows_ref, sums, top, total):
    step = pl.program_id(0)
    rows = rows_ref.shape[0]

    @pl.when(step == 0)
    def _():
        images, slots, width = gathered_ref.shape
        flat = gathered_ref[...].reshape(images * slots, width)
        rows_ref[...] = compact(flat, places_ref[2], places_ref[3], rows)
        top[...] = jnp.full(top.shape, -1e30, F32)
        total[...] = jnp.zeros(total.shape, F32)
        sums[...] = jnp.zeros(sums.shape, F32)

    protos = protos_ref[...]
    logits = jnp.dot(rows_ref[...], protos, preferred_element_type=F32) * STUD
    before = top[...]
    high = jnp.maximum(before, jnp.max(logits, axis=1, keepdims=True))
    shrink = jnp.exp(before - high)
    exact = jnp.exp(logits - high)
    total[...] = total[...] * shrink + jnp.sum(exact, axis=1, keepdims=True)
    part = lax.dot_general(exact.astype(BF16), protos, (((1,), (1,)), ((), ())), preferred_element_type=F32)
    sums[...] = sums[...] * shrink + part
    top[...] = high

    @pl.when(step == pl.num_programs(0) - 1)
    def _():
        mean, own_lse = sums[...] / total[...], top[...] + jnp.log(total[...])
        put(own_ref, other_ref, *pack(mean, own_lse, 3, places_ref[0], places_ref[1]))


def blend(chunk, lse):
    joint = merged(lse)
    weights = slots_of(jnp.exp(lse - joint[None]))
    return jnp.sum(chunk * weights, axis=0), joint


def student_merge_kernel(own_ref, came_ref, out_ref):
    width = own_ref.shape[2]
    own, came = numbers_of(own_ref, 3), numbers_of(came_ref, 3)
    high = jnp.maximum(own, came)
    joint = high + jnp.log(jnp.exp(own - high) + jnp.exp(came - high))
    mean = own_ref[:, :MOST].astype(F32) * slots_of(jnp.exp(own - joint))
    mean = mean + came_ref[:, :MOST].astype(F32) * slots_of(jnp.exp(came - joint))
    out_ref[:, :MOST] = mean.astype(BF16)
    out_ref[:, MOST:] = join([part[:, None] for part in split(joint, 3)], width)


def finish_kernel(back_ref, picked_ref, order_ref, count_ref, grad_ref, loss_ref):
    patches, width = grad_ref.shape
    target = jnp.sum(back_ref[:, :SLOT].astype(F32), axis=0)
    mass = to_column((target[MOST : MOST + 1] + target[MOST + 1 : MOST + 2])[:, :LANES])[:MOST]
    tail = back_ref[:, SLOT + MOST : 2 * SLOT, :LANES].astype(F32)
    soft, lse_lanes = blend(back_ref[:, SLOT : SLOT + MOST].astype(F32), sum(tail[:, k] for k in range(3)))
    used = iota((MOST, 1), 0) < count_ref[0, 0]
    mean = target[:MOST] / jnp.where(used, mass, 1.0)
    own_lse = to_column(lse_lanes.reshape(1, LANES))[:MOST]
    cross = own_lse - STUD * jnp.sum(picked_ref[:MOST].astype(F32) * mean, axis=1, keepdims=True)
    cross = jnp.sum(jnp.where(used, cross, 0.0), axis=0, keepdims=True)
    loss_ref[...] = cross / jnp.full((1, 1), count_ref[0, 0], jnp.int32).astype(F32)
    rows = jnp.where(used, STUD * (soft - mean), 0.0)
    rows = jnp.concatenate([rows, jnp.zeros((LANES - MOST, width), F32)], axis=0).astype(BF16)
    order = jnp.broadcast_to(order_ref[:, :LANES], (patches, LANES))
    chosen = (iota((patches, LANES), 0) == order).astype(BF16)
    grad_ref[...] = jnp.dot(chosen, rows, preferred_element_type=F32).astype(BF16)


def body(student_patches, teacher_patches, mask_order, counts, student_protos, teacher_protos):
    width = lax.axis_size("proto")
    groups = lax.axis_size("dp")
    rows = MASK_DEV * width
    lines = rows // LANES
    patches, bot = student_patches.shape[1:]
    protos = student_protos.shape[1]
    steps = protos // BLOCK
    depth = 8
    index = lax.axis_index("proto").astype(jnp.int32).reshape(1, 1)
    over = functools.partial(lax.all_to_all, split_axis=0, concat_axis=0, tiled=True)
    wide = pl.BlockSpec((bot, BLOCK), lambda k: (0, k))
    peer = pl.BlockSpec((groups, BLOCK // LANES, LANES), lambda k: (0, k, 0))
    square = pl.BlockSpec((rows, BLOCK), lambda k: (0, k))
    grid = (steps,)
    dot = 2 * rows * protos * bot
    column = pltpu.VMEM((rows, 1), F32)

    teacher_sent, student_sent = call(
        pick_kernel,
        [((SLOT, bot), BF16), ((LANES, bot), BF16)],
        teacher_patches[0],
        student_patches[0],
        mask_order,
        counts,
        in_specs=[VMEM, VMEM, VMEM, SMEM],
        moved=4 * patches * bot,
    )
    gathered_student = lax.all_gather(student_sent, "proto", axis=0, tiled=False)
    gathered = lax.all_gather(teacher_sent, "proto", axis=0, tiled=False)
    share, teacher_rows, places = call(
        column_kernel,
        [((groups, protos // LANES, LANES), F32), ((rows, bot), BF16), ((4, width, LANES), F32)],
        gathered,
        index,
        teacher_protos,
        grid=grid,
        in_specs=[VMEM, SMEM, wide],
        out_specs=[peer, VMEM, VMEM],
        flops=dot,
        moved=2 * bot * protos,
    )
    shares = over(share, "dp")
    matrix, high, share = call(
        row_kernel,
        [((rows, protos), BF16), ((steps, rows, 1), F32), ((width, depth, LANES), F32)],
        shares,
        teacher_rows,
        teacher_protos,
        grid=grid,
        in_specs=[peer, VMEM, wide],
        out_specs=[square, VMEM, VMEM],
        scratch=[pltpu.VMEM((steps, rows, 1), F32)],
        flops=dot,
        moved=2 * bot * protos + 2 * rows * protos,
    )
    shares = over(share, "proto")
    share, scale = call(
        first_column_kernel,
        [((groups, protos // LANES, LANES), BF16), ((steps, rows, 1), F32)],
        shares,
        high,
        matrix,
        grid=grid,
        in_specs=[VMEM, VMEM, square],
        out_specs=[peer, VMEM],
        moved=2 * rows * protos,
    )
    shares = over(share, "dp")
    share = call(
        later_row_kernel,
        [((width, depth, LANES), F32)],
        shares,
        scale,
        matrix,
        grid=grid,
        in_specs=[peer, VMEM, square],
        scratch=[column],
        moved=2 * rows * protos,
    )[0]
    shares = over(share, "proto")
    share, scale = call(
        later_column_kernel,
        [((groups, protos // LANES, LANES), BF16), ((steps, rows, 1), F32)],
        shares,
        scale,
        matrix,
        grid=grid,
        in_specs=[VMEM, VMEM, square],
        out_specs=[peer, VMEM],
        moved=2 * rows * protos,
    )
    shares = over(share, "dp")
    packed = ((width // 2, SLOT, bot), BF16)
    student_own, student_other = call(
        student_kernel,
        [packed, packed],
        gathered_student,
        places,
        student_protos,
        grid=grid,
        in_specs=[VMEM, VMEM, wide],
        scratch=[pltpu.VMEM((rows, bot), BF16), pltpu.VMEM((rows, bot), F32), column, column],
        flops=2 * dot,
        moved=2 * bot * protos,
    )
    swap = [(p, p ^ 1) for p in range(width)]
    student_came = lax.ppermute(student_other, "proto", swap)
    student_sum = call(student_merge_kernel, [packed], student_own, student_came)[0]
    own, other = call(
        target_kernel,
        [packed, packed],
        shares,
        scale,
        matrix,
        student_protos,
        places,
        grid=grid,
        in_specs=[peer, VMEM, square, wide, VMEM],
        scratch=[pltpu.VMEM((rows, bot), F32), column],
        flops=dot,
        moved=2 * rows * protos,
    )
    came = lax.ppermute(other, "proto", swap)
    sent = call(target_merge_kernel, [((width // 2, 2 * SLOT, bot), BF16)], own, came, student_sum)[0]
    same_core = [list(range(core, width, 2)) for core in range(2)]
    back = over(sent, "proto", axis_index_groups=same_core)
    student_grad, image_loss = call(
        finish_kernel,
        [((patches, bot), BF16), ((1, 1), F32)],
        back,
        student_sent,
        mask_order,
        counts,
        in_specs=[VMEM, VMEM, VMEM, SMEM],
        moved=2 * patches * bot,
    )
    return (student_grad[None], image_loss)


def solution(mesh):
    placed = (
        P(("dp", "proto"), None, None),
        P(("dp", "proto"), None, None),
        P(("dp", "proto"), None),
        P("dp", "proto"),
        P(None, "proto"),
        P(None, "proto"),
    )
    return jax.shard_map(
        body,
        mesh=mesh,
        in_specs=placed,
        out_specs=(P(("dp", "proto"), None, None), P("dp", "proto")),
        check_vma=False,
    )
```

```python
import functools

import jax
import jax.numpy as jnp
from jax import lax
from jax.experimental import pallas as pl
from jax.experimental.pallas import tpu as pltpu
from jax.sharding import PartitionSpec as P

MASK_DEV = 24
MOST = 72
SLOT = 80
TEACH = 1.0 / 0.07
STUD = 1.0 / 0.1
F32 = jnp.float32
BF16 = jnp.bfloat16
LANES = 128
BLOCK = 2048
LIMIT = 20 << 20
VMEM = pl.BlockSpec(memory_space=pltpu.VMEM)
SMEM = pl.BlockSpec(memory_space=pltpu.SMEM)


def call(kernel, out_shape, *args, grid=None, in_specs=None, out_specs=None, scratch=(), flops=0, moved=0):
    out_shape = [jax.ShapeDtypeStruct(s, d) for s, d in out_shape]
    extra = {} if grid is None else {"grid": grid}
    return pl.pallas_call(
        kernel,
        out_shape=out_shape,
        in_specs=[VMEM] * len(args) if in_specs is None else in_specs,
        out_specs=[VMEM] * len(out_shape) if out_specs is None else out_specs,
        scratch_shapes=list(scratch),
        compiler_params=pltpu.CompilerParams(vmem_limit_bytes=LIMIT),
        cost_estimate=pl.CostEstimate(flops=flops, bytes_accessed=moved, transcendentals=0),
        **extra,
    )(*args)


def iota(shape, dim):
    return lax.broadcasted_iota(jnp.int32, shape, dim)


def eye():
    return iota((LANES, LANES), 0) == iota((LANES, LANES), 1)


def to_lanes(column):
    parts = []
    for b in range(column.shape[0] // LANES):
        part = jnp.broadcast_to(column[b * LANES : (b + 1) * LANES], (LANES, LANES))
        parts.append(jnp.sum(jnp.where(eye(), part, 0.0), axis=0, keepdims=True))
    return jnp.concatenate(parts, axis=0)


def to_column(lanes):
    parts = []
    for b in range(lanes.shape[0]):
        part = jnp.broadcast_to(lanes[b : b + 1], (LANES, LANES))
        parts.append(jnp.sum(jnp.where(eye(), part, 0.0), axis=1, keepdims=True))
    return jnp.concatenate(parts, axis=0)


def to_lines(row):
    return jnp.concatenate([row[:, b * LANES : (b + 1) * LANES] for b in range(row.shape[1] // LANES)], axis=0)


def to_row(lines):
    return jnp.concatenate([lines[b : b + 1] for b in range(lines.shape[0])], axis=1)


def merged(shares):
    top = jnp.max(shares, axis=0)
    return top + jnp.log(jnp.sum(jnp.exp(shares - top[None]), axis=0))


def pick_kernel(teacher_ref, student_ref, order_ref, count_ref, teacher_out, student_out):
    patches, width = teacher_ref.shape
    order = jnp.broadcast_to(order_ref[:, :LANES], (patches, LANES))
    chosen = (iota((patches, LANES), 0) == order).astype(BF16)
    dims = (((0,), (0,)), ((), ()))
    picked = lax.dot_general(chosen, teacher_ref[...], dims, preferred_element_type=F32)
    count = jnp.full((SLOT - MOST, width), count_ref[0, 0], jnp.int32).astype(F32)
    teacher_out[...] = jnp.concatenate([picked[:MOST], count], axis=0).astype(BF16)
    picked = lax.dot_general(chosen, student_ref[...], dims, preferred_element_type=F32)
    student_out[...] = picked.astype(BF16)


def compact(gathered, starts, counts, rows):
    total = gathered.shape[0]
    images = starts.shape[0]
    slots = total // images
    lane, image = iota((images, total), 1), iota((images, total), 0)
    within = lane - image * slots
    member = jnp.logical_and(within >= 0, within < slots)
    used = jnp.logical_and(member, within.astype(F32) < counts[:, :1])
    row = jnp.sum(jnp.where(used, starts[:, :1] + within.astype(F32) + 1.0, 0.0), axis=0, keepdims=True) - 1.0
    chosen = (iota((rows, total), 0).astype(F32) == row).astype(BF16)
    return jnp.dot(chosen, gathered, preferred_element_type=F32).astype(BF16)


def spread(starts, counts, slots, rows):
    images = starts.shape[0]
    shape = (images, slots, rows)
    within = iota(shape, 1)
    row = (iota(shape, 2) - within).astype(F32) - starts[:, :1].reshape(images, 1, 1)
    used = jnp.logical_and(row == 0.0, within.astype(F32) < counts[:, :1].reshape(images, 1, 1))
    return used.astype(F32).astype(BF16).reshape(images * slots, rows)


def column_kernel(gathered_ref, index_ref, protos_ref, share_ref, rows_ref, places_ref):
    images = gathered_ref.shape[0]
    rows = rows_ref.shape[0]

    @pl.when(pl.program_id(0) == 0)
    def _():
        counts = gathered_ref[:, MOST:MOST + 8, :LANES].astype(F32)[:, 0]
        before = (iota((images, images), 1) < iota((images, images), 0)).astype(BF16)
        starts = jnp.dot(before, counts.astype(BF16), preferred_element_type=F32)
        half, core = images // 2, index_ref[0, 0] % 2
        place = iota((images, images), 0)
        image = jnp.where(place < half, 2 * place + core, 2 * (place - half) + 1 - core)
        other = iota((images, images), 1)
        places_ref[0] = jnp.dot((other < image).astype(BF16), counts.astype(BF16), preferred_element_type=F32)
        places_ref[1] = jnp.dot((other == image).astype(BF16), counts.astype(BF16), preferred_element_type=F32)
        places_ref[2] = starts
        places_ref[3] = counts
        flat = gathered_ref[...].reshape(images * SLOT, gathered_ref.shape[2])
        rows_ref[...] = compact(flat, starts, counts, rows)

    logits = jnp.dot(rows_ref[...], protos_ref[...], preferred_element_type=F32) * TEACH
    high = jnp.max(logits, axis=0, keepdims=True)
    total = jnp.sum(jnp.exp(logits - high), axis=0, keepdims=True)
    share_ref[...] = jnp.broadcast_to(to_lines(high + jnp.log(total))[None], share_ref.shape)


def fill_share(share_ref, lines):
    blank = jnp.zeros((share_ref.shape[1] - lines.shape[0], LANES), F32)
    share_ref[...] = jnp.broadcast_to(jnp.concatenate([lines, blank], axis=0)[None], share_ref.shape)


def row_kernel(shares_ref, rows_ref, protos_ref, matrix_ref, high_ref, share_ref, sums):
    step = pl.program_id(0)
    column = to_row(merged(shares_ref[...]))
    logits = jnp.dot(rows_ref[...], protos_ref[...], preferred_element_type=F32) * TEACH
    shifted = logits - column
    high = jnp.max(shifted, axis=1, keepdims=True)
    exact = jnp.exp(shifted - high)
    matrix_ref[...] = exact.astype(BF16)
    high_ref[step] = high
    sums[step] = jnp.sum(exact, axis=1, keepdims=True)

    @pl.when(step == pl.num_programs(0) - 1)
    def _():
        highs = high_ref[...]
        top = jnp.max(highs, axis=0)
        total = jnp.sum(jnp.exp(highs - top[None]) * sums[...], axis=0)
        fill_share(share_ref, to_lanes(top + jnp.log(total)))


def column_sums(matrix_ref, scale, share_ref):
    sums = jnp.sum(matrix_ref[...].astype(F32) * scale, axis=0, keepdims=True)
    share_ref[...] = jnp.broadcast_to(to_lines(sums)[None], share_ref.shape).astype(share_ref.dtype)


def first_column_kernel(shares_ref, high_ref, matrix_ref, share_ref, scale_ref):
    step = pl.program_id(0)

    @pl.when(step == 0)
    def _():
        lines = scale_ref.shape[1] // LANES
        row_lse = merged(shares_ref[...][:, :lines])
        scale_ref[...] = jnp.exp(high_ref[...] - to_column(row_lse)[None])

    column_sums(matrix_ref, scale_ref[step], share_ref)


def later_column_kernel(shares_ref, scale_in_ref, matrix_ref, share_ref, scale_ref):
    step = pl.program_id(0)

    @pl.when(step == 0)
    def _():
        lines = scale_ref.shape[1] // LANES
        total = to_column(jnp.sum(shares_ref[...][:, :lines], axis=0))
        scale_ref[...] = scale_in_ref[...] / total[None]

    column_sums(matrix_ref, scale_ref[step], share_ref)


def later_row_kernel(shares_ref, scale_ref, matrix_ref, share_ref, sums):
    step = pl.program_id(0)
    inverse = to_row(1.0 / jnp.sum(shares_ref[...].astype(F32), axis=0))
    part = scale_ref[step] * jnp.sum(matrix_ref[...].astype(F32) * inverse, axis=1, keepdims=True)

    @pl.when(step == 0)
    def _():
        sums[...] = part

    @pl.when(step > 0)
    def _():
        sums[...] += part

    @pl.when(step == pl.num_programs(0) - 1)
    def _():
        fill_share(share_ref, to_lanes(sums[...]))


def split(values, parts):
    out = []
    for _ in range(parts):
        part = values.astype(BF16)
        out.append(part)
        values = values - part.astype(F32)
    return out


def pack(sums, numbers, parts, starts, counts):
    rows, width = sums.shape
    images = starts.shape[0]
    wide = jnp.broadcast_to(numbers, (rows, LANES))
    sent = jnp.concatenate([sums.astype(BF16)] + split(wide, parts), axis=1)
    chosen = spread(starts, counts, SLOT, rows)
    packed = jnp.dot(chosen, sent, preferred_element_type=F32).reshape(images, SLOT, width + parts * LANES)
    same = iota((1, SLOT, LANES), 1) == iota((1, SLOT, LANES), 2)
    tail = []
    for k in range(parts):
        part = packed[:, :, width + k * LANES : width + (k + 1) * LANES]
        tail.append(jnp.sum(jnp.where(same, part, 0.0), axis=1, keepdims=True))
    return packed[:, :MOST, :width].astype(BF16), join(tail, width)


def join(tail, width):
    images = tail[0].shape[0]
    filler = jnp.zeros((images, 1, width - LANES), F32)
    rows = [jnp.concatenate([part.astype(F32), filler], axis=2) for part in tail]
    rows.append(jnp.zeros((images, SLOT - MOST - len(tail), width), F32))
    return jnp.concatenate(rows, axis=1).astype(BF16)


def numbers_of(chunk, parts):
    tail = chunk[:, MOST:SLOT, :LANES].astype(F32)
    return sum(tail[:, k] for k in range(parts))


def put(own_ref, other_ref, rows, tail):
    half = own_ref.shape[0]
    own_ref[:, :MOST], own_ref[:, MOST:] = rows[:half], tail[:half]
    other_ref[:, :MOST], other_ref[:, MOST:] = rows[half:], tail[half:]


def slots_of(lanes):
    images = lanes.shape[0]
    same = iota((1, MOST, LANES), 1) == iota((1, MOST, LANES), 2)
    return jnp.sum(jnp.where(same, lanes.reshape(images, 1, LANES), 0.0), axis=2, keepdims=True)


def target_kernel(shares_ref, scale_ref, matrix_ref, protos_ref, places_ref, own_ref, other_ref, sums, total):
    step = pl.program_id(0)
    scale = scale_ref[step]
    inverse = to_row(1.0 / jnp.sum(shares_ref[...].astype(F32), axis=0))
    weights = matrix_ref[...].astype(F32) * inverse
    narrow = weights.astype(BF16)
    part = scale * lax.dot_general(narrow, protos_ref[...], (((1,), (1,)), ((), ())), preferred_element_type=F32)
    mass = scale * jnp.sum(narrow.astype(F32), axis=1, keepdims=True)

    @pl.when(step == 0)
    def _():
        sums[...] = part
        total[...] = mass

    @pl.when(step > 0)
    def _():
        sums[...] += part
        total[...] += mass

    @pl.when(step == pl.num_programs(0) - 1)
    def _():
        put(own_ref, other_ref, *pack(sums[...], total[...], 2, places_ref[0], places_ref[1]))


def target_merge_kernel(own_ref, came_ref, student_ref, out_ref):
    width = own_ref.shape[2]
    out_ref[:, :MOST] = (own_ref[:, :MOST].astype(F32) + came_ref[:, :MOST].astype(F32)).astype(BF16)
    total = numbers_of(own_ref, 2) + numbers_of(came_ref, 2)
    out_ref[:, MOST:SLOT] = join([part[:, None] for part in split(total, 2)], width)
    out_ref[:, SLOT:] = student_ref[...]


def student_kernel(gathered_ref, places_ref, protos_ref, own_ref, other_ref, rows_ref, sums, top, total):
    step = pl.program_id(0)
    rows = rows_ref.shape[0]

    @pl.when(step == 0)
    def _():
        images, slots, width = gathered_ref.shape
        flat = gathered_ref[...].reshape(images * slots, width)
        rows_ref[...] = compact(flat, places_ref[2], places_ref[3], rows)
        top[...] = jnp.full(top.shape, -1e30, F32)
        total[...] = jnp.zeros(total.shape, F32)
        sums[...] = jnp.zeros(sums.shape, F32)

    protos = protos_ref[...]
    logits = jnp.dot(rows_ref[...], protos, preferred_element_type=F32) * STUD
    before = top[...]
    high = jnp.maximum(before, jnp.max(logits, axis=1, keepdims=True))
    shrink = jnp.exp(before - high)
    exact = jnp.exp(logits - high)
    total[...] = total[...] * shrink + jnp.sum(exact, axis=1, keepdims=True)
    part = lax.dot_general(exact.astype(BF16), protos, (((1,), (1,)), ((), ())), preferred_element_type=F32)
    sums[...] = sums[...] * shrink + part
    top[...] = high

    @pl.when(step == pl.num_programs(0) - 1)
    def _():
        mean, own_lse = sums[...] / total[...], top[...] + jnp.log(total[...])
        put(own_ref, other_ref, *pack(mean, own_lse, 3, places_ref[0], places_ref[1]))


def blend(chunk, lse):
    joint = merged(lse)
    weights = slots_of(jnp.exp(lse - joint[None]))
    return jnp.sum(chunk * weights, axis=0), joint


def student_merge_kernel(own_ref, came_ref, out_ref):
    width = own_ref.shape[2]
    own, came = numbers_of(own_ref, 3), numbers_of(came_ref, 3)
    high = jnp.maximum(own, came)
    joint = high + jnp.log(jnp.exp(own - high) + jnp.exp(came - high))
    mean = own_ref[:, :MOST].astype(F32) * slots_of(jnp.exp(own - joint))
    mean = mean + came_ref[:, :MOST].astype(F32) * slots_of(jnp.exp(came - joint))
    out_ref[:, :MOST] = mean.astype(BF16)
    out_ref[:, MOST:] = join([part[:, None] for part in split(joint, 3)], width)


def finish_kernel(back_ref, picked_ref, order_ref, count_ref, grad_ref, loss_ref):
    patches, width = grad_ref.shape
    target = jnp.sum(back_ref[:, :SLOT].astype(F32), axis=0)
    mass = to_column((target[MOST : MOST + 1] + target[MOST + 1 : MOST + 2])[:, :LANES])[:MOST]
    tail = back_ref[:, SLOT + MOST : 2 * SLOT, :LANES].astype(F32)
    soft, lse_lanes = blend(back_ref[:, SLOT : SLOT + MOST].astype(F32), sum(tail[:, k] for k in range(3)))
    used = iota((MOST, 1), 0) < count_ref[0, 0]
    mean = target[:MOST] / jnp.where(used, mass, 1.0)
    own_lse = to_column(lse_lanes.reshape(1, LANES))[:MOST]
    cross = own_lse - STUD * jnp.sum(picked_ref[:MOST].astype(F32) * mean, axis=1, keepdims=True)
    cross = jnp.sum(jnp.where(used, cross, 0.0), axis=0, keepdims=True)
    loss_ref[...] = cross / jnp.full((1, 1), count_ref[0, 0], jnp.int32).astype(F32)
    rows = jnp.where(used, STUD * (soft - mean), 0.0)
    rows = jnp.concatenate([rows, jnp.zeros((LANES - MOST, width), F32)], axis=0).astype(BF16)
    order = jnp.broadcast_to(order_ref[:, :LANES], (patches, LANES))
    chosen = (iota((patches, LANES), 0) == order).astype(BF16)
    grad_ref[...] = jnp.dot(chosen, rows, preferred_element_type=F32).astype(BF16)


def body(student_patches, teacher_patches, mask_order, counts, student_protos, teacher_protos):
    width = lax.axis_size("proto")
    groups = lax.axis_size("dp")
    rows = MASK_DEV * width
    lines = rows // LANES
    patches, bot = student_patches.shape[1:]
    protos = student_protos.shape[1]
    steps = protos // BLOCK
    depth = 8
    index = lax.axis_index("proto").astype(jnp.int32).reshape(1, 1)
    over = functools.partial(lax.all_to_all, split_axis=0, concat_axis=0, tiled=True)
    wide = pl.BlockSpec((bot, BLOCK), lambda k: (0, k))
    peer = pl.BlockSpec((groups, BLOCK // LANES, LANES), lambda k: (0, k, 0))
    square = pl.BlockSpec((rows, BLOCK), lambda k: (0, k))
    grid = (steps,)
    student_patches, teacher_patches, mask_order, student_protos, teacher_protos = (
        pltpu.with_memory_space_constraint(a, pltpu.HBM)
        for a in (student_patches[0], teacher_patches[0], mask_order, student_protos, teacher_protos)
    )
    dot = 2 * rows * protos * bot
    column = pltpu.VMEM((rows, 1), F32)

    teacher_sent, student_sent = call(
        pick_kernel,
        [((SLOT, bot), BF16), ((LANES, bot), BF16)],
        teacher_patches,
        student_patches,
        mask_order,
        counts,
        in_specs=[VMEM, VMEM, VMEM, SMEM],
        moved=4 * patches * bot,
    )
    gathered_student = lax.all_gather(student_sent, "proto", axis=0, tiled=False)
    gathered = lax.all_gather(teacher_sent, "proto", axis=0, tiled=False)
    share, teacher_rows, places = call(
        column_kernel,
        [((groups, protos // LANES, LANES), F32), ((rows, bot), BF16), ((4, width, LANES), F32)],
        gathered,
        index,
        teacher_protos,
        grid=grid,
        in_specs=[VMEM, SMEM, wide],
        out_specs=[peer, VMEM, VMEM],
        flops=dot,
        moved=2 * bot * protos,
    )
    shares = over(share, "dp")
    matrix, high, share = call(
        row_kernel,
        [((rows, protos), BF16), ((steps, rows, 1), F32), ((width, depth, LANES), F32)],
        shares,
        teacher_rows,
        teacher_protos,
        grid=grid,
        in_specs=[peer, VMEM, wide],
        out_specs=[square, VMEM, VMEM],
        scratch=[pltpu.VMEM((steps, rows, 1), F32)],
        flops=dot,
        moved=2 * bot * protos + 2 * rows * protos,
    )
    shares = over(share, "proto")
    share, scale = call(
        first_column_kernel,
        [((groups, protos // LANES, LANES), BF16), ((steps, rows, 1), F32)],
        shares,
        high,
        matrix,
        grid=grid,
        in_specs=[VMEM, VMEM, square],
        out_specs=[peer, VMEM],
        moved=2 * rows * protos,
    )
    shares = over(share, "dp")
    share = call(
        later_row_kernel,
        [((width, depth, LANES), F32)],
        shares,
        scale,
        matrix,
        grid=grid,
        in_specs=[peer, VMEM, square],
        scratch=[column],
        moved=2 * rows * protos,
    )[0]
    shares = over(share, "proto")
    share, scale = call(
        later_column_kernel,
        [((groups, protos // LANES, LANES), BF16), ((steps, rows, 1), F32)],
        shares,
        scale,
        matrix,
        grid=grid,
        in_specs=[VMEM, VMEM, square],
        out_specs=[peer, VMEM],
        moved=2 * rows * protos,
    )
    shares = over(share, "dp")
    packed = ((width // 2, SLOT, bot), BF16)
    student_own, student_other = call(
        student_kernel,
        [packed, packed],
        gathered_student,
        places,
        student_protos,
        grid=grid,
        in_specs=[VMEM, VMEM, wide],
        scratch=[pltpu.VMEM((rows, bot), BF16), pltpu.VMEM((rows, bot), F32), column, column],
        flops=2 * dot,
        moved=2 * bot * protos,
    )
    swap = [(p, p ^ 1) for p in range(width)]
    student_came = lax.ppermute(student_other, "proto", swap)
    student_sum = call(student_merge_kernel, [packed], student_own, student_came)[0]
    own, other = call(
        target_kernel,
        [packed, packed],
        shares,
        scale,
        matrix,
        student_protos,
        places,
        grid=grid,
        in_specs=[peer, VMEM, square, wide, VMEM],
        scratch=[pltpu.VMEM((rows, bot), F32), column],
        flops=dot,
        moved=2 * rows * protos,
    )
    came = lax.ppermute(other, "proto", swap)
    sent = call(target_merge_kernel, [((width // 2, 2 * SLOT, bot), BF16)], own, came, student_sum)[0]
    same_core = [list(range(core, width, 2)) for core in range(2)]
    back = over(sent, "proto", axis_index_groups=same_core)
    student_grad, image_loss = call(
        finish_kernel,
        [((patches, bot), BF16), ((1, 1), F32)],
        back,
        student_sent,
        mask_order,
        counts,
        in_specs=[VMEM, VMEM, VMEM, SMEM],
        moved=2 * patches * bot,
    )
    return (student_grad[None], image_loss)


def solution(mesh):
    placed = (
        P(("dp", "proto"), None, None),
        P(("dp", "proto"), None, None),
        P(("dp", "proto"), None),
        P("dp", "proto"),
        P(None, "proto"),
        P(None, "proto"),
    )
    return jax.shard_map(
        body,
        mesh=mesh,
        in_specs=placed,
        out_specs=(P(("dp", "proto"), None, None), P("dp", "proto")),
        check_vma=False,
    )
```

```python
import functools

import jax
import jax.numpy as jnp
from jax import lax
from jax.experimental import pallas as pl
from jax.experimental.pallas import tpu as pltpu
from jax.sharding import PartitionSpec as P

MASK_DEV = 24
MOST = 72
EARLY = 40
LATE = (MOST - EARLY) // 2
SLOT = 80
TEACH = 1.0 / 0.07
STUD = 1.0 / 0.1
F32 = jnp.float32
BF16 = jnp.bfloat16
LANES = 128
BLOCK = 2048
LIMIT = 20 << 20
VMEM = pl.BlockSpec(memory_space=pltpu.VMEM)
SMEM = pl.BlockSpec(memory_space=pltpu.SMEM)


def call(kernel, out_shape, *args, grid=None, in_specs=None, out_specs=None, scratch=(), flops=0, moved=0):
    out_shape = [jax.ShapeDtypeStruct(s, d) for s, d in out_shape]
    extra = {} if grid is None else {"grid": grid}
    return pl.pallas_call(
        kernel,
        out_shape=out_shape,
        in_specs=[VMEM] * len(args) if in_specs is None else in_specs,
        out_specs=[VMEM] * len(out_shape) if out_specs is None else out_specs,
        scratch_shapes=list(scratch),
        compiler_params=pltpu.CompilerParams(vmem_limit_bytes=LIMIT),
        cost_estimate=pl.CostEstimate(flops=flops, bytes_accessed=moved, transcendentals=0),
        **extra,
    )(*args)


def iota(shape, dim):
    return lax.broadcasted_iota(jnp.int32, shape, dim)


def eye():
    return iota((LANES, LANES), 0) == iota((LANES, LANES), 1)


def to_lanes(column):
    parts = []
    for b in range(column.shape[0] // LANES):
        part = jnp.broadcast_to(column[b * LANES : (b + 1) * LANES], (LANES, LANES))
        parts.append(jnp.sum(jnp.where(eye(), part, 0.0), axis=0, keepdims=True))
    return jnp.concatenate(parts, axis=0)


def to_column(lanes):
    parts = []
    for b in range(lanes.shape[0]):
        part = jnp.broadcast_to(lanes[b : b + 1], (LANES, LANES))
        parts.append(jnp.sum(jnp.where(eye(), part, 0.0), axis=1, keepdims=True))
    return jnp.concatenate(parts, axis=0)


def to_lines(row):
    return jnp.concatenate([row[:, b * LANES : (b + 1) * LANES] for b in range(row.shape[1] // LANES)], axis=0)


def to_row(lines):
    return jnp.concatenate([lines[b : b + 1] for b in range(lines.shape[0])], axis=1)


def merged(shares):
    top = jnp.max(shares, axis=0)
    return top + jnp.log(jnp.sum(jnp.exp(shares - top[None]), axis=0))


def pick_kernel(teacher_ref, student_ref, order_ref, count_ref, sent_ref, late_ref, picked_ref):
    patches, width = teacher_ref.shape
    order = jnp.broadcast_to(order_ref[:, :LANES], (patches, LANES))
    chosen = (iota((patches, LANES), 0) == order).astype(BF16)
    dims = (((0,), (0,)), ((), ()))
    teacher = lax.dot_general(chosen, teacher_ref[...], dims, preferred_element_type=F32)
    student = lax.dot_general(chosen, student_ref[...], dims, preferred_element_type=F32)
    count = jnp.full((SLOT - MOST, width), count_ref[0, 0], jnp.int32).astype(F32)
    sent_ref[...] = jnp.concatenate([teacher[:MOST], count, student[:EARLY]], axis=0).astype(BF16)
    for half in range(2):
        late = student[EARLY + half * LATE : EARLY + (half + 1) * LATE]
        late_ref[half] = jnp.concatenate([late[:, :LANES], late[:, LANES:]], axis=0).astype(BF16)
    picked_ref[...] = student[:SLOT].astype(BF16)


def compact(gathered, starts, counts, rows, first, length, shift):
    images, slots, width = gathered.shape
    total = images * slots
    lane, image = iota((images, total), 1), iota((images, total), 0)
    within = lane - image * slots - first
    member = jnp.logical_and(within >= 0, within < length)
    place = (within + shift).astype(F32)
    used = jnp.logical_and(member, place < counts[:, :1])
    row = jnp.sum(jnp.where(used, starts[:, :1] + place + 1.0, 0.0), axis=0, keepdims=True) - 1.0
    chosen = (iota((rows, total), 0).astype(F32) == row).astype(BF16)
    return jnp.dot(chosen, gathered.reshape(total, width), preferred_element_type=F32)


def spread(starts, counts, slots, rows):
    images = starts.shape[0]
    shape = (images, slots, rows)
    within = iota(shape, 1)
    row = (iota(shape, 2) - within).astype(F32) - starts[:, :1].reshape(images, 1, 1)
    used = jnp.logical_and(row == 0.0, within.astype(F32) < counts[:, :1].reshape(images, 1, 1))
    return used.astype(F32).astype(BF16).reshape(images * slots, rows)


def column_kernel(gathered_ref, index_ref, protos_ref, share_ref, rows_ref, places_ref):
    images = gathered_ref.shape[0]
    rows = rows_ref.shape[0]

    @pl.when(pl.program_id(0) == 0)
    def _():
        counts = gathered_ref[:, MOST:MOST + 8, :LANES].astype(F32)[:, 0]
        before = (iota((images, images), 1) < iota((images, images), 0)).astype(BF16)
        starts = jnp.dot(before, counts.astype(BF16), preferred_element_type=F32)
        half, core = images // 2, index_ref[0, 0] % 2
        place = iota((images, images), 0)
        image = jnp.where(place < half, 2 * place + core, 2 * (place - half) + 1 - core)
        other = iota((images, images), 1)
        places_ref[0] = jnp.dot((other < image).astype(BF16), counts.astype(BF16), preferred_element_type=F32)
        places_ref[1] = jnp.dot((other == image).astype(BF16), counts.astype(BF16), preferred_element_type=F32)
        places_ref[2] = starts
        places_ref[3] = counts
        rows_ref[...] = compact(gathered_ref[...], starts, counts, rows, 0, MOST, 0).astype(BF16)

    logits = jnp.dot(rows_ref[...], protos_ref[...], preferred_element_type=F32) * TEACH
    high = jnp.max(logits, axis=0, keepdims=True)
    total = jnp.sum(jnp.exp(logits - high), axis=0, keepdims=True)
    share_ref[...] = jnp.broadcast_to(to_lines(high + jnp.log(total))[None], share_ref.shape)


def split(values, parts):
    out = []
    for _ in range(parts):
        part = values.astype(BF16)
        out.append(part)
        values = values - part.astype(F32)
    return out


def fill_share(share_ref, lines):
    blank = jnp.zeros((share_ref.shape[1] - lines.shape[0], LANES), F32)
    share_ref[...] = jnp.broadcast_to(jnp.concatenate([lines, blank], axis=0)[None], share_ref.shape)


def row_kernel(shares_ref, rows_ref, protos_ref, late_ref, matrix_ref, high_ref, share_ref, sums):
    step = pl.program_id(0)
    column = to_row(merged(shares_ref[...]))
    logits = jnp.dot(rows_ref[...], protos_ref[...], preferred_element_type=F32) * TEACH
    shifted = logits - column
    high = jnp.max(shifted, axis=1, keepdims=True)
    exact = jnp.exp(shifted - high)
    matrix_ref[...] = exact.astype(BF16)
    high_ref[step] = high
    sums[step] = jnp.sum(exact, axis=1, keepdims=True)

    @pl.when(step == pl.num_programs(0) - 1)
    def _():
        highs = high_ref[...]
        top = jnp.max(highs, axis=0)
        total = jnp.sum(jnp.exp(highs - top[None]) * sums[...], axis=0)
        own = jnp.concatenate([part.astype(F32) for part in split(to_lanes(top + jnp.log(total)), 3)], axis=0)
        blank = jnp.zeros((share_ref.shape[2] - 2 * LATE - own.shape[0], LANES), F32)
        numbers = jnp.concatenate([own, blank], axis=0).astype(BF16)
        for half in range(2):
            chunk = jnp.concatenate([late_ref[half], numbers], axis=0)
            share_ref[:, half] = jnp.broadcast_to(chunk[None], (share_ref.shape[0],) + chunk.shape)


def column_sums(matrix_ref, scale, share_ref):
    sums = jnp.sum(matrix_ref[...].astype(F32) * scale, axis=0, keepdims=True)
    share_ref[...] = jnp.broadcast_to(to_lines(sums)[None], share_ref.shape).astype(share_ref.dtype)


def first_column_kernel(shares_ref, high_ref, matrix_ref, share_ref, scale_ref):
    step = pl.program_id(0)

    @pl.when(step == 0)
    def _():
        lines = scale_ref.shape[1] // LANES
        numbers = shares_ref[:, 2 * LATE :].astype(F32)
        row_lse = merged(sum(numbers[:, k * lines : (k + 1) * lines] for k in range(3)))
        scale_ref[...] = jnp.exp(high_ref[...] - to_column(row_lse)[None])

    column_sums(matrix_ref, scale_ref[step], share_ref)


def later_column_kernel(shares_ref, scale_in_ref, matrix_ref, share_ref, scale_ref):
    step = pl.program_id(0)

    @pl.when(step == 0)
    def _():
        lines = scale_ref.shape[1] // LANES
        total = to_column(jnp.sum(shares_ref[...][:, :lines], axis=0))
        scale_ref[...] = scale_in_ref[...] / total[None]

    column_sums(matrix_ref, scale_ref[step], share_ref)


def later_row_kernel(shares_ref, scale_ref, matrix_ref, share_ref, sums):
    step = pl.program_id(0)
    inverse = to_row(1.0 / jnp.sum(shares_ref[...].astype(F32), axis=0))
    part = scale_ref[step] * jnp.sum(matrix_ref[...].astype(F32) * inverse, axis=1, keepdims=True)

    @pl.when(step == 0)
    def _():
        sums[...] = part

    @pl.when(step > 0)
    def _():
        sums[...] += part

    @pl.when(step == pl.num_programs(0) - 1)
    def _():
        fill_share(share_ref, to_lanes(sums[...]))


def pack(sums, numbers, parts, starts, counts):
    rows, width = sums.shape
    images = starts.shape[0]
    wide = jnp.broadcast_to(numbers, (rows, LANES))
    sent = jnp.concatenate([sums.astype(BF16)] + split(wide, parts), axis=1)
    chosen = spread(starts, counts, SLOT, rows)
    packed = jnp.dot(chosen, sent, preferred_element_type=F32).reshape(images, SLOT, width + parts * LANES)
    same = iota((1, SLOT, LANES), 1) == iota((1, SLOT, LANES), 2)
    tail = []
    for k in range(parts):
        part = packed[:, :, width + k * LANES : width + (k + 1) * LANES]
        tail.append(jnp.sum(jnp.where(same, part, 0.0), axis=1, keepdims=True))
    return packed[:, :MOST, :width].astype(BF16), join(tail, width)


def join(tail, width):
    images = tail[0].shape[0]
    filler = jnp.zeros((images, 1, width - LANES), F32)
    rows = [jnp.concatenate([part.astype(F32), filler], axis=2) for part in tail]
    rows.append(jnp.zeros((images, SLOT - MOST - len(tail), width), F32))
    return jnp.concatenate(rows, axis=1).astype(BF16)


def numbers_of(chunk, parts):
    tail = chunk[:, MOST:SLOT, :LANES].astype(F32)
    return sum(tail[:, k] for k in range(parts))


def put(own_ref, other_ref, rows, tail):
    half = own_ref.shape[0]
    own_ref[:, :MOST], own_ref[:, MOST:] = rows[:half], tail[:half]
    other_ref[:, :MOST], other_ref[:, MOST:] = rows[half:], tail[half:]


def slots_of(lanes):
    images = lanes.shape[0]
    same = iota((1, MOST, LANES), 1) == iota((1, MOST, LANES), 2)
    return jnp.sum(jnp.where(same, lanes.reshape(images, 1, LANES), 0.0), axis=2, keepdims=True)


def target_kernel(shares_ref, scale_ref, matrix_ref, protos_ref, places_ref, own_ref, other_ref, sums, total):
    step = pl.program_id(0)
    scale = scale_ref[step]
    inverse = to_row(1.0 / jnp.sum(shares_ref[...].astype(F32), axis=0))
    weights = matrix_ref[...].astype(F32) * inverse
    narrow = weights.astype(BF16)
    part = scale * lax.dot_general(narrow, protos_ref[...], (((1,), (1,)), ((), ())), preferred_element_type=F32)
    mass = scale * jnp.sum(narrow.astype(F32), axis=1, keepdims=True)

    @pl.when(step == 0)
    def _():
        sums[...] = part
        total[...] = mass

    @pl.when(step > 0)
    def _():
        sums[...] += part
        total[...] += mass

    @pl.when(step == pl.num_programs(0) - 1)
    def _():
        put(own_ref, other_ref, *pack(sums[...], total[...], 2, places_ref[0], places_ref[1]))


def target_merge_kernel(own_ref, came_ref, student_ref, out_ref):
    width = own_ref.shape[2]
    out_ref[:, :MOST] = (own_ref[:, :MOST].astype(F32) + came_ref[:, :MOST].astype(F32)).astype(BF16)
    total = numbers_of(own_ref, 2) + numbers_of(came_ref, 2)
    out_ref[:, MOST:SLOT] = join([part[:, None] for part in split(total, 2)], width)
    out_ref[:, SLOT:] = student_ref[...]


def student_kernel(
    gathered_ref, late_ref, came_ref, index_ref, places_ref, protos_ref, own_ref, other_ref, rows_ref, sums, top, total
):
    step = pl.program_id(0)
    rows = rows_ref.shape[0]

    @pl.when(step == 0)
    def _():
        starts, counts, core = places_ref[2], places_ref[3], index_ref[0, 0] % 2
        found = compact(gathered_ref[...], starts, counts, rows, SLOT, EARLY, 0)
        for ref, half in ((late_ref, core), (came_ref, 1 - core)):
            late = jnp.concatenate([ref[:, :LATE], ref[:, LATE : 2 * LATE]], axis=2)
            found += compact(late, starts, counts, rows, 0, LATE, EARLY + half * LATE)
        rows_ref[...] = found.astype(BF16)
        top[...] = jnp.full(top.shape, -1e30, F32)
        total[...] = jnp.zeros(total.shape, F32)
        sums[...] = jnp.zeros(sums.shape, F32)

    protos = protos_ref[...]
    logits = jnp.dot(rows_ref[...], protos, preferred_element_type=F32) * STUD
    before = top[...]
    high = jnp.maximum(before, jnp.max(logits, axis=1, keepdims=True))
    shrink = jnp.exp(before - high)
    exact = jnp.exp(logits - high)
    total[...] = total[...] * shrink + jnp.sum(exact, axis=1, keepdims=True)
    part = lax.dot_general(exact.astype(BF16), protos, (((1,), (1,)), ((), ())), preferred_element_type=F32)
    sums[...] = sums[...] * shrink + part
    top[...] = high

    @pl.when(step == pl.num_programs(0) - 1)
    def _():
        mean, own_lse = sums[...] / total[...], top[...] + jnp.log(total[...])
        put(own_ref, other_ref, *pack(mean, own_lse, 3, places_ref[0], places_ref[1]))


def blend(chunk, lse):
    joint = merged(lse)
    weights = slots_of(jnp.exp(lse - joint[None]))
    return jnp.sum(chunk * weights, axis=0), joint


def student_merge_kernel(own_ref, came_ref, out_ref):
    width = own_ref.shape[2]
    own, came = numbers_of(own_ref, 3), numbers_of(came_ref, 3)
    high = jnp.maximum(own, came)
    joint = high + jnp.log(jnp.exp(own - high) + jnp.exp(came - high))
    mean = own_ref[:, :MOST].astype(F32) * slots_of(jnp.exp(own - joint))
    mean = mean + came_ref[:, :MOST].astype(F32) * slots_of(jnp.exp(came - joint))
    out_ref[:, :MOST] = mean.astype(BF16)
    out_ref[:, MOST:] = join([part[:, None] for part in split(joint, 3)], width)


def finish_kernel(back_ref, picked_ref, order_ref, count_ref, grad_ref, loss_ref):
    patches, width = grad_ref.shape
    target = jnp.sum(back_ref[:, :SLOT].astype(F32), axis=0)
    mass = to_column((target[MOST : MOST + 1] + target[MOST + 1 : MOST + 2])[:, :LANES])[:MOST]
    tail = back_ref[:, SLOT + MOST : 2 * SLOT, :LANES].astype(F32)
    soft, lse_lanes = blend(back_ref[:, SLOT : SLOT + MOST].astype(F32), sum(tail[:, k] for k in range(3)))
    used = iota((MOST, 1), 0) < count_ref[0, 0]
    mean = target[:MOST] / jnp.where(used, mass, 1.0)
    own_lse = to_column(lse_lanes.reshape(1, LANES))[:MOST]
    cross = own_lse - STUD * jnp.sum(picked_ref[:MOST].astype(F32) * mean, axis=1, keepdims=True)
    cross = jnp.sum(jnp.where(used, cross, 0.0), axis=0, keepdims=True)
    loss_ref[...] = cross / jnp.full((1, 1), count_ref[0, 0], jnp.int32).astype(F32)
    rows = jnp.where(used, STUD * (soft - mean), 0.0)
    rows = jnp.concatenate([rows, jnp.zeros((LANES - MOST, width), F32)], axis=0).astype(BF16)
    order = jnp.broadcast_to(order_ref[:, :LANES], (patches, LANES))
    chosen = (iota((patches, LANES), 0) == order).astype(BF16)
    grad_ref[...] = jnp.dot(chosen, rows, preferred_element_type=F32).astype(BF16)


def body(student_patches, teacher_patches, mask_order, counts, student_protos, teacher_protos):
    width = lax.axis_size("proto")
    groups = lax.axis_size("dp")
    rows = MASK_DEV * width
    lines = rows // LANES
    patches, bot = student_patches.shape[1:]
    protos = student_protos.shape[1]
    steps = protos // BLOCK
    depth = 8
    index = lax.axis_index("proto").astype(jnp.int32).reshape(1, 1)
    over = functools.partial(lax.all_to_all, split_axis=0, concat_axis=0, tiled=True)
    wide = pl.BlockSpec((bot, BLOCK), lambda k: (0, k))
    peer = pl.BlockSpec((groups, BLOCK // LANES, LANES), lambda k: (0, k, 0))
    square = pl.BlockSpec((rows, BLOCK), lambda k: (0, k))
    grid = (steps,)
    student_patches, teacher_patches, mask_order, student_protos, teacher_protos = (
        pltpu.with_memory_space_constraint(a, pltpu.HBM)
        for a in (student_patches[0], teacher_patches[0], mask_order, student_protos, teacher_protos)
    )
    dot = 2 * rows * protos * bot
    column = pltpu.VMEM((rows, 1), F32)

    sent, late, picked = call(
        pick_kernel,
        [((SLOT + EARLY, bot), BF16), ((2, 2 * LATE, LANES), BF16), ((SLOT, bot), BF16)],
        teacher_patches,
        student_patches,
        mask_order,
        counts,
        in_specs=[VMEM, VMEM, VMEM, SMEM],
        moved=4 * patches * bot,
    )
    gathered = lax.all_gather(sent, "proto", axis=0, tiled=False)
    share, teacher_rows, places = call(
        column_kernel,
        [((groups, protos // LANES, LANES), F32), ((rows, bot), BF16), ((4, width, LANES), F32)],
        gathered,
        index,
        teacher_protos,
        grid=grid,
        in_specs=[VMEM, SMEM, wide],
        out_specs=[peer, VMEM, VMEM],
        flops=dot,
        moved=2 * bot * protos,
    )
    shares = over(share, "dp")
    matrix, high, share = call(
        row_kernel,
        [((rows, protos), BF16), ((steps, rows, 1), F32), ((width // 2, 2, 2 * LATE + 16, LANES), BF16)],
        shares,
        teacher_rows,
        teacher_protos,
        late,
        grid=grid,
        in_specs=[peer, VMEM, wide, VMEM],
        out_specs=[square, VMEM, VMEM],
        scratch=[pltpu.VMEM((steps, rows, 1), F32)],
        flops=dot,
        moved=2 * bot * protos + 2 * rows * protos,
    )
    swap = [(p, p ^ 1) for p in range(width)]
    shares = over(share.reshape((width,) + share.shape[2:]), "proto")
    late = shares
    late_came = lax.ppermute(late, "proto", swap)
    share, scale = call(
        first_column_kernel,
        [((groups, protos // LANES, LANES), BF16), ((steps, rows, 1), F32)],
        shares,
        high,
        matrix,
        grid=grid,
        in_specs=[VMEM, VMEM, square],
        out_specs=[peer, VMEM],
        moved=2 * rows * protos,
    )
    shares = over(share, "dp")
    share = call(
        later_row_kernel,
        [((width, depth, LANES), F32)],
        shares,
        scale,
        matrix,
        grid=grid,
        in_specs=[peer, VMEM, square],
        scratch=[column],
        moved=2 * rows * protos,
    )[0]
    shares = over(share, "proto")
    share, scale = call(
        later_column_kernel,
        [((groups, protos // LANES, LANES), BF16), ((steps, rows, 1), F32)],
        shares,
        scale,
        matrix,
        grid=grid,
        in_specs=[VMEM, VMEM, square],
        out_specs=[peer, VMEM],
        moved=2 * rows * protos,
    )
    shares = over(share, "dp")
    packed = ((width // 2, SLOT, bot), BF16)
    student_own, student_other = call(
        student_kernel,
        [packed, packed],
        gathered,
        late,
        late_came,
        index,
        places,
        student_protos,
        grid=grid,
        in_specs=[VMEM, VMEM, VMEM, SMEM, VMEM, wide],
        scratch=[pltpu.VMEM((rows, bot), BF16), pltpu.VMEM((rows, bot), F32), column, column],
        flops=2 * dot,
        moved=2 * bot * protos,
    )
    student_came = lax.ppermute(student_other, "proto", swap)
    student_sum = call(student_merge_kernel, [packed], student_own, student_came)[0]
    own, other = call(
        target_kernel,
        [packed, packed],
        shares,
        scale,
        matrix,
        student_protos,
        places,
        grid=grid,
        in_specs=[peer, VMEM, square, wide, VMEM],
        scratch=[pltpu.VMEM((rows, bot), F32), column],
        flops=dot,
        moved=2 * rows * protos,
    )
    came = lax.ppermute(other, "proto", swap)
    sent = call(target_merge_kernel, [((width // 2, 2 * SLOT, bot), BF16)], own, came, student_sum)[0]
    same_core = [list(range(core, width, 2)) for core in range(2)]
    back = over(sent, "proto", axis_index_groups=same_core)
    student_grad, image_loss = call(
        finish_kernel,
        [((patches, bot), BF16), ((1, 1), F32)],
        back,
        picked,
        mask_order,
        counts,
        in_specs=[VMEM, VMEM, VMEM, SMEM],
        moved=2 * patches * bot,
    )
    return (student_grad[None], image_loss)


def solution(mesh):
    placed = (
        P(("dp", "proto"), None, None),
        P(("dp", "proto"), None, None),
        P(("dp", "proto"), None),
        P("dp", "proto"),
        P(None, "proto"),
        P(None, "proto"),
    )
    return jax.shard_map(
        body,
        mesh=mesh,
        in_specs=placed,
        out_specs=(P(("dp", "proto"), None, None), P("dp", "proto")),
        check_vma=False,
    )
```

```python
import functools

import jax
import jax.numpy as jnp
from jax import lax
from jax.experimental import pallas as pl
from jax.experimental.pallas import tpu as pltpu
from jax.sharding import PartitionSpec as P

MASK_DEV = 24
MOST = 72
EARLY = 40
LATE = (MOST - EARLY) // 2
SLOT = 80
TEACH = 1.0 / 0.07
STUD = 1.0 / 0.1
F32 = jnp.float32
BF16 = jnp.bfloat16
LANES = 128
BLOCK = 2048
LIMIT = 20 << 20
VMEM = pl.BlockSpec(memory_space=pltpu.VMEM)
SMEM = pl.BlockSpec(memory_space=pltpu.SMEM)


def call(kernel, out_shape, *args, grid=None, in_specs=None, out_specs=None, scratch=(), flops=0, moved=0):
    out_shape = [jax.ShapeDtypeStruct(*o) if isinstance(o, tuple) else o for o in out_shape]
    extra = {} if grid is None else {"grid": grid}
    return pl.pallas_call(
        kernel,
        out_shape=out_shape,
        in_specs=[VMEM] * len(args) if in_specs is None else in_specs,
        out_specs=[VMEM] * len(out_shape) if out_specs is None else out_specs,
        scratch_shapes=list(scratch),
        compiler_params=pltpu.CompilerParams(vmem_limit_bytes=LIMIT),
        cost_estimate=pl.CostEstimate(flops=flops, bytes_accessed=moved, transcendentals=0),
        **extra,
    )(*args)


def iota(shape, dim):
    return lax.broadcasted_iota(jnp.int32, shape, dim)


def eye():
    return iota((LANES, LANES), 0) == iota((LANES, LANES), 1)


def to_lanes(column):
    parts = []
    for b in range(column.shape[0] // LANES):
        part = jnp.broadcast_to(column[b * LANES : (b + 1) * LANES], (LANES, LANES))
        parts.append(jnp.sum(jnp.where(eye(), part, 0.0), axis=0, keepdims=True))
    return jnp.concatenate(parts, axis=0)


def to_column(lanes):
    parts = []
    for b in range(lanes.shape[0]):
        part = jnp.broadcast_to(lanes[b : b + 1], (LANES, LANES))
        parts.append(jnp.sum(jnp.where(eye(), part, 0.0), axis=1, keepdims=True))
    return jnp.concatenate(parts, axis=0)


def to_lines(row):
    return jnp.concatenate([row[:, b * LANES : (b + 1) * LANES] for b in range(row.shape[1] // LANES)], axis=0)


def to_row(lines):
    return jnp.concatenate([lines[b : b + 1] for b in range(lines.shape[0])], axis=1)


def merged(shares):
    top = jnp.max(shares, axis=0)
    return top + jnp.log(jnp.sum(jnp.exp(shares - top[None]), axis=0))


def pick_kernel(teacher_ref, student_ref, order_ref, count_ref, sent_ref, late_ref, picked_ref):
    patches, width = teacher_ref.shape
    order = jnp.broadcast_to(order_ref[:, :LANES], (patches, LANES))
    chosen = (iota((patches, LANES), 0) == order).astype(BF16)
    dims = (((0,), (0,)), ((), ()))
    teacher = lax.dot_general(chosen, teacher_ref[...], dims, preferred_element_type=F32)
    student = lax.dot_general(chosen, student_ref[...], dims, preferred_element_type=F32)
    count = jnp.full((SLOT - MOST, width), count_ref[0, 0], jnp.int32).astype(F32)
    sent_ref[...] = jnp.concatenate([teacher[:MOST], count, student[:EARLY]], axis=0).astype(BF16)
    for half in range(2):
        late = student[EARLY + half * LATE : EARLY + (half + 1) * LATE]
        late_ref[half] = jnp.concatenate([late[:, :LANES], late[:, LANES:]], axis=0).astype(BF16)
    picked_ref[...] = student[:SLOT].astype(BF16)


def compact(gathered, starts, counts, rows, first, length, shift):
    images, slots, width = gathered.shape
    total = images * slots
    lane, image = iota((images, total), 1), iota((images, total), 0)
    within = lane - image * slots - first
    member = jnp.logical_and(within >= 0, within < length)
    place = (within + shift).astype(F32)
    used = jnp.logical_and(member, place < counts[:, :1])
    row = jnp.sum(jnp.where(used, starts[:, :1] + place + 1.0, 0.0), axis=0, keepdims=True) - 1.0
    chosen = (iota((rows, total), 0).astype(F32) == row).astype(BF16)
    return jnp.dot(chosen, gathered.reshape(total, width), preferred_element_type=F32)


def spread(starts, counts, slots, rows):
    images = starts.shape[0]
    shape = (images, slots, rows)
    within = iota(shape, 1)
    row = (iota(shape, 2) - within).astype(F32) - starts[:, :1].reshape(images, 1, 1)
    used = jnp.logical_and(row == 0.0, within.astype(F32) < counts[:, :1].reshape(images, 1, 1))
    return used.astype(F32).astype(BF16).reshape(images * slots, rows)


def column_kernel(gathered_ref, index_ref, protos_ref, share_ref, rows_ref, places_ref):
    images = gathered_ref.shape[0]
    rows = rows_ref.shape[0]

    @pl.when(pl.program_id(0) == 0)
    def _():
        counts = gathered_ref[:, MOST:MOST + 8, :LANES].astype(F32)[:, 0]
        before = (iota((images, images), 1) < iota((images, images), 0)).astype(BF16)
        starts = jnp.dot(before, counts.astype(BF16), preferred_element_type=F32)
        half, core = images // 2, index_ref[0, 0] % 2
        place = iota((images, images), 0)
        image = jnp.where(place < half, 2 * place + core, 2 * (place - half) + 1 - core)
        other = iota((images, images), 1)
        places_ref[0] = jnp.dot((other < image).astype(BF16), counts.astype(BF16), preferred_element_type=F32)
        places_ref[1] = jnp.dot((other == image).astype(BF16), counts.astype(BF16), preferred_element_type=F32)
        places_ref[2] = starts
        places_ref[3] = counts
        rows_ref[...] = compact(gathered_ref[:, :SLOT], starts, counts, rows, 0, MOST, 0).astype(BF16)

    logits = jnp.dot(rows_ref[...], protos_ref[...], preferred_element_type=F32) * TEACH
    high = jnp.max(logits, axis=0, keepdims=True)
    total = jnp.sum(jnp.exp(logits - high), axis=0, keepdims=True)
    share_ref[...] = jnp.broadcast_to(to_lines(high + jnp.log(total))[None], share_ref.shape)


def split(values, parts):
    out = []
    for _ in range(parts):
        part = values.astype(BF16)
        out.append(part)
        values = values - part.astype(F32)
    return out


def fill_share(share_ref, lines):
    blank = jnp.zeros((share_ref.shape[1] - lines.shape[0], LANES), F32)
    share_ref[...] = jnp.broadcast_to(jnp.concatenate([lines, blank], axis=0)[None], share_ref.shape)


def row_kernel(shares_ref, rows_ref, protos_ref, late_ref, matrix_ref, high_ref, share_ref, sums):
    step = pl.program_id(0)
    column = to_row(merged(shares_ref[...]))
    logits = jnp.dot(rows_ref[...], protos_ref[...], preferred_element_type=F32) * TEACH
    shifted = logits - column
    high = jnp.max(shifted, axis=1, keepdims=True)
    exact = jnp.exp(shifted - high)
    matrix_ref[...] = exact.astype(BF16)
    high_ref[step] = high
    sums[step] = jnp.sum(exact, axis=1, keepdims=True)

    @pl.when(step == pl.num_programs(0) - 1)
    def _():
        highs = high_ref[...]
        top = jnp.max(highs, axis=0)
        total = jnp.sum(jnp.exp(highs - top[None]) * sums[...], axis=0)
        own = jnp.concatenate([part.astype(F32) for part in split(to_lanes(top + jnp.log(total)), 3)], axis=0)
        blank = jnp.zeros((share_ref.shape[2] - 2 * LATE - own.shape[0], LANES), F32)
        numbers = jnp.concatenate([own, blank], axis=0).astype(BF16)
        for half in range(2):
            chunk = jnp.concatenate([late_ref[half], numbers], axis=0)
            share_ref[:, half] = jnp.broadcast_to(chunk[None], (share_ref.shape[0],) + chunk.shape)


def column_sums(matrix_ref, scale, share_ref):
    sums = jnp.sum(matrix_ref[...].astype(F32) * scale, axis=0, keepdims=True)
    share_ref[...] = jnp.broadcast_to(to_lines(sums)[None], share_ref.shape).astype(share_ref.dtype)


def first_column_kernel(shares_ref, high_ref, matrix_ref, share_ref, scale_ref):
    step = pl.program_id(0)

    @pl.when(step == 0)
    def _():
        lines = scale_ref.shape[1] // LANES
        numbers = shares_ref[:, 2 * LATE :].astype(F32)
        row_lse = merged(sum(numbers[:, k * lines : (k + 1) * lines] for k in range(3)))
        scale_ref[...] = jnp.exp(high_ref[...] - to_column(row_lse)[None])

    column_sums(matrix_ref, scale_ref[step], share_ref)


def later_column_kernel(shares_ref, scale_in_ref, matrix_ref, share_ref, scale_ref):
    step = pl.program_id(0)

    @pl.when(step == 0)
    def _():
        lines = scale_ref.shape[1] // LANES
        total = to_column(jnp.sum(shares_ref[...][:, :lines], axis=0))
        scale_ref[...] = scale_in_ref[...] / total[None]

    column_sums(matrix_ref, scale_ref[step], share_ref)


def later_row_kernel(shares_ref, scale_ref, matrix_ref, share_ref, sums):
    step = pl.program_id(0)
    inverse = to_row(1.0 / jnp.sum(shares_ref[...].astype(F32), axis=0))
    part = scale_ref[step] * jnp.sum(matrix_ref[...].astype(F32) * inverse, axis=1, keepdims=True)

    @pl.when(step == 0)
    def _():
        sums[...] = part

    @pl.when(step > 0)
    def _():
        sums[...] += part

    @pl.when(step == pl.num_programs(0) - 1)
    def _():
        fill_share(share_ref, to_lanes(sums[...]))


def pack(sums, numbers, parts, starts, counts):
    rows, width = sums.shape
    images = starts.shape[0]
    wide = jnp.broadcast_to(numbers, (rows, LANES))
    sent = jnp.concatenate([sums.astype(BF16)] + split(wide, parts), axis=1)
    chosen = spread(starts, counts, SLOT, rows)
    packed = jnp.dot(chosen, sent, preferred_element_type=F32).reshape(images, SLOT, width + parts * LANES)
    same = iota((1, SLOT, LANES), 1) == iota((1, SLOT, LANES), 2)
    tail = []
    for k in range(parts):
        part = packed[:, :, width + k * LANES : width + (k + 1) * LANES]
        tail.append(jnp.sum(jnp.where(same, part, 0.0), axis=1, keepdims=True))
    return packed[:, :MOST, :width].astype(BF16), join(tail, width)


def join(tail, width):
    images = tail[0].shape[0]
    filler = jnp.zeros((images, 1, width - LANES), F32)
    rows = [jnp.concatenate([part.astype(F32), filler], axis=2) for part in tail]
    rows.append(jnp.zeros((images, SLOT - MOST - len(tail), width), F32))
    return jnp.concatenate(rows, axis=1).astype(BF16)


def numbers_of(chunk, parts):
    tail = chunk[:, MOST:SLOT, :LANES].astype(F32)
    return sum(tail[:, k] for k in range(parts))


def put(own_ref, other_ref, rows, tail):
    half = own_ref.shape[0]
    own_ref[:, :MOST], own_ref[:, MOST:] = rows[:half], tail[:half]
    other_ref[:, :MOST], other_ref[:, MOST:] = rows[half:], tail[half:]


def slots_of(lanes):
    images = lanes.shape[0]
    same = iota((1, MOST, LANES), 1) == iota((1, MOST, LANES), 2)
    return jnp.sum(jnp.where(same, lanes.reshape(images, 1, LANES), 0.0), axis=2, keepdims=True)


def target_kernel(shares_ref, scale_ref, matrix_ref, protos_ref, places_ref, own_ref, other_ref, sums, total):
    step = pl.program_id(0)
    scale = scale_ref[step]
    inverse = to_row(1.0 / jnp.sum(shares_ref[...].astype(F32), axis=0))
    weights = matrix_ref[...].astype(F32) * inverse
    narrow = weights.astype(BF16)
    part = scale * lax.dot_general(narrow, protos_ref[...], (((1,), (1,)), ((), ())), preferred_element_type=F32)
    mass = scale * jnp.sum(narrow.astype(F32), axis=1, keepdims=True)

    @pl.when(step == 0)
    def _():
        sums[...] = part
        total[...] = mass

    @pl.when(step > 0)
    def _():
        sums[...] += part
        total[...] += mass

    @pl.when(step == pl.num_programs(0) - 1)
    def _():
        put(own_ref, other_ref, *pack(sums[...], total[...], 2, places_ref[0], places_ref[1]))


def target_merge_kernel(own_ref, came_ref, student_ref, out_ref):
    width = own_ref.shape[2]
    out_ref[:, :MOST] = (own_ref[:, :MOST].astype(F32) + came_ref[:, :MOST].astype(F32)).astype(BF16)
    total = numbers_of(own_ref, 2) + numbers_of(came_ref, 2)
    out_ref[:, MOST:SLOT] = join([part[:, None] for part in split(total, 2)], width)
    out_ref[:, SLOT:] = student_ref[...]


def student_kernel(
    gathered_ref, late_ref, came_ref, index_ref, places_ref, protos_ref, own_ref, other_ref, rows_ref, sums, top, total
):
    step = pl.program_id(0)
    rows = rows_ref.shape[0]

    @pl.when(step == 0)
    def _():
        starts, counts, core = places_ref[2], places_ref[3], index_ref[0, 0] % 2
        found = compact(gathered_ref[...], starts, counts, rows, SLOT, EARLY, 0)
        for ref, half in ((late_ref, core), (came_ref, 1 - core)):
            late = jnp.concatenate([ref[:, :LATE], ref[:, LATE : 2 * LATE]], axis=2)
            found += compact(late, starts, counts, rows, 0, LATE, EARLY + half * LATE)
        rows_ref[...] = found.astype(BF16)
        top[...] = jnp.full(top.shape, -1e30, F32)
        total[...] = jnp.zeros(total.shape, F32)
        sums[...] = jnp.zeros(sums.shape, F32)

    protos = protos_ref[...]
    logits = jnp.dot(rows_ref[...], protos, preferred_element_type=F32) * STUD
    before = top[...]
    high = jnp.maximum(before, jnp.max(logits, axis=1, keepdims=True))
    shrink = jnp.exp(before - high)
    exact = jnp.exp(logits - high)
    total[...] = total[...] * shrink + jnp.sum(exact, axis=1, keepdims=True)
    part = lax.dot_general(exact.astype(BF16), protos, (((1,), (1,)), ((), ())), preferred_element_type=F32)
    sums[...] = sums[...] * shrink + part
    top[...] = high

    @pl.when(step == pl.num_programs(0) - 1)
    def _():
        mean, own_lse = sums[...] / total[...], top[...] + jnp.log(total[...])
        put(own_ref, other_ref, *pack(mean, own_lse, 3, places_ref[0], places_ref[1]))


def blend(chunk, lse):
    joint = merged(lse)
    weights = slots_of(jnp.exp(lse - joint[None]))
    return jnp.sum(chunk * weights, axis=0), joint


def student_merge_kernel(own_ref, came_ref, out_ref):
    width = own_ref.shape[2]
    own, came = numbers_of(own_ref, 3), numbers_of(came_ref, 3)
    high = jnp.maximum(own, came)
    joint = high + jnp.log(jnp.exp(own - high) + jnp.exp(came - high))
    mean = own_ref[:, :MOST].astype(F32) * slots_of(jnp.exp(own - joint))
    mean = mean + came_ref[:, :MOST].astype(F32) * slots_of(jnp.exp(came - joint))
    out_ref[:, :MOST] = mean.astype(BF16)
    out_ref[:, MOST:] = join([part[:, None] for part in split(joint, 3)], width)


def finish_kernel(back_ref, picked_ref, order_ref, count_ref, grad_ref, loss_ref):
    patches, width = grad_ref.shape
    target = jnp.sum(back_ref[:, :SLOT].astype(F32), axis=0)
    mass = to_column((target[MOST : MOST + 1] + target[MOST + 1 : MOST + 2])[:, :LANES])[:MOST]
    tail = back_ref[:, SLOT + MOST : 2 * SLOT, :LANES].astype(F32)
    soft, lse_lanes = blend(back_ref[:, SLOT : SLOT + MOST].astype(F32), sum(tail[:, k] for k in range(3)))
    used = iota((MOST, 1), 0) < count_ref[0, 0]
    mean = target[:MOST] / jnp.where(used, mass, 1.0)
    own_lse = to_column(lse_lanes.reshape(1, LANES))[:MOST]
    cross = own_lse - STUD * jnp.sum(picked_ref[:MOST].astype(F32) * mean, axis=1, keepdims=True)
    cross = jnp.sum(jnp.where(used, cross, 0.0), axis=0, keepdims=True)
    loss_ref[...] = cross / jnp.full((1, 1), count_ref[0, 0], jnp.int32).astype(F32)
    rows = jnp.where(used, STUD * (soft - mean), 0.0)
    rows = jnp.concatenate([rows, jnp.zeros((LANES - MOST, width), F32)], axis=0).astype(BF16)
    order = jnp.broadcast_to(order_ref[:, :LANES], (patches, LANES))
    chosen = (iota((patches, LANES), 0) == order).astype(BF16)
    grad_ref[...] = jnp.dot(chosen, rows, preferred_element_type=F32).astype(BF16)


def body(student_patches, teacher_patches, mask_order, counts, student_protos, teacher_protos):
    width = lax.axis_size("proto")
    groups = lax.axis_size("dp")
    rows = MASK_DEV * width
    lines = rows // LANES
    patches, bot = student_patches.shape[1:]
    protos = student_protos.shape[1]
    steps = protos // BLOCK
    depth = 8
    index = lax.axis_index("proto").astype(jnp.int32).reshape(1, 1)
    over = functools.partial(lax.all_to_all, split_axis=0, concat_axis=0, tiled=True)
    wide = pl.BlockSpec((bot, BLOCK), lambda k: (0, k))
    peer = pl.BlockSpec((groups, BLOCK // LANES, LANES), lambda k: (0, k, 0))
    square = pl.BlockSpec((rows, BLOCK), lambda k: (0, k))
    grid = (steps,)
    student_patches, teacher_patches, mask_order, student_protos, teacher_protos = (
        pltpu.with_memory_space_constraint(a, pltpu.HBM)
        for a in (student_patches[0], teacher_patches[0], mask_order, student_protos, teacher_protos)
    )
    dot = 2 * rows * protos * bot
    column = pltpu.VMEM((rows, 1), F32)

    sent, late, picked = call(
        pick_kernel,
        [((SLOT + EARLY, bot), BF16), ((2, 2 * LATE, LANES), BF16), ((SLOT, bot), BF16)],
        teacher_patches,
        student_patches,
        mask_order,
        counts,
        in_specs=[VMEM, VMEM, VMEM, SMEM],
        moved=4 * patches * bot,
    )
    gathered = lax.all_gather(sent, "proto", axis=0, tiled=False)
    share, teacher_rows, places = call(
        column_kernel,
        [((groups, protos // LANES, LANES), F32), ((rows, bot), BF16), ((4, width, LANES), F32)],
        gathered,
        index,
        teacher_protos,
        grid=grid,
        in_specs=[VMEM, SMEM, wide],
        out_specs=[peer, VMEM, VMEM],
        flops=dot,
        moved=2 * bot * protos,
    )
    shares = over(share, "dp")
    matrix, high, share = call(
        row_kernel,
        [((rows, protos), BF16), ((steps, rows, 1), F32), ((width // 2, 2, 2 * LATE + 16, LANES), BF16)],
        shares,
        teacher_rows,
        teacher_protos,
        late,
        grid=grid,
        in_specs=[peer, VMEM, wide, VMEM],
        out_specs=[square, VMEM, VMEM],
        scratch=[pltpu.VMEM((steps, rows, 1), F32)],
        flops=dot,
        moved=2 * bot * protos + 2 * rows * protos,
    )
    swap = [(p, p ^ 1) for p in range(width)]
    shares = over(share.reshape((width,) + share.shape[2:]), "proto")
    late = shares
    late_came = lax.ppermute(late, "proto", swap)
    share, scale = call(
        first_column_kernel,
        [pltpu.HBM((groups, protos // LANES, LANES), BF16), pltpu.HBM((steps, rows, 1), F32)],
        shares,
        high,
        matrix,
        grid=grid,
        in_specs=[VMEM, VMEM, square],
        out_specs=[peer, VMEM],
        moved=2 * rows * protos,
    )
    packed = ((width // 2, SLOT, bot), BF16)
    student_own, student_other = call(
        student_kernel,
        [packed, packed],
        gathered,
        late,
        late_came,
        index,
        places,
        student_protos,
        grid=grid,
        in_specs=[VMEM, VMEM, VMEM, SMEM, VMEM, wide],
        scratch=[pltpu.VMEM((rows, bot), BF16), pltpu.VMEM((rows, bot), F32), column, column],
        flops=2 * dot,
        moved=2 * bot * protos,
    )
    student_came = lax.ppermute(student_other, "proto", swap)
    student_sum = call(student_merge_kernel, [packed], student_own, student_came)[0]
    shares, student_sum = lax.optimization_barrier((over(share, "dp"), student_sum))
    share = call(
        later_row_kernel,
        [((width, depth, LANES), F32)],
        shares,
        scale,
        matrix,
        grid=grid,
        in_specs=[peer, VMEM, square],
        scratch=[column],
        moved=2 * rows * protos,
    )[0]
    shares = over(share, "proto")
    share, scale = call(
        later_column_kernel,
        [((groups, protos // LANES, LANES), BF16), ((steps, rows, 1), F32)],
        shares,
        scale,
        matrix,
        grid=grid,
        in_specs=[VMEM, VMEM, square],
        out_specs=[peer, VMEM],
        moved=2 * rows * protos,
    )
    shares = over(share, "dp")
    own, other = call(
        target_kernel,
        [packed, packed],
        shares,
        scale,
        matrix,
        student_protos,
        places,
        grid=grid,
        in_specs=[peer, VMEM, square, wide, VMEM],
        scratch=[pltpu.VMEM((rows, bot), F32), column],
        flops=dot,
        moved=2 * rows * protos,
    )
    came = lax.ppermute(other, "proto", swap)
    sent = call(target_merge_kernel, [((width // 2, 2 * SLOT, bot), BF16)], own, came, student_sum)[0]
    same_core = [list(range(core, width, 2)) for core in range(2)]
    back = over(sent, "proto", axis_index_groups=same_core)
    student_grad, image_loss = call(
        finish_kernel,
        [((patches, bot), BF16), ((1, 1), F32)],
        back,
        picked,
        mask_order,
        counts,
        in_specs=[VMEM, VMEM, VMEM, SMEM],
        moved=2 * patches * bot,
    )
    return (student_grad[None], image_loss)


def solution(mesh):
    placed = (
        P(("dp", "proto"), None, None),
        P(("dp", "proto"), None, None),
        P(("dp", "proto"), None),
        P("dp", "proto"),
        P(None, "proto"),
        P(None, "proto"),
    )
    return jax.shard_map(
        body,
        mesh=mesh,
        in_specs=placed,
        out_specs=(P(("dp", "proto"), None, None), P("dp", "proto")),
        check_vma=False,
    )
```

```python
import functools

import jax
import jax.numpy as jnp
from jax import lax
from jax.experimental import pallas as pl
from jax.experimental.pallas import tpu as pltpu
from jax.sharding import PartitionSpec as P

MASK_DEV = 24
MOST = 72
EARLY = 40
LATE = (MOST - EARLY) // 2
SLOT = 80
TEACH = 1.0 / 0.07
STUD = 1.0 / 0.1
F32 = jnp.float32
BF16 = jnp.bfloat16
LANES = 128
BLOCK = 2048
LIMIT = 20 << 20
VMEM = pl.BlockSpec(memory_space=pltpu.VMEM)
SMEM = pl.BlockSpec(memory_space=pltpu.SMEM)


def call(kernel, out_shape, *args, grid=None, in_specs=None, out_specs=None, scratch=(), flops=0, moved=0):
    out_shape = [jax.ShapeDtypeStruct(*o) if isinstance(o, tuple) else o for o in out_shape]
    extra = {} if grid is None else {"grid": grid}
    return pl.pallas_call(
        kernel,
        out_shape=out_shape,
        in_specs=[VMEM] * len(args) if in_specs is None else in_specs,
        out_specs=[VMEM] * len(out_shape) if out_specs is None else out_specs,
        scratch_shapes=list(scratch),
        compiler_params=pltpu.CompilerParams(vmem_limit_bytes=LIMIT),
        cost_estimate=pl.CostEstimate(flops=flops, bytes_accessed=moved, transcendentals=0),
        **extra,
    )(*args)


def iota(shape, dim):
    return lax.broadcasted_iota(jnp.int32, shape, dim)


def eye():
    return iota((LANES, LANES), 0) == iota((LANES, LANES), 1)


def to_lanes(column):
    parts = []
    for b in range(column.shape[0] // LANES):
        part = jnp.broadcast_to(column[b * LANES : (b + 1) * LANES], (LANES, LANES))
        parts.append(jnp.sum(jnp.where(eye(), part, 0.0), axis=0, keepdims=True))
    return jnp.concatenate(parts, axis=0)


def to_column(lanes):
    parts = []
    for b in range(lanes.shape[0]):
        part = jnp.broadcast_to(lanes[b : b + 1], (LANES, LANES))
        parts.append(jnp.sum(jnp.where(eye(), part, 0.0), axis=1, keepdims=True))
    return jnp.concatenate(parts, axis=0)


def to_lines(row):
    return jnp.concatenate([row[:, b * LANES : (b + 1) * LANES] for b in range(row.shape[1] // LANES)], axis=0)


def to_row(lines):
    return jnp.concatenate([lines[b : b + 1] for b in range(lines.shape[0])], axis=1)


def merged(shares):
    top = jnp.max(shares, axis=0)
    return top + jnp.log(jnp.sum(jnp.exp(shares - top[None]), axis=0))


def pick_kernel(teacher_ref, student_ref, order_ref, count_ref, sent_ref, late_ref, picked_ref):
    patches, width = teacher_ref.shape
    order = jnp.broadcast_to(order_ref[:, :LANES], (patches, LANES))
    chosen = (iota((patches, LANES), 0) == order).astype(BF16)
    dims = (((0,), (0,)), ((), ()))
    teacher = lax.dot_general(chosen, teacher_ref[...], dims, preferred_element_type=F32)
    student = lax.dot_general(chosen, student_ref[...], dims, preferred_element_type=F32)
    count = jnp.full((SLOT - MOST, width), count_ref[0, 0], jnp.int32).astype(F32)
    sent_ref[...] = jnp.concatenate([teacher[:MOST], count, student[:EARLY]], axis=0).astype(BF16)
    for half in range(2):
        late = student[EARLY + half * LATE : EARLY + (half + 1) * LATE]
        late_ref[half] = jnp.concatenate([late[:, :LANES], late[:, LANES:]], axis=0).astype(BF16)
    picked_ref[...] = student[:SLOT].astype(BF16)


def compact(gathered, starts, counts, rows, first, length, shift):
    images, slots, width = gathered.shape
    total = images * slots
    lane, image = iota((images, total), 1), iota((images, total), 0)
    within = lane - image * slots - first
    member = jnp.logical_and(within >= 0, within < length)
    place = (within + shift).astype(F32)
    used = jnp.logical_and(member, place < counts[:, :1])
    row = jnp.sum(jnp.where(used, starts[:, :1] + place + 1.0, 0.0), axis=0, keepdims=True) - 1.0
    chosen = (iota((rows, total), 0).astype(F32) == row).astype(BF16)
    return jnp.dot(chosen, gathered.reshape(total, width), preferred_element_type=F32)


def spread(starts, counts, slots, rows):
    images = starts.shape[0]
    shape = (images, slots, rows)
    within = iota(shape, 1)
    row = (iota(shape, 2) - within).astype(F32) - starts[:, :1].reshape(images, 1, 1)
    used = jnp.logical_and(row == 0.0, within.astype(F32) < counts[:, :1].reshape(images, 1, 1))
    return used.astype(F32).astype(BF16).reshape(images * slots, rows)


def column_kernel(gathered_ref, index_ref, protos_ref, share_ref, rows_ref, places_ref):
    images = gathered_ref.shape[0]
    rows = rows_ref.shape[0]

    @pl.when(pl.program_id(0) == 0)
    def _():
        counts = gathered_ref[:, MOST:MOST + 8, :LANES].astype(F32)[:, 0]
        before = (iota((images, images), 1) < iota((images, images), 0)).astype(BF16)
        starts = jnp.dot(before, counts.astype(BF16), preferred_element_type=F32)
        half, core = images // 2, index_ref[0, 0] % 2
        place = iota((images, images), 0)
        image = jnp.where(place < half, 2 * place + core, 2 * (place - half) + 1 - core)
        other = iota((images, images), 1)
        places_ref[0] = jnp.dot((other < image).astype(BF16), counts.astype(BF16), preferred_element_type=F32)
        places_ref[1] = jnp.dot((other == image).astype(BF16), counts.astype(BF16), preferred_element_type=F32)
        places_ref[2] = starts
        places_ref[3] = counts
        rows_ref[...] = compact(gathered_ref[:, :SLOT], starts, counts, rows, 0, MOST, 0).astype(BF16)

    logits = jnp.dot(rows_ref[...], protos_ref[...], preferred_element_type=F32) * TEACH
    high = jnp.max(logits, axis=0, keepdims=True)
    total = jnp.sum(jnp.exp(logits - high), axis=0, keepdims=True)
    share_ref[...] = jnp.broadcast_to(to_lines(high + jnp.log(total))[None], share_ref.shape)


def split(values, parts):
    out = []
    for _ in range(parts):
        part = values.astype(BF16)
        out.append(part)
        values = values - part.astype(F32)
    return out


def fill_share(share_ref, lines):
    blank = jnp.zeros((share_ref.shape[1] - lines.shape[0], LANES), F32)
    share_ref[...] = jnp.broadcast_to(jnp.concatenate([lines, blank], axis=0)[None], share_ref.shape)


def row_kernel(shares_ref, rows_ref, protos_ref, late_ref, matrix_ref, high_ref, share_ref, sums):
    step = pl.program_id(0)
    column = to_row(merged(shares_ref[...]))
    logits = jnp.dot(rows_ref[...], protos_ref[...], preferred_element_type=F32) * TEACH
    shifted = logits - column
    high = jnp.max(shifted, axis=1, keepdims=True)
    exact = jnp.exp(shifted - high)
    matrix_ref[...] = exact.astype(BF16)
    high_ref[step] = high
    sums[step] = jnp.sum(exact, axis=1, keepdims=True)

    @pl.when(step == pl.num_programs(0) - 1)
    def _():
        highs = high_ref[...]
        top = jnp.max(highs, axis=0)
        total = jnp.sum(jnp.exp(highs - top[None]) * sums[...], axis=0)
        own = jnp.concatenate([part.astype(F32) for part in split(to_lanes(top + jnp.log(total)), 3)], axis=0)
        blank = jnp.zeros((share_ref.shape[2] - 2 * LATE - own.shape[0], LANES), F32)
        numbers = jnp.concatenate([own, blank], axis=0).astype(BF16)
        for half in range(2):
            chunk = jnp.concatenate([late_ref[half], numbers], axis=0)
            share_ref[:, half] = jnp.broadcast_to(chunk[None], (share_ref.shape[0],) + chunk.shape)


def column_sums(matrix_ref, scale, share_ref):
    sums = jnp.sum(matrix_ref[...].astype(F32) * scale, axis=0, keepdims=True)
    share_ref[...] = jnp.broadcast_to(to_lines(sums)[None], share_ref.shape).astype(share_ref.dtype)


def first_column_kernel(shares_ref, high_ref, matrix_ref, share_ref, scale_ref):
    step = pl.program_id(0)

    @pl.when(step == 0)
    def _():
        lines = scale_ref.shape[1] // LANES
        numbers = shares_ref[:, 2 * LATE :].astype(F32)
        row_lse = merged(sum(numbers[:, k * lines : (k + 1) * lines] for k in range(3)))
        scale_ref[...] = jnp.exp(high_ref[...] - to_column(row_lse)[None])

    column_sums(matrix_ref, scale_ref[step], share_ref)


def later_column_kernel(shares_ref, scale_in_ref, matrix_ref, share_ref, scale_ref):
    step = pl.program_id(0)

    @pl.when(step == 0)
    def _():
        lines = scale_ref.shape[1] // LANES
        total = to_column(jnp.sum(shares_ref[...][:, :lines], axis=0))
        scale_ref[...] = scale_in_ref[...] / total[None]

    column_sums(matrix_ref, scale_ref[step], share_ref)


def later_row_kernel(shares_ref, scale_ref, matrix_ref, share_ref, sums):
    step = pl.program_id(0)
    inverse = to_row(1.0 / jnp.sum(shares_ref[...].astype(F32), axis=0))
    part = scale_ref[step] * jnp.sum(matrix_ref[...].astype(F32) * inverse, axis=1, keepdims=True)

    @pl.when(step == 0)
    def _():
        sums[...] = part

    @pl.when(step > 0)
    def _():
        sums[...] += part

    @pl.when(step == pl.num_programs(0) - 1)
    def _():
        fill_share(share_ref, to_lanes(sums[...]))


def pack(sums, numbers, parts, starts, counts):
    rows, width = sums.shape
    images = starts.shape[0]
    wide = jnp.broadcast_to(numbers, (rows, LANES))
    sent = jnp.concatenate([sums.astype(BF16)] + split(wide, parts), axis=1)
    chosen = spread(starts, counts, SLOT, rows)
    packed = jnp.dot(chosen, sent, preferred_element_type=F32).reshape(images, SLOT, width + parts * LANES)
    same = iota((1, SLOT, LANES), 1) == iota((1, SLOT, LANES), 2)
    tail = []
    for k in range(parts):
        part = packed[:, :, width + k * LANES : width + (k + 1) * LANES]
        tail.append(jnp.sum(jnp.where(same, part, 0.0), axis=1, keepdims=True))
    return packed[:, :MOST, :width].astype(BF16), join(tail, width)


def join(tail, width):
    images = tail[0].shape[0]
    filler = jnp.zeros((images, 1, width - LANES), F32)
    rows = [jnp.concatenate([part.astype(F32), filler], axis=2) for part in tail]
    rows.append(jnp.zeros((images, SLOT - MOST - len(tail), width), F32))
    return jnp.concatenate(rows, axis=1).astype(BF16)


def numbers_of(chunk, parts):
    tail = chunk[:, MOST:SLOT, :LANES].astype(F32)
    return sum(tail[:, k] for k in range(parts))


def put(own_ref, other_ref, rows, tail):
    half = own_ref.shape[0]
    own_ref[:, :MOST], own_ref[:, MOST:] = rows[:half], tail[:half]
    other_ref[:, :MOST], other_ref[:, MOST:] = rows[half:], tail[half:]


def slots_of(lanes):
    images = lanes.shape[0]
    same = iota((1, MOST, LANES), 1) == iota((1, MOST, LANES), 2)
    return jnp.sum(jnp.where(same, lanes.reshape(images, 1, LANES), 0.0), axis=2, keepdims=True)


def target_kernel(shares_ref, scale_ref, matrix_ref, protos_ref, places_ref, own_ref, other_ref, sums, total):
    step = pl.program_id(0)
    scale = scale_ref[step]
    inverse = to_row(1.0 / jnp.sum(shares_ref[...].astype(F32), axis=0))
    weights = matrix_ref[...].astype(F32) * inverse
    narrow = weights.astype(BF16)
    part = scale * lax.dot_general(narrow, protos_ref[...], (((1,), (1,)), ((), ())), preferred_element_type=F32)
    mass = scale * jnp.sum(narrow.astype(F32), axis=1, keepdims=True)

    @pl.when(step == 0)
    def _():
        sums[...] = part
        total[...] = mass

    @pl.when(step > 0)
    def _():
        sums[...] += part
        total[...] += mass

    @pl.when(step == pl.num_programs(0) - 1)
    def _():
        put(own_ref, other_ref, *pack(sums[...], total[...], 2, places_ref[0], places_ref[1]))


def merge_kernel(own_ref, came_ref, student_own_ref, student_came_ref, out_ref):
    width = own_ref.shape[2]
    out_ref[:, :MOST] = (own_ref[:, :MOST].astype(F32) + came_ref[:, :MOST].astype(F32)).astype(BF16)
    total = numbers_of(own_ref, 2) + numbers_of(came_ref, 2)
    out_ref[:, MOST:SLOT] = join([part[:, None] for part in split(total, 2)], width)
    own, came = numbers_of(student_own_ref, 3), numbers_of(student_came_ref, 3)
    high = jnp.maximum(own, came)
    joint = high + jnp.log(jnp.exp(own - high) + jnp.exp(came - high))
    mean = student_own_ref[:, :MOST].astype(F32) * slots_of(jnp.exp(own - joint))
    mean = mean + student_came_ref[:, :MOST].astype(F32) * slots_of(jnp.exp(came - joint))
    out_ref[:, SLOT : SLOT + MOST] = mean.astype(BF16)
    out_ref[:, SLOT + MOST :] = join([part[:, None] for part in split(joint, 3)], width)


def student_kernel(
    gathered_ref, late_ref, came_ref, index_ref, places_ref, protos_ref, own_ref, other_ref, rows_ref, sums, top, total
):
    step = pl.program_id(0)
    rows = rows_ref.shape[0]

    @pl.when(step == 0)
    def _():
        starts, counts, core = places_ref[2], places_ref[3], index_ref[0, 0] % 2
        found = compact(gathered_ref[:, SLOT:], starts, counts, rows, 0, EARLY, 0)
        for ref, half in ((late_ref, core), (came_ref, 1 - core)):
            late = jnp.concatenate([ref[:, :LATE], ref[:, LATE : 2 * LATE]], axis=2)
            found += compact(late, starts, counts, rows, 0, LATE, EARLY + half * LATE)
        rows_ref[...] = found.astype(BF16)
        top[...] = jnp.full(top.shape, -1e30, F32)
        total[...] = jnp.zeros(total.shape, F32)
        sums[...] = jnp.zeros(sums.shape, F32)

    protos = protos_ref[...]
    logits = jnp.dot(rows_ref[...], protos, preferred_element_type=F32) * STUD
    before = top[...]
    high = jnp.maximum(before, jnp.max(logits, axis=1, keepdims=True))
    shrink = jnp.exp(before - high)
    exact = jnp.exp(logits - high)
    total[...] = total[...] * shrink + jnp.sum(exact, axis=1, keepdims=True)
    part = lax.dot_general(exact.astype(BF16), protos, (((1,), (1,)), ((), ())), preferred_element_type=F32)
    sums[...] = sums[...] * shrink + part
    top[...] = high

    @pl.when(step == pl.num_programs(0) - 1)
    def _():
        mean, own_lse = sums[...] / total[...], top[...] + jnp.log(total[...])
        put(own_ref, other_ref, *pack(mean, own_lse, 3, places_ref[0], places_ref[1]))


def blend(chunk, lse):
    joint = merged(lse)
    weights = slots_of(jnp.exp(lse - joint[None]))
    return jnp.sum(chunk * weights, axis=0), joint


def finish_kernel(back_ref, picked_ref, order_ref, count_ref, grad_ref, loss_ref):
    patches, width = grad_ref.shape
    target = jnp.sum(back_ref[:, :SLOT].astype(F32), axis=0)
    mass = to_column((target[MOST : MOST + 1] + target[MOST + 1 : MOST + 2])[:, :LANES])[:MOST]
    tail = back_ref[:, SLOT + MOST : 2 * SLOT, :LANES].astype(F32)
    soft, lse_lanes = blend(back_ref[:, SLOT : SLOT + MOST].astype(F32), sum(tail[:, k] for k in range(3)))
    used = iota((MOST, 1), 0) < count_ref[0, 0]
    mean = target[:MOST] / jnp.where(used, mass, 1.0)
    own_lse = to_column(lse_lanes.reshape(1, LANES))[:MOST]
    cross = own_lse - STUD * jnp.sum(picked_ref[:MOST].astype(F32) * mean, axis=1, keepdims=True)
    cross = jnp.sum(jnp.where(used, cross, 0.0), axis=0, keepdims=True)
    loss_ref[...] = cross / jnp.full((1, 1), count_ref[0, 0], jnp.int32).astype(F32)
    rows = jnp.where(used, STUD * (soft - mean), 0.0)
    rows = jnp.concatenate([rows, jnp.zeros((LANES - MOST, width), F32)], axis=0).astype(BF16)
    order = jnp.broadcast_to(order_ref[:, :LANES], (patches, LANES))
    chosen = (iota((patches, LANES), 0) == order).astype(BF16)
    grad_ref[...] = jnp.dot(chosen, rows, preferred_element_type=F32).astype(BF16)


def body(student_patches, teacher_patches, mask_order, counts, student_protos, teacher_protos):
    width = lax.axis_size("proto")
    groups = lax.axis_size("dp")
    rows = MASK_DEV * width
    lines = rows // LANES
    patches, bot = student_patches.shape[1:]
    protos = student_protos.shape[1]
    steps = protos // BLOCK
    depth = 8
    index = lax.axis_index("proto").astype(jnp.int32).reshape(1, 1)
    over = functools.partial(lax.all_to_all, split_axis=0, concat_axis=0, tiled=True)
    wide = pl.BlockSpec((bot, BLOCK), lambda k: (0, k))
    peer = pl.BlockSpec((groups, BLOCK // LANES, LANES), lambda k: (0, k, 0))
    square = pl.BlockSpec((rows, BLOCK), lambda k: (0, k))
    grid = (steps,)
    far = functools.partial(pltpu.with_memory_space_constraint, memory_space=pltpu.HBM)
    student_patches, teacher_patches, mask_order = far(student_patches[0]), far(teacher_patches[0]), far(mask_order)
    student_protos, teacher_protos = far(student_protos), far(teacher_protos)
    dot = 2 * rows * protos * bot
    column = pltpu.VMEM((rows, 1), F32)

    sent, late, picked = call(
        pick_kernel,
        [((SLOT + EARLY, bot), BF16), ((2, 2 * LATE, LANES), BF16), pltpu.HBM((SLOT, bot), BF16)],
        teacher_patches,
        student_patches,
        mask_order,
        counts,
        in_specs=[VMEM, VMEM, VMEM, SMEM],
        moved=4 * patches * bot,
    )
    gathered = lax.all_gather(sent, "proto", axis=0, tiled=False)
    share, teacher_rows, places = call(
        column_kernel,
        [((groups, protos // LANES, LANES), F32), ((rows, bot), BF16), pltpu.HBM((4, width, LANES), F32)],
        gathered,
        index,
        teacher_protos,
        grid=grid,
        in_specs=[VMEM, SMEM, wide],
        out_specs=[peer, VMEM, VMEM],
        flops=dot,
        moved=2 * bot * protos,
    )
    shares = over(share, "dp")
    matrix, high, share = call(
        row_kernel,
        [((rows, protos), BF16), ((steps, rows, 1), F32), ((width // 2, 2, 2 * LATE + 16, LANES), BF16)],
        shares,
        teacher_rows,
        teacher_protos,
        late,
        grid=grid,
        in_specs=[peer, VMEM, wide, VMEM],
        out_specs=[square, VMEM, VMEM],
        scratch=[pltpu.VMEM((steps, rows, 1), F32)],
        flops=dot,
        moved=2 * bot * protos + 2 * rows * protos,
    )
    swap = [(p, p ^ 1) for p in range(width)]
    shares = over(share.reshape((width,) + share.shape[2:]), "proto")
    share, scale = call(
        first_column_kernel,
        [pltpu.HBM((groups, protos // LANES, LANES), BF16), pltpu.HBM((steps, rows, 1), F32)],
        shares,
        high,
        matrix,
        grid=grid,
        in_specs=[VMEM, VMEM, square],
        out_specs=[peer, VMEM],
        moved=2 * rows * protos,
    )
    late, share = lax.optimization_barrier((shares, share))
    late_came = lax.ppermute(late, "proto", swap)
    packed = ((width // 2, SLOT, bot), BF16)
    student_own, student_other = call(
        student_kernel,
        [pltpu.HBM(*packed), pltpu.HBM(*packed)],
        far(gathered),
        far(late),
        far(late_came),
        index,
        far(places),
        student_protos,
        grid=grid,
        in_specs=[VMEM, VMEM, VMEM, SMEM, VMEM, wide],
        scratch=[pltpu.VMEM((rows, bot), BF16), pltpu.VMEM((rows, bot), F32), column, column],
        flops=2 * dot,
        moved=2 * bot * protos,
    )
    student_came = lax.ppermute(student_other, "proto", swap)
    shares, student_came = lax.optimization_barrier((over(share, "dp"), student_came))
    share = call(
        later_row_kernel,
        [((width, depth, LANES), F32)],
        shares,
        scale,
        matrix,
        grid=grid,
        in_specs=[peer, VMEM, square],
        scratch=[column],
        moved=2 * rows * protos,
    )[0]
    shares = over(share, "proto")
    share, scale = call(
        later_column_kernel,
        [((groups, protos // LANES, LANES), BF16), ((steps, rows, 1), F32)],
        shares,
        scale,
        matrix,
        grid=grid,
        in_specs=[VMEM, VMEM, square],
        out_specs=[peer, VMEM],
        moved=2 * rows * protos,
    )
    shares = over(share, "dp")
    own, other = call(
        target_kernel,
        [packed, packed],
        shares,
        scale,
        matrix,
        student_protos,
        far(places),
        grid=grid,
        in_specs=[peer, VMEM, square, wide, VMEM],
        scratch=[pltpu.VMEM((rows, bot), F32), column],
        flops=dot,
        moved=2 * rows * protos,
    )
    came = lax.ppermute(other, "proto", swap)
    sent = call(
        merge_kernel, [((width // 2, 2 * SLOT, bot), BF16)], own, came, student_own, student_came
    )[0]
    same_core = [list(range(core, width, 2)) for core in range(2)]
    back = over(sent, "proto", axis_index_groups=same_core)
    student_grad, image_loss = call(
        finish_kernel,
        [((patches, bot), BF16), ((1, 1), F32)],
        back,
        picked,
        mask_order,
        counts,
        in_specs=[VMEM, VMEM, VMEM, SMEM],
        moved=2 * patches * bot,
    )
    return (student_grad[None], image_loss)


def solution(mesh):
    placed = (
        P(("dp", "proto"), None, None),
        P(("dp", "proto"), None, None),
        P(("dp", "proto"), None),
        P("dp", "proto"),
        P(None, "proto"),
        P(None, "proto"),
    )
    return jax.shard_map(
        body,
        mesh=mesh,
        in_specs=placed,
        out_specs=(P(("dp", "proto"), None, None), P("dp", "proto")),
        check_vma=False,
    )
```

```python
import functools

import jax
import jax.numpy as jnp
from jax import lax
from jax.experimental import pallas as pl
from jax.experimental.pallas import tpu as pltpu
from jax.sharding import PartitionSpec as P

MASK_DEV = 24
MOST = 72
EARLY = 40
LATE = (MOST - EARLY) // 2
SLOT = 80
TEACH = 1.0 / 0.07
STUD = 1.0 / 0.1
F32 = jnp.float32
BF16 = jnp.bfloat16
LANES = 128
BLOCK = 2048
LIMIT = 20 << 20
VMEM = pl.BlockSpec(memory_space=pltpu.VMEM)
SMEM = pl.BlockSpec(memory_space=pltpu.SMEM)


def call(kernel, out_shape, *args, grid=None, in_specs=None, out_specs=None, scratch=(), flops=0, moved=0):
    out_shape = [jax.ShapeDtypeStruct(*o) if isinstance(o, tuple) else o for o in out_shape]
    extra = {} if grid is None else {"grid": grid}
    return pl.pallas_call(
        kernel,
        out_shape=out_shape,
        in_specs=[VMEM] * len(args) if in_specs is None else in_specs,
        out_specs=[VMEM] * len(out_shape) if out_specs is None else out_specs,
        scratch_shapes=list(scratch),
        compiler_params=pltpu.CompilerParams(vmem_limit_bytes=LIMIT),
        cost_estimate=pl.CostEstimate(flops=flops, bytes_accessed=moved, transcendentals=0),
        **extra,
    )(*args)


def iota(shape, dim):
    return lax.broadcasted_iota(jnp.int32, shape, dim)


def eye():
    return iota((LANES, LANES), 0) == iota((LANES, LANES), 1)


def to_lanes(column):
    parts = []
    for b in range(column.shape[0] // LANES):
        part = jnp.broadcast_to(column[b * LANES : (b + 1) * LANES], (LANES, LANES))
        parts.append(jnp.sum(jnp.where(eye(), part, 0.0), axis=0, keepdims=True))
    return jnp.concatenate(parts, axis=0)


def to_column(lanes):
    parts = []
    for b in range(lanes.shape[0]):
        part = jnp.broadcast_to(lanes[b : b + 1], (LANES, LANES))
        parts.append(jnp.sum(jnp.where(eye(), part, 0.0), axis=1, keepdims=True))
    return jnp.concatenate(parts, axis=0)


def to_lines(row):
    return jnp.concatenate([row[:, b * LANES : (b + 1) * LANES] for b in range(row.shape[1] // LANES)], axis=0)


def to_row(lines):
    return jnp.concatenate([lines[b : b + 1] for b in range(lines.shape[0])], axis=1)


def merged(shares):
    top = jnp.max(shares, axis=0)
    return top + jnp.log(jnp.sum(jnp.exp(shares - top[None]), axis=0))


def pick_kernel(teacher_ref, student_ref, order_ref, count_ref, sent_ref, late_ref, picked_ref):
    patches, width = teacher_ref.shape
    order = jnp.broadcast_to(order_ref[:, :LANES], (patches, LANES))
    chosen = (iota((patches, LANES), 0) == order).astype(BF16)
    dims = (((0,), (0,)), ((), ()))
    teacher = lax.dot_general(chosen, teacher_ref[...], dims, preferred_element_type=F32)
    student = lax.dot_general(chosen, student_ref[...], dims, preferred_element_type=F32)
    count = jnp.full((SLOT - MOST, width), count_ref[0, 0], jnp.int32).astype(F32)
    sent_ref[...] = jnp.concatenate([teacher[:MOST], count, student[:EARLY]], axis=0).astype(BF16)
    for half in range(2):
        late = student[EARLY + half * LATE : EARLY + (half + 1) * LATE]
        late_ref[half] = jnp.concatenate([late[:, :LANES], late[:, LANES:]], axis=0).astype(BF16)
    picked_ref[...] = student[:SLOT].astype(BF16)


def compact(gathered, starts, counts, rows, first, length, shift):
    images, slots, width = gathered.shape
    total = images * slots
    lane, image = iota((images, total), 1), iota((images, total), 0)
    within = lane - image * slots - first
    member = jnp.logical_and(within >= 0, within < length)
    place = (within + shift).astype(F32)
    used = jnp.logical_and(member, place < counts[:, :1])
    row = jnp.sum(jnp.where(used, starts[:, :1] + place + 1.0, 0.0), axis=0, keepdims=True) - 1.0
    chosen = (iota((rows, total), 0).astype(F32) == row).astype(BF16)
    return jnp.dot(chosen, gathered.reshape(total, width), preferred_element_type=F32)


def spread(starts, counts, slots, rows):
    images = starts.shape[0]
    shape = (images, slots, rows)
    within = iota(shape, 1)
    row = (iota(shape, 2) - within).astype(F32) - starts[:, :1].reshape(images, 1, 1)
    used = jnp.logical_and(row == 0.0, within.astype(F32) < counts[:, :1].reshape(images, 1, 1))
    return used.astype(F32).astype(BF16).reshape(images * slots, rows)


def column_kernel(gathered_ref, index_ref, protos_ref, share_ref, rows_ref, places_ref):
    images = gathered_ref.shape[0]
    rows = rows_ref.shape[0]

    @pl.when(pl.program_id(0) == 0)
    def _():
        counts = gathered_ref[:, MOST:MOST + 8, :LANES].astype(F32)[:, 0]
        before = (iota((images, images), 1) < iota((images, images), 0)).astype(BF16)
        starts = jnp.dot(before, counts.astype(BF16), preferred_element_type=F32)
        half, core = images // 2, index_ref[0, 0] % 2
        place = iota((images, images), 0)
        image = jnp.where(place < half, 2 * place + core, 2 * (place - half) + 1 - core)
        other = iota((images, images), 1)
        places_ref[0] = jnp.dot((other < image).astype(BF16), counts.astype(BF16), preferred_element_type=F32)
        places_ref[1] = jnp.dot((other == image).astype(BF16), counts.astype(BF16), preferred_element_type=F32)
        places_ref[2] = starts
        places_ref[3] = counts
        rows_ref[...] = compact(gathered_ref[:, :SLOT], starts, counts, rows, 0, MOST, 0).astype(BF16)

    logits = jnp.dot(rows_ref[...], protos_ref[...], preferred_element_type=F32) * TEACH
    high = jnp.max(logits, axis=0, keepdims=True)
    total = jnp.sum(jnp.exp(logits - high), axis=0, keepdims=True)
    share_ref[...] = jnp.broadcast_to(to_lines(high + jnp.log(total))[None], share_ref.shape)


def split(values, parts):
    out = []
    for _ in range(parts):
        part = values.astype(BF16)
        out.append(part)
        values = values - part.astype(F32)
    return out


def fill_share(share_ref, lines):
    blank = jnp.zeros((share_ref.shape[1] - lines.shape[0], LANES), F32)
    share_ref[...] = jnp.broadcast_to(jnp.concatenate([lines, blank], axis=0)[None], share_ref.shape)


def row_kernel(shares_ref, rows_ref, protos_ref, late_ref, matrix_ref, high_ref, share_ref, sums):
    step = pl.program_id(0)
    column = to_row(merged(shares_ref[...]))
    logits = jnp.dot(rows_ref[...], protos_ref[...], preferred_element_type=F32) * TEACH
    shifted = logits - column
    high = jnp.max(shifted, axis=1, keepdims=True)
    exact = jnp.exp(shifted - high)
    matrix_ref[...] = exact.astype(BF16)
    high_ref[step] = high
    sums[step] = jnp.sum(exact, axis=1, keepdims=True)

    @pl.when(step == pl.num_programs(0) - 1)
    def _():
        highs = high_ref[...]
        top = jnp.max(highs, axis=0)
        total = jnp.sum(jnp.exp(highs - top[None]) * sums[...], axis=0)
        own = jnp.concatenate([part.astype(F32) for part in split(to_lanes(top + jnp.log(total)), 3)], axis=0)
        blank = jnp.zeros((share_ref.shape[2] - 2 * LATE - own.shape[0], LANES), F32)
        numbers = jnp.concatenate([own, blank], axis=0).astype(BF16)
        for half in range(2):
            chunk = jnp.concatenate([late_ref[half], numbers], axis=0)
            share_ref[:, half] = jnp.broadcast_to(chunk[None], (share_ref.shape[0],) + chunk.shape)


def column_sums(matrix_ref, scale, share_ref):
    sums = jnp.sum(matrix_ref[...].astype(F32) * scale, axis=0, keepdims=True)
    share_ref[...] = jnp.broadcast_to(to_lines(sums)[None], share_ref.shape).astype(share_ref.dtype)


def first_column_kernel(shares_ref, high_ref, matrix_ref, share_ref, scale_ref):
    step = pl.program_id(0)

    @pl.when(step == 0)
    def _():
        lines = scale_ref.shape[1] // LANES
        numbers = shares_ref[:, 2 * LATE :].astype(F32)
        row_lse = merged(sum(numbers[:, k * lines : (k + 1) * lines] for k in range(3)))
        scale_ref[...] = jnp.exp(high_ref[...] - to_column(row_lse)[None])

    column_sums(matrix_ref, scale_ref[step], share_ref)


def later_column_kernel(shares_ref, scale_in_ref, matrix_ref, share_ref, scale_ref):
    step = pl.program_id(0)

    @pl.when(step == 0)
    def _():
        lines = scale_ref.shape[1] // LANES
        total = to_column(jnp.sum(shares_ref[...][:, :lines], axis=0))
        scale_ref[...] = scale_in_ref[...] / total[None]

    column_sums(matrix_ref, scale_ref[step], share_ref)


def later_row_kernel(shares_ref, scale_ref, matrix_ref, share_ref, sums):
    step = pl.program_id(0)
    inverse = to_row(1.0 / jnp.sum(shares_ref[...].astype(F32), axis=0))
    part = scale_ref[step] * jnp.sum(matrix_ref[...].astype(F32) * inverse, axis=1, keepdims=True)

    @pl.when(step == 0)
    def _():
        sums[...] = part

    @pl.when(step > 0)
    def _():
        sums[...] += part

    @pl.when(step == pl.num_programs(0) - 1)
    def _():
        fill_share(share_ref, to_lanes(sums[...]))


def pack(sums, numbers, parts, starts, counts):
    rows, width = sums.shape
    images = starts.shape[0]
    wide = jnp.broadcast_to(numbers, (rows, LANES))
    sent = jnp.concatenate([sums.astype(BF16)] + split(wide, parts), axis=1)
    chosen = spread(starts, counts, SLOT, rows)
    packed = jnp.dot(chosen, sent, preferred_element_type=F32).reshape(images, SLOT, width + parts * LANES)
    same = iota((1, SLOT, LANES), 1) == iota((1, SLOT, LANES), 2)
    tail = []
    for k in range(parts):
        part = packed[:, :, width + k * LANES : width + (k + 1) * LANES]
        tail.append(jnp.sum(jnp.where(same, part, 0.0), axis=1, keepdims=True))
    return packed[:, :MOST, :width].astype(BF16), join(tail, width)


def join(tail, width):
    images = tail[0].shape[0]
    filler = jnp.zeros((images, 1, width - LANES), F32)
    rows = [jnp.concatenate([part.astype(F32), filler], axis=2) for part in tail]
    rows.append(jnp.zeros((images, SLOT - MOST - len(tail), width), F32))
    return jnp.concatenate(rows, axis=1).astype(BF16)


def numbers_of(chunk, parts):
    tail = chunk[:, MOST:SLOT, :LANES].astype(F32)
    return sum(tail[:, k] for k in range(parts))


def put(own_ref, other_ref, rows, tail):
    half = own_ref.shape[0]
    own_ref[:, :MOST], own_ref[:, MOST:] = rows[:half], tail[:half]
    other_ref[:, :MOST], other_ref[:, MOST:] = rows[half:], tail[half:]


def slots_of(lanes):
    images = lanes.shape[0]
    same = iota((1, MOST, LANES), 1) == iota((1, MOST, LANES), 2)
    return jnp.sum(jnp.where(same, lanes.reshape(images, 1, LANES), 0.0), axis=2, keepdims=True)


def target_kernel(shares_ref, scale_ref, matrix_ref, protos_ref, places_ref, own_ref, other_ref, sums, total):
    step = pl.program_id(0)
    scale = scale_ref[step]
    inverse = to_row(1.0 / jnp.sum(shares_ref[...].astype(F32), axis=0))
    weights = matrix_ref[...].astype(F32) * inverse
    narrow = weights.astype(BF16)
    part = scale * lax.dot_general(narrow, protos_ref[...], (((1,), (1,)), ((), ())), preferred_element_type=F32)
    mass = scale * jnp.sum(narrow.astype(F32), axis=1, keepdims=True)

    @pl.when(step == 0)
    def _():
        sums[...] = part
        total[...] = mass

    @pl.when(step > 0)
    def _():
        sums[...] += part
        total[...] += mass

    @pl.when(step == pl.num_programs(0) - 1)
    def _():
        put(own_ref, other_ref, *pack(sums[...], total[...], 2, places_ref[0], places_ref[1]))


def merge_kernel(own_ref, came_ref, student_own_ref, student_came_ref, out_ref):
    width = own_ref.shape[2]
    out_ref[:, :MOST] = (own_ref[:, :MOST].astype(F32) + came_ref[:, :MOST].astype(F32)).astype(BF16)
    total = numbers_of(own_ref, 2) + numbers_of(came_ref, 2)
    out_ref[:, MOST:SLOT] = join([part[:, None] for part in split(total, 2)], width)
    own, came = numbers_of(student_own_ref, 3), numbers_of(student_came_ref, 3)
    high = jnp.maximum(own, came)
    joint = high + jnp.log(jnp.exp(own - high) + jnp.exp(came - high))
    mean = student_own_ref[:, :MOST].astype(F32) * slots_of(jnp.exp(own - joint))
    mean = mean + student_came_ref[:, :MOST].astype(F32) * slots_of(jnp.exp(came - joint))
    out_ref[:, SLOT : SLOT + MOST] = mean.astype(BF16)
    out_ref[:, SLOT + MOST :] = join([part[:, None] for part in split(joint, 3)], width)


def student_kernel(
    gathered_ref, late_ref, came_ref, index_ref, places_ref, protos_ref, own_ref, other_ref, rows_ref, sums, top, total
):
    step = pl.program_id(0)
    rows = rows_ref.shape[0]

    @pl.when(step == 0)
    def _():
        starts, counts, core = places_ref[2], places_ref[3], index_ref[0, 0] % 2
        found = compact(gathered_ref[:, SLOT:], starts, counts, rows, 0, EARLY, 0)
        for ref, half in ((late_ref, core), (came_ref, 1 - core)):
            late = jnp.concatenate([ref[:, :LATE], ref[:, LATE : 2 * LATE]], axis=2)
            found += compact(late, starts, counts, rows, 0, LATE, EARLY + half * LATE)
        rows_ref[...] = found.astype(BF16)
        top[...] = jnp.full(top.shape, -1e30, F32)
        total[...] = jnp.zeros(total.shape, F32)
        sums[...] = jnp.zeros(sums.shape, F32)

    protos = protos_ref[...]
    logits = jnp.dot(rows_ref[...], protos, preferred_element_type=F32) * STUD
    before = top[...]
    high = jnp.maximum(before, jnp.max(logits, axis=1, keepdims=True))
    shrink = jnp.exp(before - high)
    exact = jnp.exp(logits - high)
    total[...] = total[...] * shrink + jnp.sum(exact, axis=1, keepdims=True)
    part = lax.dot_general(exact.astype(BF16), protos, (((1,), (1,)), ((), ())), preferred_element_type=F32)
    sums[...] = sums[...] * shrink + part
    top[...] = high

    @pl.when(step == pl.num_programs(0) - 1)
    def _():
        mean, own_lse = sums[...] / total[...], top[...] + jnp.log(total[...])
        put(own_ref, other_ref, *pack(mean, own_lse, 3, places_ref[0], places_ref[1]))


def blend(chunk, lse):
    joint = merged(lse)
    weights = slots_of(jnp.exp(lse - joint[None]))
    return jnp.sum(chunk * weights, axis=0), joint


def finish_kernel(back_ref, picked_ref, order_ref, count_ref, grad_ref, loss_ref):
    patches, width = grad_ref.shape
    target = jnp.sum(back_ref[:, :SLOT].astype(F32), axis=0)
    mass = to_column((target[MOST : MOST + 1] + target[MOST + 1 : MOST + 2])[:, :LANES])[:MOST]
    tail = back_ref[:, SLOT + MOST : 2 * SLOT, :LANES].astype(F32)
    soft, lse_lanes = blend(back_ref[:, SLOT : SLOT + MOST].astype(F32), sum(tail[:, k] for k in range(3)))
    used = iota((MOST, 1), 0) < count_ref[0, 0]
    mean = target[:MOST] / jnp.where(used, mass, 1.0)
    own_lse = to_column(lse_lanes.reshape(1, LANES))[:MOST]
    cross = own_lse - STUD * jnp.sum(picked_ref[:MOST].astype(F32) * mean, axis=1, keepdims=True)
    cross = jnp.sum(jnp.where(used, cross, 0.0), axis=0, keepdims=True)
    loss_ref[...] = cross / jnp.full((1, 1), count_ref[0, 0], jnp.int32).astype(F32)
    rows = jnp.where(used, STUD * (soft - mean), 0.0)
    rows = jnp.concatenate([rows, jnp.zeros((LANES - MOST, width), F32)], axis=0).astype(BF16)
    order = jnp.broadcast_to(order_ref[:, :LANES], (patches, LANES))
    chosen = (iota((patches, LANES), 0) == order).astype(BF16)
    grad_ref[...] = jnp.dot(chosen, rows, preferred_element_type=F32).astype(BF16)


def body(student_patches, teacher_patches, mask_order, counts, student_protos, teacher_protos):
    width = lax.axis_size("proto")
    groups = lax.axis_size("dp")
    rows = MASK_DEV * width
    lines = rows // LANES
    patches, bot = student_patches.shape[1:]
    protos = student_protos.shape[1]
    steps = protos // BLOCK
    depth = 8
    index = lax.axis_index("proto").astype(jnp.int32).reshape(1, 1)
    over = functools.partial(lax.all_to_all, split_axis=0, concat_axis=0, tiled=True)
    wide = pl.BlockSpec((bot, BLOCK), lambda k: (0, k))
    peer = pl.BlockSpec((groups, BLOCK // LANES, LANES), lambda k: (0, k, 0))
    square = pl.BlockSpec((rows, BLOCK), lambda k: (0, k))
    grid = (steps,)
    far = functools.partial(pltpu.with_memory_space_constraint, memory_space=pltpu.HBM)
    student_patches, teacher_patches, mask_order = far(student_patches[0]), far(teacher_patches[0]), far(mask_order)
    student_protos, teacher_protos = far(student_protos), far(teacher_protos)
    dot = 2 * rows * protos * bot
    column = pltpu.VMEM((rows, 1), F32)

    sent, late, picked = call(
        pick_kernel,
        [((SLOT + EARLY, bot), BF16), ((2, 2 * LATE, LANES), BF16), pltpu.HBM((SLOT, bot), BF16)],
        teacher_patches,
        student_patches,
        mask_order,
        counts,
        in_specs=[VMEM, VMEM, VMEM, SMEM],
        moved=4 * patches * bot,
    )
    gathered = lax.all_gather(sent, "proto", axis=0, tiled=False)
    share, teacher_rows, places = call(
        column_kernel,
        [((groups, protos // LANES, LANES), F32), ((rows, bot), BF16), pltpu.HBM((4, width, LANES), F32)],
        gathered,
        index,
        teacher_protos,
        grid=grid,
        in_specs=[VMEM, SMEM, wide],
        out_specs=[peer, VMEM, VMEM],
        flops=dot,
        moved=2 * bot * protos,
    )
    shares = over(share, "dp")
    matrix, high, share = call(
        row_kernel,
        [((rows, protos), BF16), ((steps, rows, 1), F32), ((width // 2, 2, 2 * LATE + 16, LANES), BF16)],
        shares,
        teacher_rows,
        teacher_protos,
        late,
        grid=grid,
        in_specs=[peer, VMEM, wide, VMEM],
        out_specs=[square, VMEM, VMEM],
        scratch=[pltpu.VMEM((steps, rows, 1), F32)],
        flops=dot,
        moved=2 * bot * protos + 2 * rows * protos,
    )
    swap = [(p, p ^ 1) for p in range(width)]
    shares = over(share.reshape((width,) + share.shape[2:]), "proto")
    late = shares
    share, scale = call(
        first_column_kernel,
        [((groups, protos // LANES, LANES), BF16), ((steps, rows, 1), F32)],
        shares,
        high,
        matrix,
        grid=grid,
        in_specs=[VMEM, VMEM, square],
        out_specs=[peer, VMEM],
        moved=2 * rows * protos,
    )
    shares = over(share, "dp")
    share = call(
        later_row_kernel,
        [((width, depth, LANES), F32)],
        shares,
        scale,
        matrix,
        grid=grid,
        in_specs=[peer, VMEM, square],
        scratch=[column],
        moved=2 * rows * protos,
    )[0]
    shares = over(share, "proto")
    share, scale = call(
        later_column_kernel,
        [pltpu.HBM((groups, protos // LANES, LANES), BF16), pltpu.HBM((steps, rows, 1), F32)],
        shares,
        scale,
        matrix,
        grid=grid,
        in_specs=[VMEM, VMEM, square],
        out_specs=[peer, VMEM],
        moved=2 * rows * protos,
    )
    late_came = lax.ppermute(late, "proto", swap)
    packed = ((width // 2, SLOT, bot), BF16)
    student_own, student_other = call(
        student_kernel,
        [pltpu.HBM(*packed), pltpu.HBM(*packed)],
        far(gathered),
        far(late),
        far(late_came),
        index,
        far(places),
        student_protos,
        grid=grid,
        in_specs=[VMEM, VMEM, VMEM, SMEM, VMEM, wide],
        scratch=[pltpu.VMEM((rows, bot), BF16), pltpu.VMEM((rows, bot), F32), column, column],
        flops=2 * dot,
        moved=2 * bot * protos,
    )
    student_came = lax.ppermute(student_other, "proto", swap)
    shares = over(share, "dp")
    own, other = call(
        target_kernel,
        [packed, packed],
        shares,
        scale,
        matrix,
        student_protos,
        far(places),
        grid=grid,
        in_specs=[peer, VMEM, square, wide, VMEM],
        scratch=[pltpu.VMEM((rows, bot), F32), column],
        flops=dot,
        moved=2 * rows * protos,
    )
    came = lax.ppermute(other, "proto", swap)
    sent = call(
        merge_kernel, [((width // 2, 2 * SLOT, bot), BF16)], own, came, student_own, student_came
    )[0]
    same_core = [list(range(core, width, 2)) for core in range(2)]
    back = over(sent, "proto", axis_index_groups=same_core)
    student_grad, image_loss = call(
        finish_kernel,
        [((patches, bot), BF16), ((1, 1), F32)],
        back,
        picked,
        mask_order,
        counts,
        in_specs=[VMEM, VMEM, VMEM, SMEM],
        moved=2 * patches * bot,
    )
    return (student_grad[None], image_loss)


def solution(mesh):
    placed = (
        P(("dp", "proto"), None, None),
        P(("dp", "proto"), None, None),
        P(("dp", "proto"), None),
        P("dp", "proto"),
        P(None, "proto"),
        P(None, "proto"),
    )
    return jax.shard_map(
        body,
        mesh=mesh,
        in_specs=placed,
        out_specs=(P(("dp", "proto"), None, None), P("dp", "proto")),
        check_vma=False,
    )
```

```python
import functools

import jax
import jax.numpy as jnp
from jax import lax
from jax.experimental import pallas as pl
from jax.experimental.pallas import tpu as pltpu
from jax.sharding import PartitionSpec as P

MASK_DEV = 24
MOST = 72
EARLY = 40
LATE = (MOST - EARLY) // 2
SLOT = 80
TEACH = 1.0 / 0.07
STUD = 1.0 / 0.1
F32 = jnp.float32
BF16 = jnp.bfloat16
LANES = 128
BLOCK = 2048
PIECE = 1024
LIMIT = 24 << 20
VMEM = pl.BlockSpec(memory_space=pltpu.VMEM)
SMEM = pl.BlockSpec(memory_space=pltpu.SMEM)


HBM = pl.BlockSpec(memory_space=pl.ANY)


def call(kernel, out_shape, *args, in_specs=None, scratch=(), flops=0, moved=0):
    out_shape = [jax.ShapeDtypeStruct(*o) if isinstance(o, tuple) else o for o in out_shape]
    return pl.pallas_call(
        kernel,
        out_shape=out_shape,
        in_specs=[VMEM] * len(args) if in_specs is None else in_specs,
        out_specs=[VMEM] * len(out_shape),
        scratch_shapes=list(scratch),
        compiler_params=pltpu.CompilerParams(vmem_limit_bytes=LIMIT),
        cost_estimate=pl.CostEstimate(flops=flops, bytes_accessed=moved, transcendentals=0),
    )(*args)


def fetch(far_ref, near_ref, sems):
    copies = []
    for k in range(near_ref.shape[1] // PIECE):
        piece = slice(k * PIECE, (k + 1) * PIECE)
        copies.append(pltpu.make_async_copy(far_ref.at[:, piece], near_ref.at[:, piece], sems.at[k]))
        copies[-1].start()

    def block(b):
        for copy in copies[b * BLOCK // PIECE : (b + 1) * BLOCK // PIECE]:
            copy.wait()
        return near_ref[:, b * BLOCK : (b + 1) * BLOCK]

    return block, range(near_ref.shape[1] // BLOCK)


def columns(b):
    return slice(b * BLOCK, (b + 1) * BLOCK)


def lines_of(b):
    return slice(b * BLOCK // LANES, (b + 1) * BLOCK // LANES)


def iota(shape, dim):
    return lax.broadcasted_iota(jnp.int32, shape, dim)


def eye():
    return iota((LANES, LANES), 0) == iota((LANES, LANES), 1)


def to_lanes(column):
    parts = []
    for b in range(column.shape[0] // LANES):
        part = jnp.broadcast_to(column[b * LANES : (b + 1) * LANES], (LANES, LANES))
        parts.append(jnp.sum(jnp.where(eye(), part, 0.0), axis=0, keepdims=True))
    return jnp.concatenate(parts, axis=0)


def to_column(lanes):
    parts = []
    for b in range(lanes.shape[0]):
        part = jnp.broadcast_to(lanes[b : b + 1], (LANES, LANES))
        parts.append(jnp.sum(jnp.where(eye(), part, 0.0), axis=1, keepdims=True))
    return jnp.concatenate(parts, axis=0)


def to_lines(row):
    return jnp.concatenate([row[:, b * LANES : (b + 1) * LANES] for b in range(row.shape[1] // LANES)], axis=0)


def to_row(lines):
    return jnp.concatenate([lines[b : b + 1] for b in range(lines.shape[0])], axis=1)


def merged(shares):
    top = jnp.max(shares, axis=0)
    return top + jnp.log(jnp.sum(jnp.exp(shares - top[None]), axis=0))


def pick_kernel(teacher_ref, student_ref, order_ref, count_ref, sent_ref, late_ref, picked_ref):
    patches, width = teacher_ref.shape
    order = jnp.broadcast_to(order_ref[:, :LANES], (patches, LANES))
    chosen = (iota((patches, LANES), 0) == order).astype(BF16)
    dims = (((0,), (0,)), ((), ()))
    teacher = lax.dot_general(chosen, teacher_ref[...], dims, preferred_element_type=F32)
    student = lax.dot_general(chosen, student_ref[...], dims, preferred_element_type=F32)
    count = jnp.full((SLOT - MOST, width), count_ref[0, 0], jnp.int32).astype(F32)
    sent_ref[...] = jnp.concatenate([teacher[:MOST], count, student[:EARLY]], axis=0).astype(BF16)
    for half in range(2):
        late = student[EARLY + half * LATE : EARLY + (half + 1) * LATE]
        late_ref[half] = jnp.concatenate([late[:, :LANES], late[:, LANES:]], axis=0).astype(BF16)
    picked_ref[...] = student[:SLOT].astype(BF16)


def compact(gathered, starts, counts, rows, first, length, shift):
    images, slots, width = gathered.shape
    total = images * slots
    lane, image = iota((images, total), 1), iota((images, total), 0)
    within = lane - image * slots - first
    member = jnp.logical_and(within >= 0, within < length)
    place = (within + shift).astype(F32)
    used = jnp.logical_and(member, place < counts[:, :1])
    row = jnp.sum(jnp.where(used, starts[:, :1] + place + 1.0, 0.0), axis=0, keepdims=True) - 1.0
    chosen = (iota((rows, total), 0).astype(F32) == row).astype(BF16)
    return jnp.dot(chosen, gathered.reshape(total, width), preferred_element_type=F32)


def spread(starts, counts, slots, rows):
    images = starts.shape[0]
    shape = (images, slots, rows)
    within = iota(shape, 1)
    row = (iota(shape, 2) - within).astype(F32) - starts[:, :1].reshape(images, 1, 1)
    used = jnp.logical_and(row == 0.0, within.astype(F32) < counts[:, :1].reshape(images, 1, 1))
    return used.astype(F32).astype(BF16).reshape(images * slots, rows)


def column_kernel(gathered_ref, index_ref, far_ref, share_ref, rows_ref, places_ref, near_ref, sems):
    block, blocks = fetch(far_ref, near_ref, sems)
    images = gathered_ref.shape[0]
    counts = gathered_ref[:, MOST:SLOT, :LANES].astype(F32)[:, 0]
    before = (iota((images, images), 1) < iota((images, images), 0)).astype(BF16)
    starts = jnp.dot(before, counts.astype(BF16), preferred_element_type=F32)
    half, core = images // 2, index_ref[0, 0] % 2
    place = iota((images, images), 0)
    image = jnp.where(place < half, 2 * place + core, 2 * (place - half) + 1 - core)
    other = iota((images, images), 1)
    places_ref[0] = jnp.dot((other < image).astype(BF16), counts.astype(BF16), preferred_element_type=F32)
    places_ref[1] = jnp.dot((other == image).astype(BF16), counts.astype(BF16), preferred_element_type=F32)
    places_ref[2] = starts
    places_ref[3] = counts
    rows = compact(gathered_ref[:, :SLOT], starts, counts, rows_ref.shape[0], 0, MOST, 0).astype(BF16)
    rows_ref[...] = rows
    for b in blocks:
        logits = jnp.dot(rows, block(b), preferred_element_type=F32) * TEACH
        high = jnp.max(logits, axis=0, keepdims=True)
        total = jnp.sum(jnp.exp(logits - high), axis=0, keepdims=True)
        lines = to_lines(high + jnp.log(total))
        share_ref[:, lines_of(b)] = jnp.broadcast_to(lines[None], (share_ref.shape[0],) + lines.shape)


def split(values, parts):
    out = []
    for _ in range(parts):
        part = values.astype(BF16)
        out.append(part)
        values = values - part.astype(F32)
    return out


def fill_share(share_ref, lines):
    blank = jnp.zeros((share_ref.shape[1] - lines.shape[0], LANES), F32)
    share_ref[...] = jnp.broadcast_to(jnp.concatenate([lines, blank], axis=0)[None], share_ref.shape)


def row_kernel(shares_ref, rows_ref, protos_ref, late_ref, matrix_ref, high_ref, share_ref):
    column = merged(shares_ref[...])
    rows = rows_ref[...]
    highs, sums = [], []
    for b in range(high_ref.shape[0]):
        logits = jnp.dot(rows, protos_ref[:, columns(b)], preferred_element_type=F32) * TEACH
        shifted = logits - to_row(column[lines_of(b)])
        high = jnp.max(shifted, axis=1, keepdims=True)
        exact = jnp.exp(shifted - high)
        matrix_ref[:, columns(b)] = exact.astype(BF16)
        high_ref[b] = high
        highs.append(high)
        sums.append(jnp.sum(exact, axis=1, keepdims=True))
    top = functools.reduce(jnp.maximum, highs)
    total = sum(jnp.exp(high - top) * part for high, part in zip(highs, sums))
    own = jnp.concatenate([part.astype(F32) for part in split(to_lanes(top + jnp.log(total)), 3)], axis=0)
    blank = jnp.zeros((share_ref.shape[2] - 2 * LATE - own.shape[0], LANES), F32)
    numbers = jnp.concatenate([own, blank], axis=0).astype(BF16)
    for half in range(2):
        chunk = jnp.concatenate([late_ref[half], numbers], axis=0)
        share_ref[:, half] = jnp.broadcast_to(chunk[None], (share_ref.shape[0],) + chunk.shape)


def column_sums(matrix_ref, scale, share_ref):
    for b in range(scale.shape[0]):
        sums = jnp.sum(matrix_ref[:, columns(b)].astype(F32) * scale[b], axis=0, keepdims=True)
        lines = to_lines(sums)
        shape = (share_ref.shape[0],) + lines.shape
        share_ref[:, lines_of(b)] = jnp.broadcast_to(lines[None], shape).astype(share_ref.dtype)


def first_column_kernel(shares_ref, high_ref, matrix_ref, share_ref, scale_ref):
    lines = scale_ref.shape[1] // LANES
    numbers = shares_ref[:, 2 * LATE :].astype(F32)
    row_lse = merged(sum(numbers[:, k * lines : (k + 1) * lines] for k in range(3)))
    scale = jnp.exp(high_ref[...] - to_column(row_lse)[None])
    scale_ref[...] = scale
    column_sums(matrix_ref, scale, share_ref)


def later_column_kernel(shares_ref, scale_in_ref, matrix_ref, share_ref, scale_ref):
    lines = scale_ref.shape[1] // LANES
    total = to_column(jnp.sum(shares_ref[...][:, :lines], axis=0))
    scale = scale_in_ref[...] / total[None]
    scale_ref[...] = scale
    column_sums(matrix_ref, scale, share_ref)


def inverse_of(shares_ref):
    return 1.0 / jnp.sum(shares_ref[...].astype(F32), axis=0)


def later_row_kernel(shares_ref, scale_ref, matrix_ref, share_ref):
    inverse = inverse_of(shares_ref)
    sums = 0.0
    for b in range(scale_ref.shape[0]):
        scaled = matrix_ref[:, columns(b)].astype(F32) * to_row(inverse[lines_of(b)])
        sums += scale_ref[b] * jnp.sum(scaled, axis=1, keepdims=True)
    fill_share(share_ref, to_lanes(sums))


def pack(sums, numbers, parts, starts, counts):
    rows, width = sums.shape
    images = starts.shape[0]
    chosen = spread(starts, counts, SLOT, rows)
    packed = jnp.dot(chosen, sums.astype(BF16), preferred_element_type=F32).astype(BF16)
    row = split(to_row(to_lanes(numbers)), parts)
    row = jnp.concatenate([part.astype(F32) for part in row] + [jnp.zeros((SLOT - MOST - parts, rows), F32)], axis=0)
    tail = lax.dot_general(row.astype(BF16), chosen, (((1,), (1,)), ((), ())), preferred_element_type=F32)
    tail = jnp.concatenate([tail, jnp.zeros((SLOT - MOST, LANES), F32)], axis=1)
    blank = jnp.zeros((SLOT - MOST, width - LANES), F32)
    tail = [jnp.concatenate([tail[:, j * SLOT : j * SLOT + LANES], blank], axis=1)[None] for j in range(images)]
    return packed.reshape(images, SLOT, width)[:, :MOST], jnp.concatenate(tail, axis=0).astype(BF16)


def join(tail, width):
    images = tail[0].shape[0]
    filler = jnp.zeros((images, 1, width - LANES), F32)
    rows = [jnp.concatenate([part.astype(F32), filler], axis=2) for part in tail]
    rows.append(jnp.zeros((images, SLOT - MOST - len(tail), width), F32))
    return jnp.concatenate(rows, axis=1).astype(BF16)


def numbers_of(chunk, parts):
    tail = chunk[:, MOST:SLOT, :LANES].astype(F32)
    return sum(tail[:, k] for k in range(parts))


def put(own_ref, other_ref, rows, tail):
    half = own_ref.shape[0]
    own_ref[:, :MOST], own_ref[:, MOST:] = rows[:half], tail[:half]
    other_ref[:, :MOST], other_ref[:, MOST:] = rows[half:], tail[half:]


def slots_of(lanes):
    images = lanes.shape[0]
    same = iota((1, MOST, LANES), 1) == iota((1, MOST, LANES), 2)
    return jnp.sum(jnp.where(same, lanes.reshape(images, 1, LANES), 0.0), axis=2, keepdims=True)


def target_kernel(shares_ref, scale_ref, matrix_ref, protos_ref, places_ref, own_ref, other_ref):
    inverse = inverse_of(shares_ref)
    sums, total = 0.0, 0.0
    for b in range(scale_ref.shape[0]):
        weights = (matrix_ref[:, columns(b)].astype(F32) * to_row(inverse[lines_of(b)])).astype(BF16)
        part = lax.dot_general(weights, protos_ref[:, columns(b)], (((1,), (1,)), ((), ())), preferred_element_type=F32)
        sums += scale_ref[b] * part
        total += scale_ref[b] * jnp.sum(weights.astype(F32), axis=1, keepdims=True)
    put(own_ref, other_ref, *pack(sums, total, 2, places_ref[0], places_ref[1]))


def merge_kernel(own_ref, came_ref, student_own_ref, student_came_ref, out_ref):
    width = own_ref.shape[2]
    out_ref[:, :MOST] = (own_ref[:, :MOST].astype(F32) + came_ref[:, :MOST].astype(F32)).astype(BF16)
    total = numbers_of(own_ref, 2) + numbers_of(came_ref, 2)
    out_ref[:, MOST:SLOT] = join([part[:, None] for part in split(total, 2)], width)
    own, came = numbers_of(student_own_ref, 3), numbers_of(student_came_ref, 3)
    high = jnp.maximum(own, came)
    joint = high + jnp.log(jnp.exp(own - high) + jnp.exp(came - high))
    mean = student_own_ref[:, :MOST].astype(F32) * slots_of(jnp.exp(own - joint))
    mean = mean + student_came_ref[:, :MOST].astype(F32) * slots_of(jnp.exp(came - joint))
    out_ref[:, SLOT : SLOT + MOST] = mean.astype(BF16)
    out_ref[:, SLOT + MOST :] = join([part[:, None] for part in split(joint, 3)], width)


def student_kernel(
    gathered_ref, late_ref, came_ref, index_ref, places_ref, far_ref, own_ref, other_ref, near_ref, sems
):
    block, blocks = fetch(far_ref, near_ref, sems)
    rows = places_ref.shape[1] * MASK_DEV
    starts, counts, core = places_ref[2], places_ref[3], index_ref[0, 0] % 2
    found = compact(gathered_ref[:, SLOT:], starts, counts, rows, 0, EARLY, 0)
    for ref, half in ((late_ref, core), (came_ref, 1 - core)):
        late = jnp.concatenate([ref[:, :LATE], ref[:, LATE : 2 * LATE]], axis=2)
        found += compact(late, starts, counts, rows, 0, LATE, EARLY + half * LATE)
    found = found.astype(BF16)
    top, total, sums = -1e30, 0.0, 0.0
    for b in blocks:
        protos = block(b)
        logits = jnp.dot(found, protos, preferred_element_type=F32) * STUD
        high = jnp.maximum(top, jnp.max(logits, axis=1, keepdims=True))
        shrink = jnp.exp(top - high)
        exact = jnp.exp(logits - high)
        total = total * shrink + jnp.sum(exact, axis=1, keepdims=True)
        part = lax.dot_general(exact.astype(BF16), protos, (((1,), (1,)), ((), ())), preferred_element_type=F32)
        sums = sums * shrink + part
        top = high
    put(own_ref, other_ref, *pack(sums / total, top + jnp.log(total), 3, places_ref[0], places_ref[1]))


def blend(chunk, lse):
    joint = merged(lse)
    weights = slots_of(jnp.exp(lse - joint[None]))
    return jnp.sum(chunk * weights, axis=0), joint


def finish_kernel(back_ref, picked_ref, order_ref, count_ref, grad_ref, loss_ref):
    patches, width = grad_ref.shape
    target = jnp.sum(back_ref[:, :SLOT].astype(F32), axis=0)
    mass = to_column((target[MOST : MOST + 1] + target[MOST + 1 : MOST + 2])[:, :LANES])[:MOST]
    tail = back_ref[:, SLOT + MOST : 2 * SLOT, :LANES].astype(F32)
    soft, lse_lanes = blend(back_ref[:, SLOT : SLOT + MOST].astype(F32), sum(tail[:, k] for k in range(3)))
    used = iota((MOST, 1), 0) < count_ref[0, 0]
    mean = target[:MOST] / jnp.where(used, mass, 1.0)
    own_lse = to_column(lse_lanes.reshape(1, LANES))[:MOST]
    cross = own_lse - STUD * jnp.sum(picked_ref[:MOST].astype(F32) * mean, axis=1, keepdims=True)
    cross = jnp.sum(jnp.where(used, cross, 0.0), axis=0, keepdims=True)
    loss_ref[...] = cross / jnp.full((1, 1), count_ref[0, 0], jnp.int32).astype(F32)
    rows = jnp.where(used, STUD * (soft - mean), 0.0)
    rows = jnp.concatenate([rows, jnp.zeros((LANES - MOST, width), F32)], axis=0).astype(BF16)
    order = jnp.broadcast_to(order_ref[:, :LANES], (patches, LANES))
    chosen = (iota((patches, LANES), 0) == order).astype(BF16)
    grad_ref[...] = jnp.dot(chosen, rows, preferred_element_type=F32).astype(BF16)


def body(student_patches, teacher_patches, mask_order, counts, student_protos, teacher_protos):
    width = lax.axis_size("proto")
    groups = lax.axis_size("dp")
    rows = MASK_DEV * width
    lines = rows // LANES
    patches, bot = student_patches.shape[1:]
    protos = student_protos.shape[1]
    steps = protos // BLOCK
    depth = 8
    index = lax.axis_index("proto").astype(jnp.int32).reshape(1, 1)
    over = functools.partial(lax.all_to_all, split_axis=0, concat_axis=0, tiled=True)
    near = ((bot, protos), BF16)
    sems = [pltpu.SemaphoreType.DMA((protos // PIECE,))]
    far = functools.partial(pltpu.with_memory_space_constraint, memory_space=pltpu.HBM)
    student_patches, teacher_patches, mask_order = far(student_patches[0]), far(teacher_patches[0]), far(mask_order)
    student_protos, teacher_protos = far(student_protos), far(teacher_protos)
    dot = 2 * rows * protos * bot

    sent, late, picked = call(
        pick_kernel,
        [((SLOT + EARLY, bot), BF16), ((2, 2 * LATE, LANES), BF16), pltpu.HBM((SLOT, bot), BF16)],
        teacher_patches,
        student_patches,
        mask_order,
        counts,
        in_specs=[VMEM, VMEM, VMEM, SMEM],
        moved=4 * patches * bot,
    )
    gathered = lax.all_gather(sent, "proto", axis=0, tiled=False)
    share, teacher_rows, places, near_teacher = call(
        column_kernel,
        [((groups, protos // LANES, LANES), F32), ((rows, bot), BF16), pltpu.HBM((4, width, LANES), F32), near],
        gathered,
        index,
        teacher_protos,
        in_specs=[VMEM, SMEM, HBM],
        scratch=sems,
        flops=dot,
        moved=2 * bot * protos,
    )
    shares = over(share, "dp")
    matrix, high, share = call(
        row_kernel,
        [((rows, protos), BF16), ((steps, rows, 1), F32), ((width // 2, 2, 2 * LATE + 16, LANES), BF16)],
        shares,
        teacher_rows,
        near_teacher,
        late,
        flops=dot,
        moved=2 * bot * protos + 2 * rows * protos,
    )
    swap = [(p, p ^ 1) for p in range(width)]
    shares = over(share.reshape((width,) + share.shape[2:]), "proto")
    late = shares
    share, scale = call(
        first_column_kernel,
        [((groups, protos // LANES, LANES), BF16), ((steps, rows, 1), F32)],
        shares,
        high,
        matrix,
        moved=2 * rows * protos,
    )
    shares = over(share, "dp")
    share = call(
        later_row_kernel,
        [((width, depth, LANES), F32)],
        shares,
        scale,
        matrix,
        moved=2 * rows * protos,
    )[0]
    shares = over(share, "proto")
    share, scale = call(
        later_column_kernel,
        [pltpu.HBM((groups, protos // LANES, LANES), BF16), pltpu.HBM((steps, rows, 1), F32)],
        shares,
        scale,
        matrix,
        moved=2 * rows * protos,
    )
    late_came = lax.ppermute(late, "proto", swap)
    packed = ((width // 2, SLOT, bot), BF16)
    student_own, student_other, near_student = call(
        student_kernel,
        [pltpu.HBM(*packed), pltpu.HBM(*packed), near],
        far(gathered),
        far(late),
        far(late_came),
        index,
        far(places),
        student_protos,
        in_specs=[VMEM, VMEM, VMEM, SMEM, VMEM, HBM],
        scratch=sems,
        flops=2 * dot,
        moved=2 * bot * protos,
    )
    student_came = lax.ppermute(student_other, "proto", swap)
    shares = over(share, "dp")
    own, other = call(
        target_kernel,
        [packed, packed],
        shares,
        scale,
        matrix,
        near_student,
        far(places),
        flops=dot,
        moved=2 * rows * protos,
    )
    came = lax.ppermute(other, "proto", swap)
    sent = call(
        merge_kernel, [((width // 2, 2 * SLOT, bot), BF16)], own, came, student_own, student_came
    )[0]
    same_core = [list(range(core, width, 2)) for core in range(2)]
    back = over(sent, "proto", axis_index_groups=same_core)
    student_grad, image_loss = call(
        finish_kernel,
        [((patches, bot), BF16), ((1, 1), F32)],
        back,
        picked,
        mask_order,
        counts,
        in_specs=[VMEM, VMEM, VMEM, SMEM],
        moved=2 * patches * bot,
    )
    return (student_grad[None], image_loss)


def solution(mesh):
    placed = (
        P(("dp", "proto"), None, None),
        P(("dp", "proto"), None, None),
        P(("dp", "proto"), None),
        P("dp", "proto"),
        P(None, "proto"),
        P(None, "proto"),
    )
    return jax.shard_map(
        body,
        mesh=mesh,
        in_specs=placed,
        out_specs=(P(("dp", "proto"), None, None), P("dp", "proto")),
        check_vma=False,
    )
```

```python
import functools

import jax
import jax.numpy as jnp
from jax import lax
from jax.experimental import pallas as pl
from jax.experimental.pallas import tpu as pltpu
from jax.sharding import PartitionSpec as P

MASK_DEV = 24
MOST = 72
EARLY = 40
LATE = (MOST - EARLY) // 2
SLOT = 80
TEACH = 1.0 / 0.07
STUD = 1.0 / 0.1
F32 = jnp.float32
BF16 = jnp.bfloat16
LANES = 128
BLOCK = 2048
PIECE = 1024
LIMIT = 24 << 20
VMEM = pl.BlockSpec(memory_space=pltpu.VMEM)
SMEM = pl.BlockSpec(memory_space=pltpu.SMEM)


HBM = pl.BlockSpec(memory_space=pl.ANY)


def call(kernel, out_shape, *args, in_specs=None, scratch=(), grid=None, flops=0, moved=0):
    out_shape = [jax.ShapeDtypeStruct(*o) if isinstance(o, tuple) else o for o in out_shape]
    extra = {} if grid is None else {"grid": grid}
    return pl.pallas_call(
        kernel,
        out_shape=out_shape,
        in_specs=[VMEM] * len(args) if in_specs is None else in_specs,
        out_specs=[VMEM] * len(out_shape),
        scratch_shapes=list(scratch),
        compiler_params=pltpu.CompilerParams(vmem_limit_bytes=LIMIT),
        cost_estimate=pl.CostEstimate(flops=flops, bytes_accessed=moved, transcendentals=0),
        **extra,
    )(*args)


def fetch(far_ref, near_ref, sems):
    copies = []
    for k in range(near_ref.shape[1] // PIECE):
        piece = slice(k * PIECE, (k + 1) * PIECE)
        copies.append(pltpu.make_async_copy(far_ref.at[:, piece], near_ref.at[:, piece], sems.at[k]))
        copies[-1].start()

    def block(b):
        for copy in copies[b * BLOCK // PIECE : (b + 1) * BLOCK // PIECE]:
            copy.wait()
        return near_ref[:, b * BLOCK : (b + 1) * BLOCK]

    return block, range(near_ref.shape[1] // BLOCK)


def columns(b):
    return slice(b * BLOCK, (b + 1) * BLOCK)


def lines_of(b):
    return slice(b * BLOCK // LANES, (b + 1) * BLOCK // LANES)


def iota(shape, dim):
    return lax.broadcasted_iota(jnp.int32, shape, dim)


def eye():
    return iota((LANES, LANES), 0) == iota((LANES, LANES), 1)


def to_lanes(column):
    parts = []
    for b in range(column.shape[0] // LANES):
        part = jnp.broadcast_to(column[b * LANES : (b + 1) * LANES], (LANES, LANES))
        parts.append(jnp.sum(jnp.where(eye(), part, 0.0), axis=0, keepdims=True))
    return jnp.concatenate(parts, axis=0)


def to_column(lanes):
    parts = []
    for b in range(lanes.shape[0]):
        part = jnp.broadcast_to(lanes[b : b + 1], (LANES, LANES))
        parts.append(jnp.sum(jnp.where(eye(), part, 0.0), axis=1, keepdims=True))
    return jnp.concatenate(parts, axis=0)


def to_lines(row):
    return jnp.concatenate([row[:, b * LANES : (b + 1) * LANES] for b in range(row.shape[1] // LANES)], axis=0)


def to_row(lines):
    return jnp.concatenate([lines[b : b + 1] for b in range(lines.shape[0])], axis=1)


def merged(shares):
    top = jnp.max(shares, axis=0)
    return top + jnp.log(jnp.sum(jnp.exp(shares - top[None]), axis=0))


def pick_kernel(teacher_ref, student_ref, order_ref, count_ref, sent_ref, late_ref, picked_ref):
    patches, width = teacher_ref.shape
    order = jnp.broadcast_to(order_ref[:, :LANES], (patches, LANES))
    chosen = (iota((patches, LANES), 0) == order).astype(BF16)
    dims = (((0,), (0,)), ((), ()))
    teacher = lax.dot_general(chosen, teacher_ref[...], dims, preferred_element_type=F32)
    student = lax.dot_general(chosen, student_ref[...], dims, preferred_element_type=F32)
    count = jnp.full((SLOT - MOST, width), count_ref[0, 0], jnp.int32).astype(F32)
    sent_ref[...] = jnp.concatenate([teacher[:MOST], count, student[:EARLY]], axis=0).astype(BF16)
    for half in range(2):
        late = student[EARLY + half * LATE : EARLY + (half + 1) * LATE]
        late_ref[half] = jnp.concatenate([late[:, :LANES], late[:, LANES:]], axis=0).astype(BF16)
    picked_ref[...] = student[:SLOT].astype(BF16)


def compact(gathered, starts, counts, rows, first, length, shift):
    images, slots, width = gathered.shape
    total = images * slots
    lane, image = iota((images, total), 1), iota((images, total), 0)
    within = lane - image * slots - first
    member = jnp.logical_and(within >= 0, within < length)
    place = (within + shift).astype(F32)
    used = jnp.logical_and(member, place < counts[:, :1])
    row = jnp.sum(jnp.where(used, starts[:, :1] + place + 1.0, 0.0), axis=0, keepdims=True) - 1.0
    chosen = (iota((rows, total), 0).astype(F32) == row).astype(BF16)
    return jnp.dot(chosen, gathered.reshape(total, width), preferred_element_type=F32)


def spread(starts, counts, slots, rows):
    images = starts.shape[0]
    shape = (images, slots, rows)
    within = iota(shape, 1)
    row = (iota(shape, 2) - within).astype(F32) - starts[:, :1].reshape(images, 1, 1)
    used = jnp.logical_and(row == 0.0, within.astype(F32) < counts[:, :1].reshape(images, 1, 1))
    return used.astype(F32).astype(BF16).reshape(images * slots, rows)


def column_kernel(gathered_ref, index_ref, far_ref, share_ref, rows_ref, places_ref, near_ref, sems):
    block, blocks = fetch(far_ref, near_ref, sems)
    images = gathered_ref.shape[0]
    counts = gathered_ref[:, MOST:SLOT, :LANES].astype(F32)[:, 0]
    before = (iota((images, images), 1) < iota((images, images), 0)).astype(BF16)
    starts = jnp.dot(before, counts.astype(BF16), preferred_element_type=F32)
    half, core = images // 2, index_ref[0, 0] % 2
    place = iota((images, images), 0)
    image = jnp.where(place < half, 2 * place + core, 2 * (place - half) + 1 - core)
    other = iota((images, images), 1)
    places_ref[0] = jnp.dot((other < image).astype(BF16), counts.astype(BF16), preferred_element_type=F32)
    places_ref[1] = jnp.dot((other == image).astype(BF16), counts.astype(BF16), preferred_element_type=F32)
    places_ref[2] = starts
    places_ref[3] = counts
    rows = compact(gathered_ref[:, :SLOT], starts, counts, rows_ref.shape[0], 0, MOST, 0).astype(BF16)
    rows_ref[...] = rows
    for b in blocks:
        logits = jnp.dot(rows, block(b), preferred_element_type=F32) * TEACH
        high = jnp.max(logits, axis=0, keepdims=True)
        total = jnp.sum(jnp.exp(logits - high), axis=0, keepdims=True)
        lines = to_lines(high + jnp.log(total))
        share_ref[:, lines_of(b)] = jnp.broadcast_to(lines[None], (share_ref.shape[0],) + lines.shape)


def split(values, parts):
    out = []
    for _ in range(parts):
        part = values.astype(BF16)
        out.append(part)
        values = values - part.astype(F32)
    return out


def fill_share(share_ref, lines):
    blank = jnp.zeros((share_ref.shape[1] - lines.shape[0], LANES), F32)
    share_ref[...] = jnp.broadcast_to(jnp.concatenate([lines, blank], axis=0)[None], share_ref.shape)


def row_kernel(shares_ref, rows_ref, protos_ref, late_ref, matrix_ref, high_ref, share_ref):
    column = merged(shares_ref[...])
    rows = rows_ref[...]
    highs, sums = [], []
    for b in range(high_ref.shape[0]):
        logits = jnp.dot(rows, protos_ref[:, columns(b)], preferred_element_type=F32) * TEACH
        shifted = logits - to_row(column[lines_of(b)])
        high = jnp.max(shifted, axis=1, keepdims=True)
        exact = jnp.exp(shifted - high)
        matrix_ref[:, columns(b)] = exact.astype(BF16)
        high_ref[b] = high
        highs.append(high)
        sums.append(jnp.sum(exact, axis=1, keepdims=True))
    top = functools.reduce(jnp.maximum, highs)
    total = sum(jnp.exp(high - top) * part for high, part in zip(highs, sums))
    own = jnp.concatenate([part.astype(F32) for part in split(to_lanes(top + jnp.log(total)), 3)], axis=0)
    blank = jnp.zeros((share_ref.shape[2] - 2 * LATE - own.shape[0], LANES), F32)
    numbers = jnp.concatenate([own, blank], axis=0).astype(BF16)
    for half in range(2):
        chunk = jnp.concatenate([late_ref[half], numbers], axis=0)
        share_ref[:, half] = jnp.broadcast_to(chunk[None], (share_ref.shape[0],) + chunk.shape)


def column_sums(matrix_ref, scale, share_ref):
    for b in range(scale.shape[0]):
        sums = jnp.sum(matrix_ref[:, columns(b)].astype(F32) * scale[b], axis=0, keepdims=True)
        lines = to_lines(sums)
        shape = (share_ref.shape[0],) + lines.shape
        share_ref[:, lines_of(b)] = jnp.broadcast_to(lines[None], shape).astype(share_ref.dtype)


def first_column_kernel(shares_ref, high_ref, matrix_ref, share_ref, scale_ref):
    lines = scale_ref.shape[1] // LANES
    numbers = shares_ref[:, 2 * LATE :].astype(F32)
    row_lse = merged(sum(numbers[:, k * lines : (k + 1) * lines] for k in range(3)))
    scale = jnp.exp(high_ref[...] - to_column(row_lse)[None])
    scale_ref[...] = scale
    column_sums(matrix_ref, scale, share_ref)


def later_column_kernel(shares_ref, scale_in_ref, matrix_ref, share_ref, scale_ref):
    lines = scale_ref.shape[1] // LANES
    total = to_column(jnp.sum(shares_ref[...][:, :lines], axis=0))
    scale = scale_in_ref[...] / total[None]
    scale_ref[...] = scale
    column_sums(matrix_ref, scale, share_ref)


def inverse_of(shares_ref):
    return 1.0 / jnp.sum(shares_ref[...].astype(F32), axis=0)


def later_row_kernel(shares_ref, scale_ref, matrix_ref, share_ref):
    inverse = inverse_of(shares_ref)
    sums = 0.0
    for b in range(scale_ref.shape[0]):
        scaled = matrix_ref[:, columns(b)].astype(F32) * to_row(inverse[lines_of(b)])
        sums += scale_ref[b] * jnp.sum(scaled, axis=1, keepdims=True)
    fill_share(share_ref, to_lanes(sums))


def pack(sums, numbers, parts, starts, counts):
    rows, width = sums.shape
    images = starts.shape[0]
    chosen = spread(starts, counts, SLOT, rows)
    packed = jnp.dot(chosen, sums.astype(BF16), preferred_element_type=F32).astype(BF16)
    row = split(to_row(to_lanes(numbers)), parts)
    row = jnp.concatenate([part.astype(F32) for part in row] + [jnp.zeros((SLOT - MOST - parts, rows), F32)], axis=0)
    tail = lax.dot_general(row.astype(BF16), chosen, (((1,), (1,)), ((), ())), preferred_element_type=F32)
    tail = jnp.concatenate([tail, jnp.zeros((SLOT - MOST, LANES), F32)], axis=1)
    blank = jnp.zeros((SLOT - MOST, width - LANES), F32)
    tail = [jnp.concatenate([tail[:, j * SLOT : j * SLOT + LANES], blank], axis=1)[None] for j in range(images)]
    return packed.reshape(images, SLOT, width)[:, :MOST], jnp.concatenate(tail, axis=0).astype(BF16)


def join(tail, width):
    images = tail[0].shape[0]
    filler = jnp.zeros((images, 1, width - LANES), F32)
    rows = [jnp.concatenate([part.astype(F32), filler], axis=2) for part in tail]
    rows.append(jnp.zeros((images, SLOT - MOST - len(tail), width), F32))
    return jnp.concatenate(rows, axis=1).astype(BF16)


def numbers_of(chunk, parts):
    tail = chunk[:, MOST:SLOT, :LANES].astype(F32)
    return sum(tail[:, k] for k in range(parts))


def put(own_ref, other_ref, rows, tail):
    half = own_ref.shape[0]
    own_ref[:, :MOST], own_ref[:, MOST:] = rows[:half], tail[:half]
    other_ref[:, :MOST], other_ref[:, MOST:] = rows[half:], tail[half:]


def slots_of(lanes):
    images = lanes.shape[0]
    same = iota((1, MOST, LANES), 1) == iota((1, MOST, LANES), 2)
    return jnp.sum(jnp.where(same, lanes.reshape(images, 1, LANES), 0.0), axis=2, keepdims=True)


def target_kernel(shares_ref, scale_ref, matrix_ref, protos_ref, places_ref, own_ref, other_ref, sums, total):
    step = pl.program_id(0)
    scale = scale_ref[step]
    weights = (matrix_ref[...].astype(F32) * to_row(inverse_of(shares_ref))).astype(BF16)
    part = scale * lax.dot_general(weights, protos_ref[...], (((1,), (1,)), ((), ())), preferred_element_type=F32)
    mass = scale * jnp.sum(weights.astype(F32), axis=1, keepdims=True)

    @pl.when(step == 0)
    def _():
        sums[...] = part
        total[...] = mass

    @pl.when(step > 0)
    def _():
        sums[...] += part
        total[...] += mass

    @pl.when(step == pl.num_programs(0) - 1)
    def _():
        put(own_ref, other_ref, *pack(sums[...], total[...], 2, places_ref[0], places_ref[1]))


def merge_kernel(own_ref, came_ref, student_own_ref, student_came_ref, out_ref):
    width = own_ref.shape[2]
    out_ref[:, :MOST] = (own_ref[:, :MOST].astype(F32) + came_ref[:, :MOST].astype(F32)).astype(BF16)
    total = numbers_of(own_ref, 2) + numbers_of(came_ref, 2)
    out_ref[:, MOST:SLOT] = join([part[:, None] for part in split(total, 2)], width)
    own, came = numbers_of(student_own_ref, 3), numbers_of(student_came_ref, 3)
    high = jnp.maximum(own, came)
    joint = high + jnp.log(jnp.exp(own - high) + jnp.exp(came - high))
    mean = student_own_ref[:, :MOST].astype(F32) * slots_of(jnp.exp(own - joint))
    mean = mean + student_came_ref[:, :MOST].astype(F32) * slots_of(jnp.exp(came - joint))
    out_ref[:, SLOT : SLOT + MOST] = mean.astype(BF16)
    out_ref[:, SLOT + MOST :] = join([part[:, None] for part in split(joint, 3)], width)


def student_kernel(
    gathered_ref, late_ref, came_ref, index_ref, places_ref, protos_ref, own_ref, other_ref, rows_ref, sums, top, total
):
    step = pl.program_id(0)

    @pl.when(step == 0)
    def _():
        starts, counts, core = places_ref[2], places_ref[3], index_ref[0, 0] % 2
        rows = rows_ref.shape[0]
        found = compact(gathered_ref[:, SLOT:], starts, counts, rows, 0, EARLY, 0)
        for ref, half in ((late_ref, core), (came_ref, 1 - core)):
            late = jnp.concatenate([ref[:, :LATE], ref[:, LATE : 2 * LATE]], axis=2)
            found += compact(late, starts, counts, rows, 0, LATE, EARLY + half * LATE)
        rows_ref[...] = found.astype(BF16)
        top[...] = jnp.full(top.shape, -1e30, F32)
        total[...] = jnp.zeros(total.shape, F32)
        sums[...] = jnp.zeros(sums.shape, F32)

    protos = protos_ref[...]
    logits = jnp.dot(rows_ref[...], protos, preferred_element_type=F32) * STUD
    before = top[...]
    high = jnp.maximum(before, jnp.max(logits, axis=1, keepdims=True))
    shrink = jnp.exp(before - high)
    exact = jnp.exp(logits - high)
    total[...] = total[...] * shrink + jnp.sum(exact, axis=1, keepdims=True)
    part = lax.dot_general(exact.astype(BF16), protos, (((1,), (1,)), ((), ())), preferred_element_type=F32)
    sums[...] = sums[...] * shrink + part
    top[...] = high

    @pl.when(step == pl.num_programs(0) - 1)
    def _():
        mean, own_lse = sums[...] / total[...], top[...] + jnp.log(total[...])
        put(own_ref, other_ref, *pack(mean, own_lse, 3, places_ref[0], places_ref[1]))


def blend(chunk, lse):
    joint = merged(lse)
    weights = slots_of(jnp.exp(lse - joint[None]))
    return jnp.sum(chunk * weights, axis=0), joint


def finish_kernel(back_ref, picked_ref, order_ref, count_ref, grad_ref, loss_ref):
    patches, width = grad_ref.shape
    target = jnp.sum(back_ref[:, :SLOT].astype(F32), axis=0)
    mass = to_column((target[MOST : MOST + 1] + target[MOST + 1 : MOST + 2])[:, :LANES])[:MOST]
    tail = back_ref[:, SLOT + MOST : 2 * SLOT, :LANES].astype(F32)
    soft, lse_lanes = blend(back_ref[:, SLOT : SLOT + MOST].astype(F32), sum(tail[:, k] for k in range(3)))
    used = iota((MOST, 1), 0) < count_ref[0, 0]
    mean = target[:MOST] / jnp.where(used, mass, 1.0)
    own_lse = to_column(lse_lanes.reshape(1, LANES))[:MOST]
    cross = own_lse - STUD * jnp.sum(picked_ref[:MOST].astype(F32) * mean, axis=1, keepdims=True)
    cross = jnp.sum(jnp.where(used, cross, 0.0), axis=0, keepdims=True)
    loss_ref[...] = cross / jnp.full((1, 1), count_ref[0, 0], jnp.int32).astype(F32)
    rows = jnp.where(used, STUD * (soft - mean), 0.0)
    rows = jnp.concatenate([rows, jnp.zeros((LANES - MOST, width), F32)], axis=0).astype(BF16)
    order = jnp.broadcast_to(order_ref[:, :LANES], (patches, LANES))
    chosen = (iota((patches, LANES), 0) == order).astype(BF16)
    grad_ref[...] = jnp.dot(chosen, rows, preferred_element_type=F32).astype(BF16)


def body(student_patches, teacher_patches, mask_order, counts, student_protos, teacher_protos):
    width = lax.axis_size("proto")
    groups = lax.axis_size("dp")
    rows = MASK_DEV * width
    lines = rows // LANES
    patches, bot = student_patches.shape[1:]
    protos = student_protos.shape[1]
    steps = protos // BLOCK
    depth = 8
    index = lax.axis_index("proto").astype(jnp.int32).reshape(1, 1)
    over = functools.partial(lax.all_to_all, split_axis=0, concat_axis=0, tiled=True)
    near = ((bot, protos), BF16)
    grid = (steps,)
    wide = pl.BlockSpec((bot, BLOCK), lambda k: (0, k))
    peer = pl.BlockSpec((groups, BLOCK // LANES, LANES), lambda k: (0, k, 0))
    square = pl.BlockSpec((rows, BLOCK), lambda k: (0, k))
    column = pltpu.VMEM((rows, 1), F32)
    sems = [pltpu.SemaphoreType.DMA((protos // PIECE,))]
    far = functools.partial(pltpu.with_memory_space_constraint, memory_space=pltpu.HBM)
    student_patches, teacher_patches, mask_order = far(student_patches[0]), far(teacher_patches[0]), far(mask_order)
    student_protos, teacher_protos = far(student_protos), far(teacher_protos)
    dot = 2 * rows * protos * bot

    sent, late, picked = call(
        pick_kernel,
        [((SLOT + EARLY, bot), BF16), ((2, 2 * LATE, LANES), BF16), pltpu.HBM((SLOT, bot), BF16)],
        teacher_patches,
        student_patches,
        mask_order,
        counts,
        in_specs=[VMEM, VMEM, VMEM, SMEM],
        moved=4 * patches * bot,
    )
    gathered = lax.all_gather(sent, "proto", axis=0, tiled=False)
    share, teacher_rows, places, near_teacher = call(
        column_kernel,
        [((groups, protos // LANES, LANES), F32), ((rows, bot), BF16), pltpu.HBM((4, width, LANES), F32), near],
        gathered,
        index,
        teacher_protos,
        in_specs=[VMEM, SMEM, HBM],
        scratch=sems,
        flops=dot,
        moved=2 * bot * protos,
    )
    shares = over(share, "dp")
    matrix, high, share = call(
        row_kernel,
        [((rows, protos), BF16), ((steps, rows, 1), F32), ((width // 2, 2, 2 * LATE + 16, LANES), BF16)],
        shares,
        teacher_rows,
        near_teacher,
        late,
        flops=dot,
        moved=2 * bot * protos + 2 * rows * protos,
    )
    swap = [(p, p ^ 1) for p in range(width)]
    shares = over(share.reshape((width,) + share.shape[2:]), "proto")
    late = shares
    share, scale = call(
        first_column_kernel,
        [pltpu.HBM((groups, protos // LANES, LANES), BF16), ((steps, rows, 1), F32)],
        far(shares),
        high,
        matrix,
        moved=2 * rows * protos,
    )
    shares = over(share, "dp")
    share = call(
        later_row_kernel,
        [((width, depth, LANES), F32)],
        shares,
        scale,
        matrix,
        moved=2 * rows * protos,
    )[0]
    shares = over(share, "proto")
    share, scale = call(
        later_column_kernel,
        [pltpu.HBM((groups, protos // LANES, LANES), BF16), pltpu.HBM((steps, rows, 1), F32)],
        shares,
        scale,
        matrix,
        moved=2 * rows * protos,
    )
    late_came = lax.ppermute(late, "proto", swap)
    packed = ((width // 2, SLOT, bot), BF16)
    student_own, student_other = call(
        student_kernel,
        [pltpu.HBM(*packed), pltpu.HBM(*packed)],
        far(gathered),
        far(late),
        late_came,
        index,
        far(places),
        student_protos,
        grid=grid,
        in_specs=[VMEM, VMEM, VMEM, SMEM, VMEM, wide],
        scratch=[pltpu.VMEM((rows, bot), BF16), pltpu.VMEM((rows, bot), F32), column, column],
        flops=2 * dot,
        moved=2 * bot * protos,
    )
    student_came = lax.ppermute(student_other, "proto", swap)
    shares = over(share, "dp")
    shares, student_came = lax.optimization_barrier((shares, student_came))
    own, other = call(
        target_kernel,
        [packed, packed],
        shares,
        far(scale),
        matrix,
        student_protos,
        far(places),
        grid=grid,
        in_specs=[peer, VMEM, square, wide, VMEM],
        scratch=[pltpu.VMEM((rows, bot), F32), column],
        flops=dot,
        moved=2 * rows * protos,
    )
    came = lax.ppermute(other, "proto", swap)
    sent = call(
        merge_kernel, [((width // 2, 2 * SLOT, bot), BF16)], own, came, student_own, student_came
    )[0]
    same_core = [list(range(core, width, 2)) for core in range(2)]
    back = over(sent, "proto", axis_index_groups=same_core)
    student_grad, image_loss = call(
        finish_kernel,
        [((patches, bot), BF16), ((1, 1), F32)],
        back,
        picked,
        mask_order,
        counts,
        in_specs=[VMEM, VMEM, VMEM, SMEM],
        moved=2 * patches * bot,
    )
    return (student_grad[None], image_loss)


def solution(mesh):
    placed = (
        P(("dp", "proto"), None, None),
        P(("dp", "proto"), None, None),
        P(("dp", "proto"), None),
        P("dp", "proto"),
        P(None, "proto"),
        P(None, "proto"),
    )
    return jax.shard_map(
        body,
        mesh=mesh,
        in_specs=placed,
        out_specs=(P(("dp", "proto"), None, None), P("dp", "proto")),
        check_vma=False,
    )
```

```python
import functools

import jax
import jax.numpy as jnp
from jax import lax
from jax.experimental import pallas as pl
from jax.experimental.pallas import tpu as pltpu
from jax.sharding import PartitionSpec as P

MASK_DEV = 24
MOST = 72
EARLY = 40
LATE = (MOST - EARLY) // 2
SLOT = 80
TEACH = 1.0 / 0.07
STUD = 1.0 / 0.1
F32 = jnp.float32
BF16 = jnp.bfloat16
LANES = 128
BLOCK = 2048
PIECE = 1024
LIMIT = 24 << 20
VMEM = pl.BlockSpec(memory_space=pltpu.VMEM)
SMEM = pl.BlockSpec(memory_space=pltpu.SMEM)


HBM = pl.BlockSpec(memory_space=pl.ANY)


def call(kernel, out_shape, *args, in_specs=None, scratch=(), grid=None, flops=0, moved=0):
    out_shape = [jax.ShapeDtypeStruct(*o) if isinstance(o, tuple) else o for o in out_shape]
    extra = {} if grid is None else {"grid": grid}
    return pl.pallas_call(
        kernel,
        out_shape=out_shape,
        in_specs=[VMEM] * len(args) if in_specs is None else in_specs,
        out_specs=[VMEM] * len(out_shape),
        scratch_shapes=list(scratch),
        compiler_params=pltpu.CompilerParams(vmem_limit_bytes=LIMIT),
        cost_estimate=pl.CostEstimate(flops=flops, bytes_accessed=moved, transcendentals=0),
        **extra,
    )(*args)


def fetch(far_ref, near_ref, sems):
    copies = []
    for k in range(near_ref.shape[1] // PIECE):
        piece = slice(k * PIECE, (k + 1) * PIECE)
        copies.append(pltpu.make_async_copy(far_ref.at[:, piece], near_ref.at[:, piece], sems.at[k]))
        copies[-1].start()

    def block(b):
        for copy in copies[b * BLOCK // PIECE : (b + 1) * BLOCK // PIECE]:
            copy.wait()
        return near_ref[:, b * BLOCK : (b + 1) * BLOCK]

    return block, range(near_ref.shape[1] // BLOCK)


def columns(b):
    return slice(b * BLOCK, (b + 1) * BLOCK)


def lines_of(b):
    return slice(b * BLOCK // LANES, (b + 1) * BLOCK // LANES)


def iota(shape, dim):
    return lax.broadcasted_iota(jnp.int32, shape, dim)


def eye():
    return iota((LANES, LANES), 0) == iota((LANES, LANES), 1)


def to_lanes(column):
    parts = []
    for b in range(column.shape[0] // LANES):
        part = jnp.broadcast_to(column[b * LANES : (b + 1) * LANES], (LANES, LANES))
        parts.append(jnp.sum(jnp.where(eye(), part, 0.0), axis=0, keepdims=True))
    return jnp.concatenate(parts, axis=0)


def to_column(lanes):
    parts = []
    for b in range(lanes.shape[0]):
        part = jnp.broadcast_to(lanes[b : b + 1], (LANES, LANES))
        parts.append(jnp.sum(jnp.where(eye(), part, 0.0), axis=1, keepdims=True))
    return jnp.concatenate(parts, axis=0)


def to_lines(row):
    return jnp.concatenate([row[:, b * LANES : (b + 1) * LANES] for b in range(row.shape[1] // LANES)], axis=0)


def to_row(lines):
    return jnp.concatenate([lines[b : b + 1] for b in range(lines.shape[0])], axis=1)


def merged(shares):
    top = jnp.max(shares, axis=0)
    return top + jnp.log(jnp.sum(jnp.exp(shares - top[None]), axis=0))


def pick_kernel(teacher_ref, student_ref, order_ref, count_ref, sent_ref, late_ref, picked_ref):
    patches, width = teacher_ref.shape
    order = jnp.broadcast_to(order_ref[:, :LANES], (patches, LANES))
    chosen = (iota((patches, LANES), 0) == order).astype(BF16)
    dims = (((0,), (0,)), ((), ()))
    teacher = lax.dot_general(chosen, teacher_ref[...], dims, preferred_element_type=F32)
    student = lax.dot_general(chosen, student_ref[...], dims, preferred_element_type=F32)
    count = jnp.full((SLOT - MOST, width), count_ref[0, 0], jnp.int32).astype(F32)
    sent_ref[...] = jnp.concatenate([teacher[:MOST], count, student[:EARLY]], axis=0).astype(BF16)
    for half in range(2):
        late = student[EARLY + half * LATE : EARLY + (half + 1) * LATE]
        late_ref[half] = jnp.concatenate([late[:, :LANES], late[:, LANES:]], axis=0).astype(BF16)
    picked_ref[...] = student[:SLOT].astype(BF16)


def compact(gathered, starts, counts, rows, first, length, shift):
    images, slots, width = gathered.shape
    total = images * slots
    lane, image = iota((images, total), 1), iota((images, total), 0)
    within = lane - image * slots - first
    member = jnp.logical_and(within >= 0, within < length)
    place = (within + shift).astype(F32)
    used = jnp.logical_and(member, place < counts[:, :1])
    row = jnp.sum(jnp.where(used, starts[:, :1] + place + 1.0, 0.0), axis=0, keepdims=True) - 1.0
    chosen = (iota((rows, total), 0).astype(F32) == row).astype(BF16)
    return jnp.dot(chosen, gathered.reshape(total, width), preferred_element_type=F32)


def spread(starts, counts, slots, rows):
    images = starts.shape[0]
    shape = (images, slots, rows)
    within = iota(shape, 1)
    row = (iota(shape, 2) - within).astype(F32) - starts[:, :1].reshape(images, 1, 1)
    used = jnp.logical_and(row == 0.0, within.astype(F32) < counts[:, :1].reshape(images, 1, 1))
    return used.astype(F32).astype(BF16).reshape(images * slots, rows)


def column_kernel(gathered_ref, index_ref, far_ref, share_ref, rows_ref, places_ref, near_ref, sems):
    block, blocks = fetch(far_ref, near_ref, sems)
    images = gathered_ref.shape[0]
    counts = gathered_ref[:, MOST:SLOT, :LANES].astype(F32)[:, 0]
    before = (iota((images, images), 1) < iota((images, images), 0)).astype(BF16)
    starts = jnp.dot(before, counts.astype(BF16), preferred_element_type=F32)
    half, core = images // 2, index_ref[0, 0] % 2
    place = iota((images, images), 0)
    image = jnp.where(place < half, 2 * place + core, 2 * (place - half) + 1 - core)
    other = iota((images, images), 1)
    places_ref[0] = jnp.dot((other < image).astype(BF16), counts.astype(BF16), preferred_element_type=F32)
    places_ref[1] = jnp.dot((other == image).astype(BF16), counts.astype(BF16), preferred_element_type=F32)
    places_ref[2] = starts
    places_ref[3] = counts
    rows = compact(gathered_ref[:, :SLOT], starts, counts, rows_ref.shape[0], 0, MOST, 0).astype(BF16)
    rows_ref[...] = rows
    for b in blocks:
        logits = jnp.dot(rows, block(b), preferred_element_type=F32) * TEACH
        high = jnp.max(logits, axis=0, keepdims=True)
        total = jnp.sum(jnp.exp(logits - high), axis=0, keepdims=True)
        lines = to_lines(high + jnp.log(total))
        share_ref[:, lines_of(b)] = jnp.broadcast_to(lines[None], (share_ref.shape[0],) + lines.shape)


def split(values, parts):
    out = []
    for _ in range(parts):
        part = values.astype(BF16)
        out.append(part)
        values = values - part.astype(F32)
    return out


def fill_share(share_ref, lines):
    blank = jnp.zeros((share_ref.shape[1] - lines.shape[0], LANES), F32)
    share_ref[...] = jnp.broadcast_to(jnp.concatenate([lines, blank], axis=0)[None], share_ref.shape)


def row_kernel(shares_ref, rows_ref, protos_ref, late_ref, matrix_ref, high_ref, share_ref):
    column = merged(shares_ref[...])
    rows = rows_ref[...]
    highs, sums = [], []
    for b in range(high_ref.shape[0]):
        logits = jnp.dot(rows, protos_ref[:, columns(b)], preferred_element_type=F32) * TEACH
        shifted = logits - to_row(column[lines_of(b)])
        high = jnp.max(shifted, axis=1, keepdims=True)
        exact = jnp.exp(shifted - high)
        matrix_ref[:, columns(b)] = exact.astype(BF16)
        high_ref[b] = high
        highs.append(high)
        sums.append(jnp.sum(exact, axis=1, keepdims=True))
    top = functools.reduce(jnp.maximum, highs)
    total = sum(jnp.exp(high - top) * part for high, part in zip(highs, sums))
    own = jnp.concatenate([part.astype(F32) for part in split(to_lanes(top + jnp.log(total)), 3)], axis=0)
    blank = jnp.zeros((share_ref.shape[2] - 2 * LATE - own.shape[0], LANES), F32)
    numbers = jnp.concatenate([own, blank], axis=0).astype(BF16)
    for half in range(2):
        chunk = jnp.concatenate([late_ref[half], numbers], axis=0)
        share_ref[:, half] = jnp.broadcast_to(chunk[None], (share_ref.shape[0],) + chunk.shape)


def column_sums(matrix_ref, scale, share_ref):
    for b in range(scale.shape[0]):
        sums = jnp.sum(matrix_ref[:, columns(b)].astype(F32) * scale[b], axis=0, keepdims=True)
        lines = to_lines(sums)
        shape = (share_ref.shape[0],) + lines.shape
        share_ref[:, lines_of(b)] = jnp.broadcast_to(lines[None], shape).astype(share_ref.dtype)


def first_column_kernel(shares_ref, high_ref, matrix_ref, share_ref, scale_ref, late_ref):
    late_ref[...] = shares_ref[:, : 2 * LATE]
    lines = scale_ref.shape[1] // LANES
    numbers = shares_ref[:, 2 * LATE :].astype(F32)
    row_lse = merged(sum(numbers[:, k * lines : (k + 1) * lines] for k in range(3)))
    scale = jnp.exp(high_ref[...] - to_column(row_lse)[None])
    scale_ref[...] = scale
    column_sums(matrix_ref, scale, share_ref)


def later_column_kernel(shares_ref, scale_in_ref, matrix_ref, share_ref, scale_ref):
    lines = scale_in_ref.shape[1] // LANES
    total = to_column(jnp.sum(shares_ref[...][:, :lines], axis=0))
    scale = scale_in_ref[...] / total[None]
    for b in range(scale.shape[0]):
        scale_ref[b] = to_lanes(scale[b])
    column_sums(matrix_ref, scale, share_ref)


def inverse_of(shares_ref):
    return 1.0 / jnp.sum(shares_ref[...].astype(F32), axis=0)


def later_row_kernel(shares_ref, scale_ref, matrix_ref, share_ref):
    inverse = inverse_of(shares_ref)
    sums = 0.0
    for b in range(scale_ref.shape[0]):
        scaled = matrix_ref[:, columns(b)].astype(F32) * to_row(inverse[lines_of(b)])
        sums += scale_ref[b] * jnp.sum(scaled, axis=1, keepdims=True)
    fill_share(share_ref, to_lanes(sums))


def pack(sums, numbers, parts, starts, counts):
    rows, width = sums.shape
    images = starts.shape[0]
    chosen = spread(starts, counts, SLOT, rows)
    packed = jnp.dot(chosen, sums.astype(BF16), preferred_element_type=F32).astype(BF16)
    row = split(to_row(to_lanes(numbers)), parts)
    row = jnp.concatenate([part.astype(F32) for part in row] + [jnp.zeros((SLOT - MOST - parts, rows), F32)], axis=0)
    tail = lax.dot_general(row.astype(BF16), chosen, (((1,), (1,)), ((), ())), preferred_element_type=F32)
    tail = jnp.concatenate([tail, jnp.zeros((SLOT - MOST, LANES), F32)], axis=1)
    blank = jnp.zeros((SLOT - MOST, width - LANES), F32)
    tail = [jnp.concatenate([tail[:, j * SLOT : j * SLOT + LANES], blank], axis=1)[None] for j in range(images)]
    return packed.reshape(images, SLOT, width)[:, :MOST], jnp.concatenate(tail, axis=0).astype(BF16)


def join(tail, width):
    images = tail[0].shape[0]
    filler = jnp.zeros((images, 1, width - LANES), F32)
    rows = [jnp.concatenate([part.astype(F32), filler], axis=2) for part in tail]
    rows.append(jnp.zeros((images, SLOT - MOST - len(tail), width), F32))
    return jnp.concatenate(rows, axis=1).astype(BF16)


def numbers_of(chunk, parts):
    tail = chunk[:, MOST:SLOT, :LANES].astype(F32)
    return sum(tail[:, k] for k in range(parts))


def put(own_ref, other_ref, rows, tail):
    half = own_ref.shape[0]
    own_ref[:, :MOST], own_ref[:, MOST:] = rows[:half], tail[:half]
    other_ref[:, :MOST], other_ref[:, MOST:] = rows[half:], tail[half:]


def slots_of(lanes):
    images = lanes.shape[0]
    same = iota((1, MOST, LANES), 1) == iota((1, MOST, LANES), 2)
    return jnp.sum(jnp.where(same, lanes.reshape(images, 1, LANES), 0.0), axis=2, keepdims=True)


def target_kernel(shares_ref, scale_ref, matrix_ref, protos_ref, places_ref, own_ref, other_ref, sums, total):
    step = pl.program_id(0)
    scale = to_column(scale_ref[step])
    weights = (matrix_ref[...].astype(F32) * to_row(inverse_of(shares_ref))).astype(BF16)
    part = scale * lax.dot_general(weights, protos_ref[...], (((1,), (1,)), ((), ())), preferred_element_type=F32)
    mass = scale * jnp.sum(weights.astype(F32), axis=1, keepdims=True)

    @pl.when(step == 0)
    def _():
        sums[...] = part
        total[...] = mass

    @pl.when(step > 0)
    def _():
        sums[...] += part
        total[...] += mass

    @pl.when(step == pl.num_programs(0) - 1)
    def _():
        put(own_ref, other_ref, *pack(sums[...], total[...], 2, places_ref[0], places_ref[1]))


def merge_kernel(own_ref, came_ref, student_own_ref, student_came_ref, out_ref):
    width = own_ref.shape[2]
    out_ref[:, :MOST] = (own_ref[:, :MOST].astype(F32) + came_ref[:, :MOST].astype(F32)).astype(BF16)
    total = numbers_of(own_ref, 2) + numbers_of(came_ref, 2)
    own, came = numbers_of(student_own_ref, 3), numbers_of(student_came_ref, 3)
    high = jnp.maximum(own, came)
    joint = high + jnp.log(jnp.exp(own - high) + jnp.exp(came - high))
    mean = student_own_ref[:, :MOST].astype(F32) * slots_of(jnp.exp(own - joint))
    mean = mean + student_came_ref[:, :MOST].astype(F32) * slots_of(jnp.exp(came - joint))
    out_ref[:, MOST : 2 * MOST] = mean.astype(BF16)
    out_ref[:, 2 * MOST :] = join([part[:, None] for part in split(total, 2) + split(joint, 3)], width)


def student_kernel(
    gathered_ref, late_ref, came_ref, index_ref, places_ref, protos_ref, own_ref, other_ref, rows_ref, sums, top, total
):
    step = pl.program_id(0)

    @pl.when(step == 0)
    def _():
        starts, counts, core = places_ref[2], places_ref[3], index_ref[0, 0] % 2
        rows = rows_ref.shape[0]
        found = compact(gathered_ref[:, SLOT:], starts, counts, rows, 0, EARLY, 0)
        for ref, half in ((late_ref, core), (came_ref, 1 - core)):
            late = jnp.concatenate([ref[:, :LATE], ref[:, LATE : 2 * LATE]], axis=2)
            found += compact(late, starts, counts, rows, 0, LATE, EARLY + half * LATE)
        rows_ref[...] = found.astype(BF16)
        top[...] = jnp.full(top.shape, -1e30, F32)
        total[...] = jnp.zeros(total.shape, F32)
        sums[...] = jnp.zeros(sums.shape, F32)

    protos = protos_ref[...]
    logits = jnp.dot(rows_ref[...], protos, preferred_element_type=F32) * STUD
    before = top[...]
    high = jnp.maximum(before, jnp.max(logits, axis=1, keepdims=True))
    shrink = jnp.exp(before - high)
    exact = jnp.exp(logits - high)
    total[...] = total[...] * shrink + jnp.sum(exact, axis=1, keepdims=True)
    part = lax.dot_general(exact.astype(BF16), protos, (((1,), (1,)), ((), ())), preferred_element_type=F32)
    sums[...] = sums[...] * shrink + part
    top[...] = high

    @pl.when(step == pl.num_programs(0) - 1)
    def _():
        mean, own_lse = sums[...] / total[...], top[...] + jnp.log(total[...])
        put(own_ref, other_ref, *pack(mean, own_lse, 3, places_ref[0], places_ref[1]))


def blend(chunk, lse):
    joint = merged(lse)
    weights = slots_of(jnp.exp(lse - joint[None]))
    return jnp.sum(chunk * weights, axis=0), joint


def finish_kernel(back_ref, picked_ref, order_ref, count_ref, grad_ref, loss_ref):
    patches, width = grad_ref.shape
    target = jnp.sum(back_ref[:, :MOST].astype(F32), axis=0)
    tail = back_ref[:, 2 * MOST :, :LANES].astype(F32)
    mass = to_column(jnp.sum(tail[:, 0] + tail[:, 1], axis=0, keepdims=True))[:MOST]
    soft, lse_lanes = blend(back_ref[:, MOST : 2 * MOST].astype(F32), tail[:, 2] + tail[:, 3] + tail[:, 4])
    used = iota((MOST, 1), 0) < count_ref[0, 0]
    mean = target / jnp.where(used, mass, 1.0)
    own_lse = to_column(lse_lanes.reshape(1, LANES))[:MOST]
    cross = own_lse - STUD * jnp.sum(picked_ref[:MOST].astype(F32) * mean, axis=1, keepdims=True)
    cross = jnp.sum(jnp.where(used, cross, 0.0), axis=0, keepdims=True)
    loss_ref[...] = cross / jnp.full((1, 1), count_ref[0, 0], jnp.int32).astype(F32)
    rows = jnp.where(used, STUD * (soft - mean), 0.0)
    rows = jnp.concatenate([rows, jnp.zeros((LANES - MOST, width), F32)], axis=0).astype(BF16)
    order = jnp.broadcast_to(order_ref[:, :LANES], (patches, LANES))
    chosen = (iota((patches, LANES), 0) == order).astype(BF16)
    grad_ref[...] = jnp.dot(chosen, rows, preferred_element_type=F32).astype(BF16)


def body(student_patches, teacher_patches, mask_order, counts, student_protos, teacher_protos):
    width = lax.axis_size("proto")
    groups = lax.axis_size("dp")
    rows = MASK_DEV * width
    lines = rows // LANES
    patches, bot = student_patches.shape[1:]
    protos = student_protos.shape[1]
    steps = protos // BLOCK
    depth = 8
    index = lax.axis_index("proto").astype(jnp.int32).reshape(1, 1)
    over = functools.partial(lax.all_to_all, split_axis=0, concat_axis=0, tiled=True)
    near = ((bot, protos), BF16)
    grid = (steps,)
    wide = pl.BlockSpec((bot, BLOCK), lambda k: (0, k))
    peer = pl.BlockSpec((groups, BLOCK // LANES, LANES), lambda k: (0, k, 0))
    square = pl.BlockSpec((rows, BLOCK), lambda k: (0, k))
    column = pltpu.VMEM((rows, 1), F32)
    sems = [pltpu.SemaphoreType.DMA((protos // PIECE,))]
    far = functools.partial(pltpu.with_memory_space_constraint, memory_space=pltpu.HBM)
    student_patches, teacher_patches, mask_order = far(student_patches[0]), far(teacher_patches[0]), far(mask_order)
    student_protos, teacher_protos = far(student_protos), far(teacher_protos)
    dot = 2 * rows * protos * bot

    sent, late, picked = call(
        pick_kernel,
        [((SLOT + EARLY, bot), BF16), ((2, 2 * LATE, LANES), BF16), pltpu.HBM((SLOT, bot), BF16)],
        teacher_patches,
        student_patches,
        mask_order,
        counts,
        in_specs=[VMEM, VMEM, VMEM, SMEM],
        moved=4 * patches * bot,
    )
    gathered = lax.all_gather(sent, "proto", axis=0, tiled=False)
    share, teacher_rows, places, near_teacher = call(
        column_kernel,
        [((groups, protos // LANES, LANES), F32), ((rows, bot), BF16), pltpu.HBM((4, width, LANES), F32), near],
        gathered,
        index,
        teacher_protos,
        in_specs=[VMEM, SMEM, HBM],
        scratch=sems,
        flops=dot,
        moved=2 * bot * protos,
    )
    shares = over(share, "dp")
    matrix, high, share = call(
        row_kernel,
        [((rows, protos), BF16), ((steps, rows, 1), F32), ((width // 2, 2, 2 * LATE + 16, LANES), BF16)],
        shares,
        teacher_rows,
        near_teacher,
        late,
        flops=dot,
        moved=2 * bot * protos + 2 * rows * protos,
    )
    swap = [(p, p ^ 1) for p in range(width)]
    shares = over(share.reshape((width,) + share.shape[2:]), "proto")
    share, scale, late = call(
        first_column_kernel,
        [
            ((groups, protos // LANES, LANES), BF16),
            ((steps, rows, 1), F32),
            pltpu.HBM((width, 2 * LATE, LANES), BF16),
        ],
        shares,
        high,
        matrix,
        moved=2 * rows * protos,
    )
    shares = over(share, "dp")
    share = call(
        later_row_kernel,
        [pltpu.HBM((width, depth, LANES), F32)],
        shares,
        scale,
        matrix,
        moved=2 * rows * protos,
    )[0]
    shares = over(share, "proto")
    share, scale = call(
        later_column_kernel,
        [pltpu.HBM((groups, protos // LANES, LANES), BF16), pltpu.HBM((steps, rows // LANES, LANES), F32)],
        shares,
        scale,
        matrix,
        moved=2 * rows * protos,
    )
    late_came = lax.ppermute(late, "proto", swap)
    packed = ((width // 2, SLOT, bot), BF16)
    student_own, student_other = call(
        student_kernel,
        [pltpu.HBM(*packed), pltpu.HBM(*packed)],
        far(gathered),
        far(late),
        late_came,
        index,
        far(places),
        student_protos,
        grid=grid,
        in_specs=[VMEM, VMEM, VMEM, SMEM, VMEM, wide],
        scratch=[pltpu.VMEM((rows, bot), BF16), pltpu.VMEM((rows, bot), F32), column, column],
        flops=2 * dot,
        moved=2 * bot * protos,
    )
    student_came = lax.ppermute(student_other, "proto", swap)
    shares = over(share, "dp")
    shares, student_came = lax.optimization_barrier((shares, student_came))
    own, other = call(
        target_kernel,
        [packed, packed],
        shares,
        far(scale),
        matrix,
        student_protos,
        far(places),
        grid=grid,
        in_specs=[peer, VMEM, square, wide, VMEM],
        scratch=[pltpu.VMEM((rows, bot), F32), column],
        flops=dot,
        moved=2 * rows * protos,
    )
    came = lax.ppermute(other, "proto", swap)
    sent = call(
        merge_kernel, [((width // 2, MOST + SLOT, bot), BF16)], own, came, student_own, student_came
    )[0]
    same_core = [list(range(core, width, 2)) for core in range(2)]
    back = over(sent, "proto", axis_index_groups=same_core)
    student_grad, image_loss = call(
        finish_kernel,
        [((patches, bot), BF16), ((1, 1), F32)],
        back,
        picked,
        mask_order,
        counts,
        in_specs=[VMEM, VMEM, VMEM, SMEM],
        moved=2 * patches * bot,
    )
    return (student_grad[None], image_loss)


def solution(mesh):
    placed = (
        P(("dp", "proto"), None, None),
        P(("dp", "proto"), None, None),
        P(("dp", "proto"), None),
        P("dp", "proto"),
        P(None, "proto"),
        P(None, "proto"),
    )
    return jax.shard_map(
        body,
        mesh=mesh,
        in_specs=placed,
        out_specs=(P(("dp", "proto"), None, None), P("dp", "proto")),
        check_vma=False,
    )
```

```python
import functools

import jax
import jax.numpy as jnp
from jax import lax
from jax.experimental import pallas as pl
from jax.experimental.pallas import tpu as pltpu
from jax.sharding import PartitionSpec as P

MASK_DEV = 24
MOST = 72
EARLY = 48
LATE = MOST - EARLY
UNUSED = 100.0
SLOT = 80
TEACH = 1.0 / 0.07
STUD = 1.0 / 0.1
F32 = jnp.float32
BF16 = jnp.bfloat16
LANES = 128
BLOCK = 2048
PIECE = 1024
LIMIT = 24 << 20
VMEM = pl.BlockSpec(memory_space=pltpu.VMEM)
SMEM = pl.BlockSpec(memory_space=pltpu.SMEM)


HBM = pl.BlockSpec(memory_space=pl.ANY)


def call(kernel, out_shape, *args, in_specs=None, scratch=(), grid=None, flops=0, moved=0):
    out_shape = [jax.ShapeDtypeStruct(*o) if isinstance(o, tuple) else o for o in out_shape]
    extra = {} if grid is None else {"grid": grid}
    return pl.pallas_call(
        kernel,
        out_shape=out_shape,
        in_specs=[VMEM] * len(args) if in_specs is None else in_specs,
        out_specs=[VMEM] * len(out_shape),
        scratch_shapes=list(scratch),
        compiler_params=pltpu.CompilerParams(vmem_limit_bytes=LIMIT),
        cost_estimate=pl.CostEstimate(flops=flops, bytes_accessed=moved, transcendentals=0),
        **extra,
    )(*args)


def fetch(far_ref, near_ref, sems):
    copies = []
    for k in range(near_ref.shape[1] // PIECE):
        piece = slice(k * PIECE, (k + 1) * PIECE)
        copies.append(pltpu.make_async_copy(far_ref.at[:, piece], near_ref.at[:, piece], sems.at[k]))
        copies[-1].start()

    def block(b):
        for copy in copies[b * BLOCK // PIECE : (b + 1) * BLOCK // PIECE]:
            copy.wait()
        return near_ref[:, b * BLOCK : (b + 1) * BLOCK]

    return block, range(near_ref.shape[1] // BLOCK)


def columns(b):
    return slice(b * BLOCK, (b + 1) * BLOCK)


def lines_of(b):
    return slice(b * BLOCK // LANES, (b + 1) * BLOCK // LANES)


def iota(shape, dim):
    return lax.broadcasted_iota(jnp.int32, shape, dim)


def eye():
    return iota((LANES, LANES), 0) == iota((LANES, LANES), 1)


def to_lanes(column):
    parts = []
    for b in range(column.shape[0] // LANES):
        part = jnp.broadcast_to(column[b * LANES : (b + 1) * LANES], (LANES, LANES))
        parts.append(jnp.sum(jnp.where(eye(), part, 0.0), axis=0, keepdims=True))
    return jnp.concatenate(parts, axis=0)


def to_column(lanes):
    parts = []
    for b in range(lanes.shape[0]):
        part = jnp.broadcast_to(lanes[b : b + 1], (LANES, LANES))
        parts.append(jnp.sum(jnp.where(eye(), part, 0.0), axis=1, keepdims=True))
    return jnp.concatenate(parts, axis=0)


def to_lines(row):
    return jnp.concatenate([row[:, b * LANES : (b + 1) * LANES] for b in range(row.shape[1] // LANES)], axis=0)


def to_row(lines):
    return jnp.concatenate([lines[b : b + 1] for b in range(lines.shape[0])], axis=1)


def merged(shares):
    top = jnp.max(shares, axis=0)
    return top + jnp.log(jnp.sum(jnp.exp(shares - top[None]), axis=0))


def pick_kernel(teacher_ref, student_ref, order_ref, count_ref, sent_ref, late_ref, picked_ref):
    patches, width = teacher_ref.shape
    order = jnp.broadcast_to(order_ref[:, :LANES], (patches, LANES))
    chosen = (iota((patches, LANES), 0) == order).astype(BF16)
    dims = (((0,), (0,)), ((), ()))
    teacher = lax.dot_general(chosen, teacher_ref[...], dims, preferred_element_type=F32)
    student = lax.dot_general(chosen, student_ref[...], dims, preferred_element_type=F32)
    teacher = jnp.where(iota((MOST, width), 0) < count_ref[0, 0], teacher[:MOST], UNUSED)
    sent_ref[...] = jnp.concatenate([student[:EARLY], teacher], axis=0).astype(BF16)
    late = student[EARLY:MOST]
    late_ref[...] = jnp.concatenate([late[:, :LANES], late[:, LANES:]], axis=0).astype(BF16)
    picked_ref[...] = student[:SLOT].astype(BF16)


def compact(gathered, starts, counts, rows, first, length, shift):
    images, slots, width = gathered.shape
    total = images * slots
    lane, image = iota((images, total), 1), iota((images, total), 0)
    within = lane - image * slots - first
    member = jnp.logical_and(within >= 0, within < length)
    place = (within + shift).astype(F32)
    used = jnp.logical_and(member, place < counts[:, :1])
    row = jnp.sum(jnp.where(used, starts[:, :1] + place + 1.0, 0.0), axis=0, keepdims=True) - 1.0
    chosen = (iota((rows, total), 0).astype(F32) == row).astype(BF16)
    return jnp.dot(chosen, gathered.reshape(total, width), preferred_element_type=F32)


def spread(starts, counts, slots, rows):
    images = starts.shape[0]
    shape = (images, slots, rows)
    within = iota(shape, 1)
    row = (iota(shape, 2) - within).astype(F32) - starts[:, :1].reshape(images, 1, 1)
    used = jnp.logical_and(row == 0.0, within.astype(F32) < counts[:, :1].reshape(images, 1, 1))
    return used.astype(F32).astype(BF16).reshape(images * slots, rows)


def column_kernel(gathered_ref, index_ref, far_ref, share_ref, rows_ref, places_ref, near_ref, sems):
    block, blocks = fetch(far_ref, near_ref, sems)
    images = gathered_ref.shape[0]
    teacher = gathered_ref[:, EARLY:]
    counts = jnp.sum((teacher[:, :, :LANES].astype(F32) < UNUSED / 2).astype(F32), axis=1)
    before = (iota((images, images), 1) < iota((images, images), 0)).astype(BF16)
    starts = jnp.dot(before, counts.astype(BF16), preferred_element_type=F32)
    half, core = images // 2, index_ref[0, 0] % 2
    place = iota((images, images), 0)
    image = jnp.where(place < half, 2 * place + core, 2 * (place - half) + 1 - core)
    other = iota((images, images), 1)
    places_ref[0] = jnp.dot((other < image).astype(BF16), counts.astype(BF16), preferred_element_type=F32)
    places_ref[1] = jnp.dot((other == image).astype(BF16), counts.astype(BF16), preferred_element_type=F32)
    places_ref[2] = starts
    places_ref[3] = counts
    rows = compact(teacher, starts, counts, rows_ref.shape[0], 0, MOST, 0).astype(BF16)
    rows_ref[...] = rows
    for b in blocks:
        logits = jnp.dot(rows, block(b), preferred_element_type=F32) * TEACH
        high = jnp.max(logits, axis=0, keepdims=True)
        total = jnp.sum(jnp.exp(logits - high), axis=0, keepdims=True)
        lines = to_lines(high + jnp.log(total))
        share_ref[:, lines_of(b)] = jnp.broadcast_to(lines[None], (share_ref.shape[0],) + lines.shape)


def split(values, parts):
    out = []
    for _ in range(parts):
        part = values.astype(BF16)
        out.append(part)
        values = values - part.astype(F32)
    return out


def fill_share(share_ref, lines):
    blank = jnp.zeros((share_ref.shape[1] - lines.shape[0], LANES), F32)
    share_ref[...] = jnp.broadcast_to(jnp.concatenate([lines, blank], axis=0)[None], share_ref.shape)


def row_kernel(shares_ref, rows_ref, protos_ref, late_ref, matrix_ref, high_ref, share_ref):
    column = merged(shares_ref[...])
    rows = rows_ref[...]
    highs, sums = [], []
    for b in range(high_ref.shape[0]):
        logits = jnp.dot(rows, protos_ref[:, columns(b)], preferred_element_type=F32) * TEACH
        shifted = logits - to_row(column[lines_of(b)])
        high = jnp.max(shifted, axis=1, keepdims=True)
        exact = jnp.exp(shifted - high)
        matrix_ref[:, columns(b)] = exact.astype(BF16)
        high_ref[b] = high
        highs.append(high)
        sums.append(jnp.sum(exact, axis=1, keepdims=True))
    top = functools.reduce(jnp.maximum, highs)
    total = sum(jnp.exp(high - top) * part for high, part in zip(highs, sums))
    own = jnp.concatenate([part.astype(F32) for part in split(to_lanes(top + jnp.log(total)), 3)], axis=0)
    blank = jnp.zeros((share_ref.shape[1] - 2 * LATE - own.shape[0], LANES), F32)
    chunk = jnp.concatenate([late_ref[...].astype(F32), own, blank], axis=0).astype(BF16)
    share_ref[...] = jnp.broadcast_to(chunk[None], share_ref.shape)


def column_sums(matrix_ref, scale, share_ref):
    for b in range(scale.shape[0]):
        sums = jnp.sum(matrix_ref[:, columns(b)].astype(F32) * scale[b], axis=0, keepdims=True)
        lines = to_lines(sums)
        shape = (share_ref.shape[0],) + lines.shape
        share_ref[:, lines_of(b)] = jnp.broadcast_to(lines[None], shape).astype(share_ref.dtype)


def first_column_kernel(shares_ref, high_ref, matrix_ref, share_ref, scale_ref):
    lines = scale_ref.shape[1] // LANES
    numbers = shares_ref[:, 2 * LATE :].astype(F32)
    row_lse = merged(sum(numbers[:, k * lines : (k + 1) * lines] for k in range(3)))
    scale = jnp.exp(high_ref[...] - to_column(row_lse)[None])
    scale_ref[...] = scale
    column_sums(matrix_ref, scale, share_ref)


def later_column_kernel(shares_ref, scale_in_ref, matrix_ref, share_ref, scale_ref):
    lines = scale_in_ref.shape[1] // LANES
    total = to_column(jnp.sum(shares_ref[...][:, :lines], axis=0))
    scale = scale_in_ref[...] / total[None]
    for b in range(scale.shape[0]):
        scale_ref[b] = to_lanes(scale[b])
    column_sums(matrix_ref, scale, share_ref)


def inverse_of(shares_ref):
    return 1.0 / jnp.sum(shares_ref[...].astype(F32), axis=0)


def later_row_kernel(shares_ref, scale_ref, matrix_ref, share_ref):
    inverse = inverse_of(shares_ref)
    sums = 0.0
    for b in range(scale_ref.shape[0]):
        scaled = matrix_ref[:, columns(b)].astype(F32) * to_row(inverse[lines_of(b)])
        sums += scale_ref[b] * jnp.sum(scaled, axis=1, keepdims=True)
    fill_share(share_ref, to_lanes(sums))


def pack(sums, numbers, parts, starts, counts):
    rows, width = sums.shape
    images = starts.shape[0]
    chosen = spread(starts, counts, SLOT, rows)
    packed = jnp.dot(chosen, sums.astype(BF16), preferred_element_type=F32).astype(BF16)
    row = split(to_row(to_lanes(numbers)), parts)
    row = jnp.concatenate([part.astype(F32) for part in row] + [jnp.zeros((SLOT - MOST - parts, rows), F32)], axis=0)
    tail = lax.dot_general(row.astype(BF16), chosen, (((1,), (1,)), ((), ())), preferred_element_type=F32)
    tail = jnp.concatenate([tail, jnp.zeros((SLOT - MOST, LANES), F32)], axis=1)
    blank = jnp.zeros((SLOT - MOST, width - LANES), F32)
    tail = [jnp.concatenate([tail[:, j * SLOT : j * SLOT + LANES], blank], axis=1)[None] for j in range(images)]
    return packed.reshape(images, SLOT, width)[:, :MOST], jnp.concatenate(tail, axis=0).astype(BF16)


def join(tail, width):
    images = tail[0].shape[0]
    filler = jnp.zeros((images, 1, width - LANES), F32)
    rows = [jnp.concatenate([part.astype(F32), filler], axis=2) for part in tail]
    rows.append(jnp.zeros((images, SLOT - MOST - len(tail), width), F32))
    return jnp.concatenate(rows, axis=1).astype(BF16)


def numbers_of(chunk, parts):
    tail = chunk[:, MOST:SLOT, :LANES].astype(F32)
    return sum(tail[:, k] for k in range(parts))


def put(own_ref, other_ref, rows, tail):
    half = own_ref.shape[0]
    own_ref[:, :MOST], own_ref[:, MOST:] = rows[:half], tail[:half]
    other_ref[:, :MOST], other_ref[:, MOST:] = rows[half:], tail[half:]


def slots_of(lanes):
    images = lanes.shape[0]
    same = iota((1, MOST, LANES), 1) == iota((1, MOST, LANES), 2)
    return jnp.sum(jnp.where(same, lanes.reshape(images, 1, LANES), 0.0), axis=2, keepdims=True)


def target_kernel(shares_ref, scale_ref, matrix_ref, protos_ref, places_ref, own_ref, other_ref, sums, total):
    step = pl.program_id(0)
    scale = to_column(scale_ref[step])
    weights = (matrix_ref[...].astype(F32) * to_row(inverse_of(shares_ref))).astype(BF16)
    part = scale * lax.dot_general(weights, protos_ref[...], (((1,), (1,)), ((), ())), preferred_element_type=F32)
    mass = scale * jnp.sum(weights.astype(F32), axis=1, keepdims=True)

    @pl.when(step == 0)
    def _():
        sums[...] = part
        total[...] = mass

    @pl.when(step > 0)
    def _():
        sums[...] += part
        total[...] += mass

    @pl.when(step == pl.num_programs(0) - 1)
    def _():
        put(own_ref, other_ref, *pack(sums[...], total[...], 2, places_ref[0], places_ref[1]))


def merge_kernel(own_ref, came_ref, student_own_ref, student_came_ref, out_ref):
    width = own_ref.shape[2]
    out_ref[:, :MOST] = (own_ref[:, :MOST].astype(F32) + came_ref[:, :MOST].astype(F32)).astype(BF16)
    total = numbers_of(own_ref, 2) + numbers_of(came_ref, 2)
    own, came = numbers_of(student_own_ref, 3), numbers_of(student_came_ref, 3)
    high = jnp.maximum(own, came)
    joint = high + jnp.log(jnp.exp(own - high) + jnp.exp(came - high))
    mean = student_own_ref[:, :MOST].astype(F32) * slots_of(jnp.exp(own - joint))
    mean = mean + student_came_ref[:, :MOST].astype(F32) * slots_of(jnp.exp(came - joint))
    out_ref[:, MOST : 2 * MOST] = mean.astype(BF16)
    out_ref[:, 2 * MOST :] = join([part[:, None] for part in split(total, 2) + split(joint, 3)], width)


def student_kernel(
    gathered_ref, shares_ref, places_ref, protos_ref, own_ref, other_ref, rows_ref, sums, top, total
):
    step = pl.program_id(0)

    @pl.when(step == 0)
    def _():
        starts, counts, rows = places_ref[2], places_ref[3], rows_ref.shape[0]
        late = jnp.concatenate([shares_ref[:, :LATE], shares_ref[:, LATE : 2 * LATE]], axis=2)
        found = compact(gathered_ref[...], starts, counts, rows, 0, EARLY, 0)
        found += compact(late, starts, counts, rows, 0, LATE, EARLY)
        rows_ref[...] = found.astype(BF16)
        top[...] = jnp.full(top.shape, -1e30, F32)
        total[...] = jnp.zeros(total.shape, F32)
        sums[...] = jnp.zeros(sums.shape, F32)

    protos = protos_ref[...]
    logits = jnp.dot(rows_ref[...], protos, preferred_element_type=F32) * STUD
    before = top[...]
    high = jnp.maximum(before, jnp.max(logits, axis=1, keepdims=True))
    shrink = jnp.exp(before - high)
    exact = jnp.exp(logits - high)
    total[...] = total[...] * shrink + jnp.sum(exact, axis=1, keepdims=True)
    part = lax.dot_general(exact.astype(BF16), protos, (((1,), (1,)), ((), ())), preferred_element_type=F32)
    sums[...] = sums[...] * shrink + part
    top[...] = high

    @pl.when(step == pl.num_programs(0) - 1)
    def _():
        mean, own_lse = sums[...] / total[...], top[...] + jnp.log(total[...])
        put(own_ref, other_ref, *pack(mean, own_lse, 3, places_ref[0], places_ref[1]))


def blend(chunk, lse):
    joint = merged(lse)
    weights = slots_of(jnp.exp(lse - joint[None]))
    return jnp.sum(chunk * weights, axis=0), joint


def finish_kernel(back_ref, picked_ref, order_ref, count_ref, grad_ref, loss_ref):
    patches, width = grad_ref.shape
    target = jnp.sum(back_ref[:, :MOST].astype(F32), axis=0)
    tail = back_ref[:, 2 * MOST :, :LANES].astype(F32)
    mass = to_column(jnp.sum(tail[:, 0] + tail[:, 1], axis=0, keepdims=True))[:MOST]
    soft, lse_lanes = blend(back_ref[:, MOST : 2 * MOST].astype(F32), tail[:, 2] + tail[:, 3] + tail[:, 4])
    used = iota((MOST, 1), 0) < count_ref[0, 0]
    mean = target / jnp.where(used, mass, 1.0)
    own_lse = to_column(lse_lanes.reshape(1, LANES))[:MOST]
    cross = own_lse - STUD * jnp.sum(picked_ref[:MOST].astype(F32) * mean, axis=1, keepdims=True)
    cross = jnp.sum(jnp.where(used, cross, 0.0), axis=0, keepdims=True)
    loss_ref[...] = cross / jnp.full((1, 1), count_ref[0, 0], jnp.int32).astype(F32)
    rows = jnp.where(used, STUD * (soft - mean), 0.0)
    rows = jnp.concatenate([rows, jnp.zeros((LANES - MOST, width), F32)], axis=0).astype(BF16)
    order = jnp.broadcast_to(order_ref[:, :LANES], (patches, LANES))
    chosen = (iota((patches, LANES), 0) == order).astype(BF16)
    grad_ref[...] = jnp.dot(chosen, rows, preferred_element_type=F32).astype(BF16)


def body(student_patches, teacher_patches, mask_order, counts, student_protos, teacher_protos):
    width = lax.axis_size("proto")
    groups = lax.axis_size("dp")
    rows = MASK_DEV * width
    lines = rows // LANES
    patches, bot = student_patches.shape[1:]
    protos = student_protos.shape[1]
    steps = protos // BLOCK
    depth = 8
    index = lax.axis_index("proto").astype(jnp.int32).reshape(1, 1)
    over = functools.partial(lax.all_to_all, split_axis=0, concat_axis=0, tiled=True)
    near = ((bot, protos), BF16)
    grid = (steps,)
    wide = pl.BlockSpec((bot, BLOCK), lambda k: (0, k))
    peer = pl.BlockSpec((groups, BLOCK // LANES, LANES), lambda k: (0, k, 0))
    square = pl.BlockSpec((rows, BLOCK), lambda k: (0, k))
    column = pltpu.VMEM((rows, 1), F32)
    sems = [pltpu.SemaphoreType.DMA((protos // PIECE,))]
    far = functools.partial(pltpu.with_memory_space_constraint, memory_space=pltpu.HBM)
    student_patches, teacher_patches, mask_order = far(student_patches[0]), far(teacher_patches[0]), far(mask_order)
    student_protos, teacher_protos = far(student_protos), far(teacher_protos)
    dot = 2 * rows * protos * bot

    sent, late, picked = call(
        pick_kernel,
        [((EARLY + MOST, bot), BF16), ((2 * LATE, LANES), BF16), pltpu.HBM((SLOT, bot), BF16)],
        teacher_patches,
        student_patches,
        mask_order,
        counts,
        in_specs=[VMEM, VMEM, VMEM, SMEM],
        moved=4 * patches * bot,
    )
    gathered = lax.all_gather(sent, "proto", axis=0, tiled=False)
    share, teacher_rows, places, near_teacher = call(
        column_kernel,
        [((groups, protos // LANES, LANES), F32), ((rows, bot), BF16), pltpu.HBM((4, width, LANES), F32), near],
        gathered,
        index,
        teacher_protos,
        in_specs=[VMEM, SMEM, HBM],
        scratch=sems,
        flops=dot,
        moved=2 * bot * protos,
    )
    shares = over(share, "dp")
    matrix, high, share = call(
        row_kernel,
        [((rows, protos), BF16), ((steps, rows, 1), F32), ((width, 2 * LATE + 16, LANES), BF16)],
        shares,
        teacher_rows,
        near_teacher,
        late,
        flops=dot,
        moved=2 * bot * protos + 2 * rows * protos,
    )
    swap = [(p, p ^ 1) for p in range(width)]
    shares = row_shares = over(share, "proto")
    share, scale = call(
        first_column_kernel,
        [
            ((groups, protos // LANES, LANES), BF16),
            ((steps, rows, 1), F32),
        ],
        shares,
        high,
        matrix,
        moved=2 * rows * protos,
    )
    shares = over(share, "dp")
    share = call(
        later_row_kernel,
        [((width, depth, LANES), F32)],
        shares,
        scale,
        matrix,
        moved=2 * rows * protos,
    )[0]
    shares = over(share, "proto")
    share, scale = call(
        later_column_kernel,
        [pltpu.HBM((groups, protos // LANES, LANES), BF16), pltpu.HBM((steps, rows // LANES, LANES), F32)],
        shares,
        scale,
        matrix,
        moved=2 * rows * protos,
    )
    packed = ((width // 2, SLOT, bot), BF16)
    student_own, student_other = call(
        student_kernel,
        [pltpu.HBM(*packed), pltpu.HBM(*packed)],
        far(gathered),
        far(row_shares),
        far(places),
        student_protos,
        grid=grid,
        in_specs=[pl.BlockSpec((width, EARLY, bot), lambda k: (0, 0, 0)), VMEM, VMEM, wide],
        scratch=[pltpu.VMEM((rows, bot), BF16), pltpu.VMEM((rows, bot), F32), column, column],
        flops=2 * dot,
        moved=2 * bot * protos,
    )
    student_came = lax.ppermute(student_other, "proto", swap)
    shares = over(share, "dp")
    shares, student_came = lax.optimization_barrier((shares, student_came))
    own, other = call(
        target_kernel,
        [packed, packed],
        shares,
        far(scale),
        matrix,
        student_protos,
        far(places),
        grid=grid,
        in_specs=[peer, VMEM, square, wide, VMEM],
        scratch=[pltpu.VMEM((rows, bot), F32), column],
        flops=dot,
        moved=2 * rows * protos,
    )
    came = lax.ppermute(other, "proto", swap)
    sent = call(
        merge_kernel, [((width // 2, MOST + SLOT, bot), BF16)], own, came, student_own, student_came
    )[0]
    same_core = [list(range(core, width, 2)) for core in range(2)]
    back = over(sent, "proto", axis_index_groups=same_core)
    student_grad, image_loss = call(
        finish_kernel,
        [((patches, bot), BF16), ((1, 1), F32)],
        back,
        picked,
        mask_order,
        counts,
        in_specs=[VMEM, VMEM, VMEM, SMEM],
        moved=2 * patches * bot,
    )
    return (student_grad[None], image_loss)


def solution(mesh):
    placed = (
        P(("dp", "proto"), None, None),
        P(("dp", "proto"), None, None),
        P(("dp", "proto"), None),
        P("dp", "proto"),
        P(None, "proto"),
        P(None, "proto"),
    )
    return jax.shard_map(
        body,
        mesh=mesh,
        in_specs=placed,
        out_specs=(P(("dp", "proto"), None, None), P("dp", "proto")),
        check_vma=False,
    )
```

```python
import functools

import jax
import jax.numpy as jnp
from jax import lax
from jax.experimental import pallas as pl
from jax.experimental.pallas import tpu as pltpu
from jax.sharding import PartitionSpec as P

MASK_DEV = 24
MOST = 72
EARLY = 54
LATE = MOST - EARLY
UNUSED = 100.0
SLOT = 80
TEACH = 1.0 / 0.07
STUD = 1.0 / 0.1
LOG2E = 1.4426950408889634
F32 = jnp.float32
BF16 = jnp.bfloat16
LANES = 128
BLOCK = 2048
PIECE = 1024
LIMIT = 24 << 20
VMEM = pl.BlockSpec(memory_space=pltpu.VMEM)
SMEM = pl.BlockSpec(memory_space=pltpu.SMEM)


HBM = pl.BlockSpec(memory_space=pl.ANY)


def call(kernel, out_shape, *args, in_specs=None, scratch=(), grid=None, flops=0, moved=0):
    out_shape = [jax.ShapeDtypeStruct(*o) if isinstance(o, tuple) else o for o in out_shape]
    extra = {} if grid is None else {"grid": grid}
    return pl.pallas_call(
        kernel,
        out_shape=out_shape,
        in_specs=[VMEM] * len(args) if in_specs is None else in_specs,
        out_specs=[VMEM] * len(out_shape),
        scratch_shapes=list(scratch),
        compiler_params=pltpu.CompilerParams(vmem_limit_bytes=LIMIT),
        cost_estimate=pl.CostEstimate(flops=flops, bytes_accessed=moved, transcendentals=0),
        **extra,
    )(*args)


def fetch(far_ref, near_ref, sems):
    copies = []
    for k in range(near_ref.shape[1] // PIECE):
        piece = slice(k * PIECE, (k + 1) * PIECE)
        copies.append(pltpu.make_async_copy(far_ref.at[:, piece], near_ref.at[:, piece], sems.at[k]))
        copies[-1].start()

    def block(b):
        for copy in copies[b * BLOCK // PIECE : (b + 1) * BLOCK // PIECE]:
            copy.wait()
        return near_ref[:, b * BLOCK : (b + 1) * BLOCK]

    return block, range(near_ref.shape[1] // BLOCK)


def columns(b):
    return slice(b * BLOCK, (b + 1) * BLOCK)


def lines_of(b):
    return slice(b * BLOCK // LANES, (b + 1) * BLOCK // LANES)


def iota(shape, dim):
    return lax.broadcasted_iota(jnp.int32, shape, dim)


def eye():
    return iota((LANES, LANES), 0) == iota((LANES, LANES), 1)


def to_lanes(column):
    parts = []
    for b in range(column.shape[0] // LANES):
        part = jnp.broadcast_to(column[b * LANES : (b + 1) * LANES], (LANES, LANES))
        parts.append(jnp.sum(jnp.where(eye(), part, 0.0), axis=0, keepdims=True))
    return jnp.concatenate(parts, axis=0)


def to_column(lanes):
    parts = []
    for b in range(lanes.shape[0]):
        part = jnp.broadcast_to(lanes[b : b + 1], (LANES, LANES))
        parts.append(jnp.sum(jnp.where(eye(), part, 0.0), axis=1, keepdims=True))
    return jnp.concatenate(parts, axis=0)


def to_lines(row):
    return jnp.concatenate([row[:, b * LANES : (b + 1) * LANES] for b in range(row.shape[1] // LANES)], axis=0)


def to_row(lines):
    return jnp.concatenate([lines[b : b + 1] for b in range(lines.shape[0])], axis=1)


def merged(shares):
    top = jnp.max(shares, axis=0)
    return top + jnp.log(jnp.sum(jnp.exp(shares - top[None]), axis=0))


def pick_kernel(teacher_ref, student_ref, order_ref, count_ref, sent_ref, late_ref, picked_ref):
    patches, width = teacher_ref.shape
    order = jnp.broadcast_to(order_ref[:, :LANES], (patches, LANES))
    chosen = (iota((patches, LANES), 0) == order).astype(BF16)
    dims = (((0,), (0,)), ((), ()))
    teacher = lax.dot_general(chosen, teacher_ref[...], dims, preferred_element_type=F32)
    student = lax.dot_general(chosen, student_ref[...], dims, preferred_element_type=F32)
    teacher = jnp.where(iota((MOST, width), 0) < count_ref[0, 0], teacher[:MOST], UNUSED)
    sent_ref[...] = jnp.concatenate([teacher, student[:EARLY]], axis=0).astype(BF16)
    late = student[EARLY:MOST]
    late_ref[...] = jnp.concatenate([late[:, :LANES], late[:, LANES:]], axis=0).astype(BF16)
    picked_ref[...] = student[:SLOT].astype(BF16)


def compact(gathered, starts, counts, rows, first, length, shift):
    images, slots, width = gathered.shape
    total = images * slots
    lane, image = iota((images, total), 1), iota((images, total), 0)
    within = lane - image * slots - first
    member = jnp.logical_and(within >= 0, within < length)
    place = (within + shift).astype(F32)
    used = jnp.logical_and(member, place < counts[:, :1])
    row = jnp.sum(jnp.where(used, starts[:, :1] + place + 1.0, 0.0), axis=0, keepdims=True) - 1.0
    chosen = (iota((rows, total), 0).astype(F32) == row).astype(BF16)
    return jnp.dot(chosen, gathered.reshape(total, width), preferred_element_type=F32)


def padded(values):
    images, slots, width = values.shape
    blank = jnp.zeros((images, -slots % 8, width), F32)
    return jnp.concatenate([values, blank], axis=1).astype(BF16)


def spread(starts, counts, slots, rows):
    images = starts.shape[0]
    shape = (images, slots, rows)
    within = iota(shape, 1)
    row = (iota(shape, 2) - within).astype(F32) - starts[:, :1].reshape(images, 1, 1)
    used = jnp.logical_and(row == 0.0, within.astype(F32) < counts[:, :1].reshape(images, 1, 1))
    return used.astype(F32).astype(BF16).reshape(images * slots, rows)


def column_kernel(gathered_ref, index_ref, far_ref, share_ref, rows_ref, places_ref, near_ref, sems):
    block, blocks = fetch(far_ref, near_ref, sems)
    images = gathered_ref.shape[0]
    teacher = gathered_ref[:, :MOST]
    counts = jnp.sum((teacher[:, :, :LANES].astype(F32) < UNUSED / 2).astype(F32), axis=1)
    before = (iota((images, images), 1) < iota((images, images), 0)).astype(BF16)
    starts = jnp.dot(before, counts.astype(BF16), preferred_element_type=F32)
    half, core = images // 2, index_ref[0, 0] % 2
    place = iota((images, images), 0)
    image = jnp.where(place < half, 2 * place + core, 2 * (place - half) + 1 - core)
    other = iota((images, images), 1)
    places_ref[0] = jnp.dot((other < image).astype(BF16), counts.astype(BF16), preferred_element_type=F32)
    places_ref[1] = jnp.dot((other == image).astype(BF16), counts.astype(BF16), preferred_element_type=F32)
    places_ref[2] = starts
    places_ref[3] = counts
    rows = compact(teacher, starts, counts, rows_ref.shape[0], 0, MOST, 0).astype(BF16)
    rows_ref[...] = rows
    for b in blocks:
        products = jnp.dot(rows, block(b), preferred_element_type=F32)
        high = jnp.max(products, axis=0, keepdims=True)
        total = jnp.sum(jnp.exp2((products - high) * (TEACH * LOG2E)), axis=0, keepdims=True)
        lines = to_lines(high * TEACH + jnp.log(total))
        share_ref[:, lines_of(b)] = jnp.broadcast_to(lines[None], (share_ref.shape[0],) + lines.shape)


def split(values, parts):
    out = []
    for _ in range(parts):
        part = values.astype(BF16)
        out.append(part)
        values = values - part.astype(F32)
    return out


def fill_share(share_ref, lines):
    blank = jnp.zeros((share_ref.shape[1] - lines.shape[0], LANES), F32)
    share_ref[...] = jnp.broadcast_to(jnp.concatenate([lines, blank], axis=0)[None], share_ref.shape)


def row_kernel(shares_ref, rows_ref, protos_ref, late_ref, matrix_ref, high_ref, share_ref):
    column = merged(shares_ref[...])
    rows = rows_ref[...]
    highs, sums = [], []
    for b in range(high_ref.shape[0]):
        products = jnp.dot(rows, protos_ref[:, columns(b)], preferred_element_type=F32)
        shifted = products * (TEACH * LOG2E) - to_row(column[lines_of(b)] * LOG2E)
        high = jnp.max(shifted, axis=1, keepdims=True)
        exact = jnp.exp2(shifted - high)
        high = high * (1.0 / LOG2E)
        matrix_ref[:, columns(b)] = exact.astype(BF16)
        high_ref[b] = high
        highs.append(high)
        sums.append(jnp.sum(exact, axis=1, keepdims=True))
    top = functools.reduce(jnp.maximum, highs)
    total = sum(jnp.exp(high - top) * part for high, part in zip(highs, sums))
    own = jnp.concatenate([part.astype(F32) for part in split(to_lanes(top + jnp.log(total)), 3)], axis=0)
    blank = jnp.zeros((share_ref.shape[1] - 2 * LATE - own.shape[0], LANES), F32)
    chunk = jnp.concatenate([late_ref[...].astype(F32), own, blank], axis=0).astype(BF16)
    share_ref[...] = jnp.broadcast_to(chunk[None], share_ref.shape)


def column_sums(matrix_ref, scale, share_ref):
    for b in range(scale.shape[0]):
        sums = jnp.sum(matrix_ref[:, columns(b)].astype(F32) * scale[b], axis=0, keepdims=True)
        lines = to_lines(sums)
        shape = (share_ref.shape[0],) + lines.shape
        share_ref[:, lines_of(b)] = jnp.broadcast_to(lines[None], shape).astype(share_ref.dtype)


def first_column_kernel(shares_ref, high_ref, matrix_ref, share_ref, scale_ref):
    lines = scale_ref.shape[1] // LANES
    numbers = shares_ref[...].astype(F32)[:, 2 * LATE :]
    row_lse = merged(sum(numbers[:, k * lines : (k + 1) * lines] for k in range(3)))
    scale = jnp.exp(high_ref[...] - to_column(row_lse)[None])
    scale_ref[...] = scale
    column_sums(matrix_ref, scale, share_ref)


def later_column_kernel(shares_ref, scale_in_ref, matrix_ref, share_ref, scale_ref):
    lines = scale_in_ref.shape[1] // LANES
    total = to_column(jnp.sum(shares_ref[...][:, :lines], axis=0))
    scale = scale_in_ref[...] / total[None]
    for b in range(scale.shape[0]):
        scale_ref[b] = to_lanes(scale[b])
    column_sums(matrix_ref, scale, share_ref)


def inverse_of(shares_ref):
    return 1.0 / jnp.sum(shares_ref[...].astype(F32), axis=0)


def later_row_kernel(shares_ref, scale_ref, matrix_ref, share_ref):
    inverse = inverse_of(shares_ref)
    sums = 0.0
    for b in range(scale_ref.shape[0]):
        scaled = matrix_ref[:, columns(b)].astype(F32) * to_row(inverse[lines_of(b)])
        sums += scale_ref[b] * jnp.sum(scaled, axis=1, keepdims=True)
    fill_share(share_ref, to_lanes(sums))


def pack(sums, numbers, parts, starts, counts):
    rows, width = sums.shape
    images = starts.shape[0]
    chosen = spread(starts, counts, SLOT, rows)
    packed = jnp.dot(chosen, sums.astype(BF16), preferred_element_type=F32).astype(BF16)
    row = split(to_row(to_lanes(numbers)), parts)
    row = jnp.concatenate([part.astype(F32) for part in row] + [jnp.zeros((SLOT - MOST - parts, rows), F32)], axis=0)
    tail = lax.dot_general(row.astype(BF16), chosen, (((1,), (1,)), ((), ())), preferred_element_type=F32)
    tail = jnp.concatenate([tail, jnp.zeros((SLOT - MOST, LANES), F32)], axis=1)
    blank = jnp.zeros((SLOT - MOST, width - LANES), F32)
    tail = [jnp.concatenate([tail[:, j * SLOT : j * SLOT + LANES], blank], axis=1)[None] for j in range(images)]
    return packed.reshape(images, SLOT, width)[:, :MOST], jnp.concatenate(tail, axis=0).astype(BF16)


def join(tail, width):
    images = tail[0].shape[0]
    filler = jnp.zeros((images, 1, width - LANES), F32)
    rows = [jnp.concatenate([part.astype(F32), filler], axis=2) for part in tail]
    rows.append(jnp.zeros((images, SLOT - MOST - len(tail), width), F32))
    return jnp.concatenate(rows, axis=1).astype(BF16)


def numbers_of(chunk, parts):
    tail = chunk[:, MOST:SLOT, :LANES].astype(F32)
    return sum(tail[:, k] for k in range(parts))


def put(own_ref, other_ref, rows, tail):
    half = own_ref.shape[0]
    own_ref[:, :MOST], own_ref[:, MOST:] = rows[:half], tail[:half]
    other_ref[:, :MOST], other_ref[:, MOST:] = rows[half:], tail[half:]


def slots_of(lanes):
    images = lanes.shape[0]
    same = iota((1, MOST, LANES), 1) == iota((1, MOST, LANES), 2)
    return jnp.sum(jnp.where(same, lanes.reshape(images, 1, LANES), 0.0), axis=2, keepdims=True)


def target_kernel(shares_ref, scale_ref, matrix_ref, protos_ref, places_ref, own_ref, other_ref, sums, total):
    step = pl.program_id(0)
    scale = to_column(scale_ref[step])
    weights = (matrix_ref[...].astype(F32) * to_row(inverse_of(shares_ref))).astype(BF16)
    part = scale * lax.dot_general(weights, protos_ref[...], (((1,), (1,)), ((), ())), preferred_element_type=F32)
    mass = scale * jnp.sum(weights.astype(F32), axis=1, keepdims=True)

    @pl.when(step == 0)
    def _():
        sums[...] = part
        total[...] = mass

    @pl.when(step > 0)
    def _():
        sums[...] += part
        total[...] += mass

    @pl.when(step == pl.num_programs(0) - 1)
    def _():
        put(own_ref, other_ref, *pack(sums[...], total[...], 2, places_ref[0], places_ref[1]))


def merge_kernel(own_ref, came_ref, student_own_ref, student_came_ref, out_ref):
    width = own_ref.shape[2]
    out_ref[:, :MOST] = (own_ref[:, :MOST].astype(F32) + came_ref[:, :MOST].astype(F32)).astype(BF16)
    total = numbers_of(own_ref, 2) + numbers_of(came_ref, 2)
    own, came = numbers_of(student_own_ref, 3), numbers_of(student_came_ref, 3)
    high = jnp.maximum(own, came)
    joint = high + jnp.log(jnp.exp(own - high) + jnp.exp(came - high))
    mean = student_own_ref[:, :MOST].astype(F32) * slots_of(jnp.exp(own - joint))
    mean = mean + student_came_ref[:, :MOST].astype(F32) * slots_of(jnp.exp(came - joint))
    out_ref[:, MOST : 2 * MOST] = mean.astype(BF16)
    out_ref[:, 2 * MOST :] = join([part[:, None] for part in split(total, 2) + split(joint, 3)], width)


def student_kernel(
    gathered_ref, shares_ref, places_ref, protos_ref, own_ref, other_ref, rows_ref, sums, top, total
):
    step = pl.program_id(0)

    @pl.when(step == 0)
    def _():
        starts, counts, rows = places_ref[2], places_ref[3], rows_ref.shape[0]
        late = shares_ref[...].astype(F32)
        late = jnp.concatenate([late[:, :LATE], late[:, LATE : 2 * LATE]], axis=2)
        early = gathered_ref[:, MOST:].astype(F32)
        found = compact(padded(early), starts, counts, rows, 0, EARLY, 0)
        found += compact(padded(late), starts, counts, rows, 0, LATE, EARLY)
        rows_ref[...] = found.astype(BF16)
        top[...] = jnp.full(top.shape, -1e30, F32)
        total[...] = jnp.zeros(total.shape, F32)
        sums[...] = jnp.zeros(sums.shape, F32)

    protos = protos_ref[...]
    products = jnp.dot(rows_ref[...], protos, preferred_element_type=F32)
    before = top[...]
    high = jnp.maximum(before, jnp.max(products, axis=1, keepdims=True))
    shrink = jnp.exp2((before - high) * (STUD * LOG2E))
    exact = jnp.exp2((products - high) * (STUD * LOG2E))
    total[...] = total[...] * shrink + jnp.sum(exact, axis=1, keepdims=True)
    part = lax.dot_general(exact.astype(BF16), protos, (((1,), (1,)), ((), ())), preferred_element_type=F32)
    sums[...] = sums[...] * shrink + part
    top[...] = high

    @pl.when(step == pl.num_programs(0) - 1)
    def _():
        mean, own_lse = sums[...] / total[...], top[...] * STUD + jnp.log(total[...])
        put(own_ref, other_ref, *pack(mean, own_lse, 3, places_ref[0], places_ref[1]))


def blend(chunk, lse):
    joint = merged(lse)
    weights = slots_of(jnp.exp(lse - joint[None]))
    return jnp.sum(chunk * weights, axis=0), joint


def finish_kernel(back_ref, picked_ref, order_ref, count_ref, grad_ref, loss_ref):
    patches, width = grad_ref.shape
    target = jnp.sum(back_ref[:, :MOST].astype(F32), axis=0)
    tail = back_ref[:, 2 * MOST :, :LANES].astype(F32)
    mass = to_column(jnp.sum(tail[:, 0] + tail[:, 1], axis=0, keepdims=True))[:MOST]
    soft, lse_lanes = blend(back_ref[:, MOST : 2 * MOST].astype(F32), tail[:, 2] + tail[:, 3] + tail[:, 4])
    used = iota((MOST, 1), 0) < count_ref[0, 0]
    mean = target / jnp.where(used, mass, 1.0)
    own_lse = to_column(lse_lanes.reshape(1, LANES))[:MOST]
    cross = own_lse - STUD * jnp.sum(picked_ref[:MOST].astype(F32) * mean, axis=1, keepdims=True)
    cross = jnp.sum(jnp.where(used, cross, 0.0), axis=0, keepdims=True)
    loss_ref[...] = cross / jnp.full((1, 1), count_ref[0, 0], jnp.int32).astype(F32)
    rows = jnp.where(used, STUD * (soft - mean), 0.0)
    rows = jnp.concatenate([rows, jnp.zeros((LANES - MOST, width), F32)], axis=0).astype(BF16)
    order = jnp.broadcast_to(order_ref[:, :LANES], (patches, LANES))
    chosen = (iota((patches, LANES), 0) == order).astype(BF16)
    grad_ref[...] = jnp.dot(chosen, rows, preferred_element_type=F32).astype(BF16)


def body(student_patches, teacher_patches, mask_order, counts, student_protos, teacher_protos):
    width = lax.axis_size("proto")
    groups = lax.axis_size("dp")
    rows = MASK_DEV * width
    lines = rows // LANES
    patches, bot = student_patches.shape[1:]
    protos = student_protos.shape[1]
    steps = protos // BLOCK
    depth = 8
    index = lax.axis_index("proto").astype(jnp.int32).reshape(1, 1)
    over = functools.partial(lax.all_to_all, split_axis=0, concat_axis=0, tiled=True)
    near = ((bot, protos), BF16)
    grid = (steps,)
    wide = pl.BlockSpec((bot, BLOCK), lambda k: (0, k))
    peer = pl.BlockSpec((groups, BLOCK // LANES, LANES), lambda k: (0, k, 0))
    square = pl.BlockSpec((rows, BLOCK), lambda k: (0, k))
    column = pltpu.VMEM((rows, 1), F32)
    sems = [pltpu.SemaphoreType.DMA((protos // PIECE,))]
    far = functools.partial(pltpu.with_memory_space_constraint, memory_space=pltpu.HBM)
    student_patches, teacher_patches, mask_order = far(student_patches[0]), far(teacher_patches[0]), far(mask_order)
    student_protos, teacher_protos = far(student_protos), far(teacher_protos)
    dot = 2 * rows * protos * bot

    sent, late, picked = call(
        pick_kernel,
        [((EARLY + MOST, bot), BF16), ((2 * LATE, LANES), BF16), pltpu.HBM((SLOT, bot), BF16)],
        teacher_patches,
        student_patches,
        mask_order,
        counts,
        in_specs=[VMEM, VMEM, VMEM, SMEM],
        moved=4 * patches * bot,
    )
    gathered = lax.all_gather(sent, "proto", axis=0, tiled=False)
    share, teacher_rows, places, near_teacher = call(
        column_kernel,
        [((groups, protos // LANES, LANES), F32), ((rows, bot), BF16), pltpu.HBM((4, width, LANES), F32), near],
        gathered,
        index,
        teacher_protos,
        in_specs=[VMEM, SMEM, HBM],
        scratch=sems,
        flops=dot,
        moved=2 * bot * protos,
    )
    shares = over(share, "dp")
    matrix, high, share = call(
        row_kernel,
        [((rows, protos), BF16), ((steps, rows, 1), F32), ((width, 48, LANES), BF16)],
        shares,
        teacher_rows,
        near_teacher,
        late,
        flops=dot,
        moved=2 * bot * protos + 2 * rows * protos,
    )
    swap = [(p, p ^ 1) for p in range(width)]
    shares = row_shares = over(share, "proto")
    share, scale = call(
        first_column_kernel,
        [
            ((groups, protos // LANES, LANES), BF16),
            ((steps, rows, 1), F32),
        ],
        shares,
        high,
        matrix,
        moved=2 * rows * protos,
    )
    shares = over(share, "dp")
    share = call(
        later_row_kernel,
        [((width, depth, LANES), F32)],
        shares,
        scale,
        matrix,
        moved=2 * rows * protos,
    )[0]
    shares = over(share, "proto")
    share, scale = call(
        later_column_kernel,
        [pltpu.HBM((groups, protos // LANES, LANES), BF16), pltpu.HBM((steps, rows // LANES, LANES), F32)],
        shares,
        scale,
        matrix,
        moved=2 * rows * protos,
    )
    packed = ((width // 2, SLOT, bot), BF16)
    student_own, student_other = call(
        student_kernel,
        [pltpu.HBM(*packed), pltpu.HBM(*packed)],
        far(gathered),
        far(row_shares),
        far(places),
        student_protos,
        grid=grid,
        in_specs=[VMEM, VMEM, VMEM, wide],
        scratch=[pltpu.VMEM((rows, bot), BF16), pltpu.VMEM((rows, bot), F32), column, column],
        flops=2 * dot,
        moved=2 * bot * protos,
    )
    student_came = lax.ppermute(student_other, "proto", swap)
    shares = over(share, "dp")
    shares, student_came = lax.optimization_barrier((shares, student_came))
    own, other = call(
        target_kernel,
        [packed, packed],
        shares,
        far(scale),
        matrix,
        student_protos,
        far(places),
        grid=grid,
        in_specs=[peer, VMEM, square, wide, VMEM],
        scratch=[pltpu.VMEM((rows, bot), F32), column],
        flops=dot,
        moved=2 * rows * protos,
    )
    came = lax.ppermute(other, "proto", swap)
    sent = call(
        merge_kernel, [((width // 2, MOST + SLOT, bot), BF16)], own, came, student_own, student_came
    )[0]
    same_core = [list(range(core, width, 2)) for core in range(2)]
    back = over(sent, "proto", axis_index_groups=same_core)
    student_grad, image_loss = call(
        finish_kernel,
        [((patches, bot), BF16), ((1, 1), F32)],
        back,
        picked,
        mask_order,
        counts,
        in_specs=[VMEM, VMEM, VMEM, SMEM],
        moved=2 * patches * bot,
    )
    return (student_grad[None], image_loss)


def solution(mesh):
    placed = (
        P(("dp", "proto"), None, None),
        P(("dp", "proto"), None, None),
        P(("dp", "proto"), None),
        P("dp", "proto"),
        P(None, "proto"),
        P(None, "proto"),
    )
    return jax.shard_map(
        body,
        mesh=mesh,
        in_specs=placed,
        out_specs=(P(("dp", "proto"), None, None), P("dp", "proto")),
        check_vma=False,
    )
```

```python
import functools

import jax
import jax.numpy as jnp
from jax import lax
from jax.experimental import pallas as pl
from jax.experimental.pallas import tpu as pltpu
from jax.sharding import PartitionSpec as P

MASK_DEV = 24
MOST = 72
EARLY = 54
LATE = MOST - EARLY
UNUSED = 100.0
SLOT = 80
TEACH = 1.0 / 0.07
STUD = 1.0 / 0.1
LOG2E = 1.4426950408889634
F32 = jnp.float32
BF16 = jnp.bfloat16
LANES = 128
BLOCK = 2048
PIECE = 1024
LIMIT = 24 << 20
VMEM = pl.BlockSpec(memory_space=pltpu.VMEM)
SMEM = pl.BlockSpec(memory_space=pltpu.SMEM)


HBM = pl.BlockSpec(memory_space=pl.ANY)


def call(kernel, out_shape, *args, in_specs=None, scratch=(), grid=None, flops=0, moved=0):
    out_shape = [jax.ShapeDtypeStruct(*o) if isinstance(o, tuple) else o for o in out_shape]
    extra = {} if grid is None else {"grid": grid}
    return pl.pallas_call(
        kernel,
        out_shape=out_shape,
        in_specs=[VMEM] * len(args) if in_specs is None else in_specs,
        out_specs=[VMEM] * len(out_shape),
        scratch_shapes=list(scratch),
        compiler_params=pltpu.CompilerParams(vmem_limit_bytes=LIMIT),
        cost_estimate=pl.CostEstimate(flops=flops, bytes_accessed=moved, transcendentals=0),
        **extra,
    )(*args)


def fetch(far_ref, near_ref, sems):
    copies = []
    for k in range(near_ref.shape[1] // PIECE):
        piece = slice(k * PIECE, (k + 1) * PIECE)
        copies.append(pltpu.make_async_copy(far_ref.at[:, piece], near_ref.at[:, piece], sems.at[k]))
        copies[-1].start()

    def block(b):
        for copy in copies[b * BLOCK // PIECE : (b + 1) * BLOCK // PIECE]:
            copy.wait()
        return near_ref[:, b * BLOCK : (b + 1) * BLOCK]

    return block, range(near_ref.shape[1] // BLOCK)


def columns(b):
    return slice(b * BLOCK, (b + 1) * BLOCK)


def lines_of(b):
    return slice(b * BLOCK // LANES, (b + 1) * BLOCK // LANES)


def iota(shape, dim):
    return lax.broadcasted_iota(jnp.int32, shape, dim)


def eye():
    return iota((LANES, LANES), 0) == iota((LANES, LANES), 1)


def to_lanes(column):
    parts = []
    for b in range(column.shape[0] // LANES):
        part = jnp.broadcast_to(column[b * LANES : (b + 1) * LANES], (LANES, LANES))
        parts.append(jnp.sum(jnp.where(eye(), part, 0.0), axis=0, keepdims=True))
    return jnp.concatenate(parts, axis=0)


def to_column(lanes):
    parts = []
    for b in range(lanes.shape[0]):
        part = jnp.broadcast_to(lanes[b : b + 1], (LANES, LANES))
        parts.append(jnp.sum(jnp.where(eye(), part, 0.0), axis=1, keepdims=True))
    return jnp.concatenate(parts, axis=0)


def to_lines(row):
    return jnp.concatenate([row[:, b * LANES : (b + 1) * LANES] for b in range(row.shape[1] // LANES)], axis=0)


def to_row(lines):
    return jnp.concatenate([lines[b : b + 1] for b in range(lines.shape[0])], axis=1)


def merged(shares):
    top = jnp.max(shares, axis=0)
    return top + jnp.log(jnp.sum(jnp.exp(shares - top[None]), axis=0))


def pick_kernel(teacher_ref, student_ref, order_ref, count_ref, sent_ref, late_ref, picked_ref):
    patches, width = teacher_ref.shape
    order = jnp.broadcast_to(order_ref[:, :LANES], (patches, LANES))
    chosen = (iota((patches, LANES), 0) == order).astype(BF16)
    dims = (((0,), (0,)), ((), ()))
    teacher = lax.dot_general(chosen, teacher_ref[...], dims, preferred_element_type=F32)
    student = lax.dot_general(chosen, student_ref[...], dims, preferred_element_type=F32)
    teacher = jnp.where(iota((MOST, width), 0) < count_ref[0, 0], teacher[:MOST], UNUSED)
    sent_ref[...] = jnp.concatenate([teacher, student[:EARLY]], axis=0).astype(BF16)
    late = student[EARLY:MOST]
    late_ref[...] = jnp.concatenate([late[:, :LANES], late[:, LANES:]], axis=0).astype(BF16)
    picked_ref[...] = student[:SLOT].astype(BF16)


def compact(gathered, starts, counts, rows, first, length, shift):
    images, slots, width = gathered.shape
    total = images * slots
    lane, image = iota((images, total), 1), iota((images, total), 0)
    within = lane - image * slots - first
    member = jnp.logical_and(within >= 0, within < length)
    place = (within + shift).astype(F32)
    used = jnp.logical_and(member, place < counts[:, :1])
    row = jnp.sum(jnp.where(used, starts[:, :1] + place + 1.0, 0.0), axis=0, keepdims=True) - 1.0
    chosen = (iota((rows, total), 0).astype(F32) == row).astype(BF16)
    return jnp.dot(chosen, gathered.reshape(total, width), preferred_element_type=F32)


def padded(values):
    images, slots, width = values.shape
    blank = jnp.zeros((images, -slots % 8, width), F32)
    return jnp.concatenate([values, blank], axis=1).astype(BF16)


def spread(starts, counts, slots, rows):
    images = starts.shape[0]
    shape = (images, slots, rows)
    within = iota(shape, 1)
    row = (iota(shape, 2) - within).astype(F32) - starts[:, :1].reshape(images, 1, 1)
    used = jnp.logical_and(row == 0.0, within.astype(F32) < counts[:, :1].reshape(images, 1, 1))
    return used.astype(F32).astype(BF16).reshape(images * slots, rows)


def column_kernel(gathered_ref, index_ref, far_ref, share_ref, rows_ref, places_ref, near_ref, sems):
    block, blocks = fetch(far_ref, near_ref, sems)
    images = gathered_ref.shape[0]
    teacher = gathered_ref[:, :MOST]
    counts = jnp.sum((teacher[:, :, :LANES].astype(F32) < UNUSED / 2).astype(F32), axis=1)
    before = (iota((images, images), 1) < iota((images, images), 0)).astype(BF16)
    starts = jnp.dot(before, counts.astype(BF16), preferred_element_type=F32)
    half, core = images // 2, index_ref[0, 0] % 2
    place = iota((images, images), 0)
    image = jnp.where(place < half, 2 * place + core, 2 * (place - half) + 1 - core)
    other = iota((images, images), 1)
    places_ref[0] = jnp.dot((other < image).astype(BF16), counts.astype(BF16), preferred_element_type=F32)
    places_ref[1] = jnp.dot((other == image).astype(BF16), counts.astype(BF16), preferred_element_type=F32)
    places_ref[2] = starts
    places_ref[3] = counts
    rows = compact(teacher, starts, counts, rows_ref.shape[0], 0, MOST, 0).astype(BF16)
    rows_ref[...] = rows
    for b in blocks:
        products = jnp.dot(rows, block(b), preferred_element_type=F32)
        high = jnp.max(products, axis=0, keepdims=True)
        total = jnp.sum(jnp.exp2((products - high) * (TEACH * LOG2E)), axis=0, keepdims=True)
        lines = to_lines(high * TEACH + jnp.log(total))
        share_ref[:, lines_of(b)] = jnp.broadcast_to(lines[None], (share_ref.shape[0],) + lines.shape)


def split(values, parts):
    out = []
    for _ in range(parts):
        part = values.astype(BF16)
        out.append(part)
        values = values - part.astype(F32)
    return out


def fill_share(share_ref, lines):
    blank = jnp.zeros((share_ref.shape[1] - lines.shape[0], LANES), F32)
    share_ref[...] = jnp.broadcast_to(jnp.concatenate([lines, blank], axis=0)[None], share_ref.shape)


def row_kernel(shares_ref, rows_ref, protos_ref, late_ref, matrix_ref, high_ref, share_ref):
    column = merged(shares_ref[...])
    rows = rows_ref[...]
    highs, sums = [], []
    for b in range(high_ref.shape[0]):
        products = jnp.dot(rows, protos_ref[:, columns(b)], preferred_element_type=F32)
        shifted = products * (TEACH * LOG2E) - to_row(column[lines_of(b)] * LOG2E)
        high = jnp.max(shifted, axis=1, keepdims=True)
        exact = jnp.exp2(shifted - high)
        high = high * (1.0 / LOG2E)
        matrix_ref[:, columns(b)] = exact.astype(BF16)
        high_ref[b] = high
        highs.append(high)
        sums.append(jnp.sum(exact, axis=1, keepdims=True))
    top = functools.reduce(jnp.maximum, highs)
    total = sum(jnp.exp(high - top) * part for high, part in zip(highs, sums))
    own = jnp.concatenate([part.astype(F32) for part in split(to_lanes(top + jnp.log(total)), 3)], axis=0)
    blank = jnp.zeros((share_ref.shape[1] - 2 * LATE - own.shape[0], LANES), F32)
    chunk = jnp.concatenate([late_ref[...].astype(F32), own, blank], axis=0).astype(BF16)
    share_ref[...] = jnp.broadcast_to(chunk[None], share_ref.shape)


def column_sums(matrix_ref, scale, share_ref):
    for b in range(scale.shape[0]):
        sums = jnp.sum(matrix_ref[:, columns(b)].astype(F32) * scale[b], axis=0, keepdims=True)
        lines = to_lines(sums)
        shape = (share_ref.shape[0],) + lines.shape
        share_ref[:, lines_of(b)] = jnp.broadcast_to(lines[None], shape).astype(share_ref.dtype)


def first_column_kernel(shares_ref, high_ref, matrix_ref, share_ref, scale_ref):
    lines = scale_ref.shape[1] // LANES
    numbers = shares_ref[...].astype(F32)[:, 2 * LATE :]
    row_lse = merged(sum(numbers[:, k * lines : (k + 1) * lines] for k in range(3)))
    scale = jnp.exp(high_ref[...] - to_column(row_lse)[None])
    scale_ref[...] = scale
    column_sums(matrix_ref, scale, share_ref)


def later_column_kernel(shares_ref, scale_in_ref, matrix_ref, share_ref, scale_ref):
    lines = scale_in_ref.shape[1] // LANES
    total = to_column(jnp.sum(shares_ref[...][:, :lines], axis=0))
    scale = scale_in_ref[...] / total[None]
    for b in range(scale.shape[0]):
        scale_ref[b] = to_lanes(scale[b])
    column_sums(matrix_ref, scale, share_ref)


def inverse_of(shares_ref):
    return 1.0 / jnp.sum(shares_ref[...].astype(F32), axis=0)


def later_row_kernel(shares_ref, scale_ref, matrix_ref, share_ref):
    inverse = inverse_of(shares_ref)
    sums = 0.0
    for b in range(scale_ref.shape[0]):
        scaled = matrix_ref[:, columns(b)].astype(F32) * to_row(inverse[lines_of(b)])
        sums += scale_ref[b] * jnp.sum(scaled, axis=1, keepdims=True)
    fill_share(share_ref, to_lanes(sums))


def pack(sums, numbers, parts, starts, counts):
    rows, width = sums.shape
    images = starts.shape[0]
    chosen = spread(starts, counts, SLOT, rows)
    packed = jnp.dot(chosen, sums.astype(BF16), preferred_element_type=F32).astype(BF16)
    row = split(to_row(to_lanes(numbers)), parts)
    row = jnp.concatenate([part.astype(F32) for part in row] + [jnp.zeros((SLOT - MOST - parts, rows), F32)], axis=0)
    tail = lax.dot_general(row.astype(BF16), chosen, (((1,), (1,)), ((), ())), preferred_element_type=F32)
    tail = jnp.concatenate([tail, jnp.zeros((SLOT - MOST, LANES), F32)], axis=1)
    blank = jnp.zeros((SLOT - MOST, width - LANES), F32)
    tail = [jnp.concatenate([tail[:, j * SLOT : j * SLOT + LANES], blank], axis=1)[None] for j in range(images)]
    return packed.reshape(images, SLOT, width)[:, :MOST], jnp.concatenate(tail, axis=0).astype(BF16)


def join(tail, width):
    images = tail[0].shape[0]
    filler = jnp.zeros((images, 1, width - LANES), F32)
    rows = [jnp.concatenate([part.astype(F32), filler], axis=2) for part in tail]
    rows.append(jnp.zeros((images, SLOT - MOST - len(tail), width), F32))
    return jnp.concatenate(rows, axis=1).astype(BF16)


def numbers_of(chunk, parts):
    tail = chunk[:, MOST:SLOT, :LANES].astype(F32)
    return sum(tail[:, k] for k in range(parts))


def put(own_ref, other_ref, rows, tail):
    half = own_ref.shape[0]
    own_ref[:, :MOST], own_ref[:, MOST:] = rows[:half], tail[:half]
    other_ref[:, :MOST], other_ref[:, MOST:] = rows[half:], tail[half:]


def slots_of(lanes):
    images = lanes.shape[0]
    same = iota((1, MOST, LANES), 1) == iota((1, MOST, LANES), 2)
    return jnp.sum(jnp.where(same, lanes.reshape(images, 1, LANES), 0.0), axis=2, keepdims=True)


def target_kernel(shares_ref, scale_ref, matrix_ref, protos_ref, places_ref, own_ref, other_ref, sums, total):
    step = pl.program_id(0)
    scale = to_column(scale_ref[step])
    here = pl.ds(pl.multiple_of(step * BLOCK, BLOCK), BLOCK)
    weights = matrix_ref[:, here].astype(F32) * to_row(inverse_of(shares_ref))
    narrow = weights.astype(BF16)
    part = scale * lax.dot_general(narrow, protos_ref[...], (((1,), (1,)), ((), ())), preferred_element_type=F32)
    mass = scale * jnp.sum(weights, axis=1, keepdims=True)

    @pl.when(step == 0)
    def _():
        sums[...] = part
        total[...] = mass

    @pl.when(step > 0)
    def _():
        sums[...] += part
        total[...] += mass

    @pl.when(step == pl.num_programs(0) - 1)
    def _():
        put(own_ref, other_ref, *pack(sums[...], total[...], 2, places_ref[0], places_ref[1]))


def merge_kernel(own_ref, came_ref, student_own_ref, student_came_ref, out_ref):
    width = own_ref.shape[2]
    out_ref[:, :MOST] = (own_ref[:, :MOST].astype(F32) + came_ref[:, :MOST].astype(F32)).astype(BF16)
    total = numbers_of(own_ref, 2) + numbers_of(came_ref, 2)
    own, came = numbers_of(student_own_ref, 3), numbers_of(student_came_ref, 3)
    high = jnp.maximum(own, came)
    joint = high + jnp.log(jnp.exp(own - high) + jnp.exp(came - high))
    mean = student_own_ref[:, :MOST].astype(F32) * slots_of(jnp.exp(own - joint))
    mean = mean + student_came_ref[:, :MOST].astype(F32) * slots_of(jnp.exp(came - joint))
    out_ref[:, MOST : 2 * MOST] = mean.astype(BF16)
    out_ref[:, 2 * MOST :] = join([part[:, None] for part in split(total, 2) + split(joint, 3)], width)


def student_kernel(
    gathered_ref, shares_ref, places_ref, protos_ref, own_ref, other_ref, rows_ref, sums, top, total
):
    step = pl.program_id(0)

    @pl.when(step == 0)
    def _():
        starts, counts, rows = places_ref[2], places_ref[3], rows_ref.shape[0]
        late = shares_ref[...].astype(F32)
        late = jnp.concatenate([late[:, :LATE], late[:, LATE : 2 * LATE]], axis=2)
        early = gathered_ref[:, MOST:].astype(F32)
        found = compact(padded(early), starts, counts, rows, 0, EARLY, 0)
        found += compact(padded(late), starts, counts, rows, 0, LATE, EARLY)
        rows_ref[...] = found.astype(BF16)
        top[...] = jnp.full(top.shape, -1e30, F32)
        total[...] = jnp.zeros(total.shape, F32)
        sums[...] = jnp.zeros(sums.shape, F32)

    protos = protos_ref[...]
    products = jnp.dot(rows_ref[...], protos, preferred_element_type=F32)
    before = top[...]
    high = jnp.maximum(before, jnp.max(products, axis=1, keepdims=True))
    shrink = jnp.exp2((before - high) * (STUD * LOG2E))
    exact = jnp.exp2((products - high) * (STUD * LOG2E))
    total[...] = total[...] * shrink + jnp.sum(exact, axis=1, keepdims=True)
    part = lax.dot_general(exact.astype(BF16), protos, (((1,), (1,)), ((), ())), preferred_element_type=F32)
    sums[...] = sums[...] * shrink + part
    top[...] = high

    @pl.when(step == pl.num_programs(0) - 1)
    def _():
        mean, own_lse = sums[...] / total[...], top[...] * STUD + jnp.log(total[...])
        put(own_ref, other_ref, *pack(mean, own_lse, 3, places_ref[0], places_ref[1]))


def blend(chunk, lse):
    joint = merged(lse)
    weights = slots_of(jnp.exp(lse - joint[None]))
    return jnp.sum(chunk * weights, axis=0), joint


def finish_kernel(back_ref, picked_ref, order_ref, count_ref, grad_ref, loss_ref):
    patches, width = grad_ref.shape
    target = jnp.sum(back_ref[:, :MOST].astype(F32), axis=0)
    tail = back_ref[:, 2 * MOST :, :LANES].astype(F32)
    mass = to_column(jnp.sum(tail[:, 0] + tail[:, 1], axis=0, keepdims=True))[:MOST]
    soft, lse_lanes = blend(back_ref[:, MOST : 2 * MOST].astype(F32), tail[:, 2] + tail[:, 3] + tail[:, 4])
    used = iota((MOST, 1), 0) < count_ref[0, 0]
    mean = target / jnp.where(used, mass, 1.0)
    own_lse = to_column(lse_lanes.reshape(1, LANES))[:MOST]
    cross = own_lse - STUD * jnp.sum(picked_ref[:MOST].astype(F32) * mean, axis=1, keepdims=True)
    cross = jnp.sum(jnp.where(used, cross, 0.0), axis=0, keepdims=True)
    loss_ref[...] = cross / jnp.full((1, 1), count_ref[0, 0], jnp.int32).astype(F32)
    rows = jnp.where(used, STUD * (soft - mean), 0.0)
    rows = jnp.concatenate([rows, jnp.zeros((LANES - MOST, width), F32)], axis=0).astype(BF16)
    order = jnp.broadcast_to(order_ref[:, :LANES], (patches, LANES))
    chosen = (iota((patches, LANES), 0) == order).astype(BF16)
    grad_ref[...] = jnp.dot(chosen, rows, preferred_element_type=F32).astype(BF16)


def body(student_patches, teacher_patches, mask_order, counts, student_protos, teacher_protos):
    width = lax.axis_size("proto")
    groups = lax.axis_size("dp")
    rows = MASK_DEV * width
    lines = rows // LANES
    patches, bot = student_patches.shape[1:]
    protos = student_protos.shape[1]
    steps = protos // BLOCK
    depth = 8
    index = lax.axis_index("proto").astype(jnp.int32).reshape(1, 1)
    over = functools.partial(lax.all_to_all, split_axis=0, concat_axis=0, tiled=True)
    near = ((bot, protos), BF16)
    grid = (steps,)
    wide = pl.BlockSpec((bot, BLOCK), lambda k: (0, k))
    peer = pl.BlockSpec((groups, BLOCK // LANES, LANES), lambda k: (0, k, 0))
    square = pl.BlockSpec((rows, BLOCK), lambda k: (0, k))
    column = pltpu.VMEM((rows, 1), F32)
    sems = [pltpu.SemaphoreType.DMA((protos // PIECE,))]
    far = functools.partial(pltpu.with_memory_space_constraint, memory_space=pltpu.HBM)
    student_patches, teacher_patches, mask_order = far(student_patches[0]), far(teacher_patches[0]), far(mask_order)
    student_protos, teacher_protos = far(student_protos), far(teacher_protos)
    dot = 2 * rows * protos * bot

    sent, late, picked = call(
        pick_kernel,
        [((EARLY + MOST, bot), BF16), ((2 * LATE, LANES), BF16), pltpu.HBM((SLOT, bot), BF16)],
        teacher_patches,
        student_patches,
        mask_order,
        counts,
        in_specs=[VMEM, VMEM, VMEM, SMEM],
        moved=4 * patches * bot,
    )
    gathered = lax.all_gather(sent, "proto", axis=0, tiled=False)
    share, teacher_rows, places, near_teacher = call(
        column_kernel,
        [((groups, protos // LANES, LANES), F32), ((rows, bot), BF16), pltpu.HBM((4, width, LANES), F32), near],
        gathered,
        index,
        teacher_protos,
        in_specs=[VMEM, SMEM, HBM],
        scratch=sems,
        flops=dot,
        moved=2 * bot * protos,
    )
    shares = over(share, "dp")
    matrix, high, share = call(
        row_kernel,
        [((rows, protos), BF16), ((steps, rows, 1), F32), ((width, 48, LANES), BF16)],
        shares,
        teacher_rows,
        near_teacher,
        late,
        flops=dot,
        moved=2 * bot * protos + 2 * rows * protos,
    )
    swap = [(p, p ^ 1) for p in range(width)]
    shares = row_shares = over(share, "proto")
    share, scale = call(
        first_column_kernel,
        [
            ((groups, protos // LANES, LANES), BF16),
            ((steps, rows, 1), F32),
        ],
        shares,
        high,
        matrix,
        moved=2 * rows * protos,
    )
    shares = over(share, "dp")
    share = call(
        later_row_kernel,
        [((width, depth, LANES), F32)],
        shares,
        scale,
        matrix,
        moved=2 * rows * protos,
    )[0]
    shares = over(share, "proto")
    share, scale = call(
        later_column_kernel,
        [pltpu.HBM((groups, protos // LANES, LANES), BF16), pltpu.HBM((steps, rows // LANES, LANES), F32)],
        shares,
        scale,
        matrix,
        moved=2 * rows * protos,
    )
    packed = ((width // 2, SLOT, bot), BF16)
    student_own, student_other = call(
        student_kernel,
        [pltpu.HBM(*packed), pltpu.HBM(*packed)],
        far(gathered),
        far(row_shares),
        far(places),
        student_protos,
        grid=grid,
        in_specs=[VMEM, VMEM, VMEM, wide],
        scratch=[pltpu.VMEM((rows, bot), BF16), pltpu.VMEM((rows, bot), F32), column, column],
        flops=2 * dot,
        moved=2 * bot * protos,
    )
    student_came = lax.ppermute(student_other, "proto", swap)
    shares = over(share, "dp")
    shares, student_came = lax.optimization_barrier((shares, student_came))
    own, other = call(
        target_kernel,
        [packed, packed],
        shares,
        far(scale),
        matrix,
        student_protos,
        far(places),
        grid=grid,
        in_specs=[peer, VMEM, VMEM, wide, VMEM],
        scratch=[pltpu.VMEM((rows, bot), F32), column],
        flops=dot,
        moved=2 * rows * protos,
    )
    came = lax.ppermute(other, "proto", swap)
    sent = call(
        merge_kernel, [((width // 2, MOST + SLOT, bot), BF16)], own, came, student_own, student_came
    )[0]
    same_core = [list(range(core, width, 2)) for core in range(2)]
    back = over(sent, "proto", axis_index_groups=same_core)
    student_grad, image_loss = call(
        finish_kernel,
        [((patches, bot), BF16), ((1, 1), F32)],
        back,
        picked,
        mask_order,
        counts,
        in_specs=[VMEM, VMEM, VMEM, SMEM],
        moved=2 * patches * bot,
    )
    return (student_grad[None], image_loss)


def solution(mesh):
    placed = (
        P(("dp", "proto"), None, None),
        P(("dp", "proto"), None, None),
        P(("dp", "proto"), None),
        P("dp", "proto"),
        P(None, "proto"),
        P(None, "proto"),
    )
    return jax.shard_map(
        body,
        mesh=mesh,
        in_specs=placed,
        out_specs=(P(("dp", "proto"), None, None), P("dp", "proto")),
        check_vma=False,
    )
```

```python
import functools

import jax
import jax.numpy as jnp
from jax import lax
from jax.experimental import pallas as pl
from jax.experimental.pallas import tpu as pltpu
from jax.sharding import PartitionSpec as P

MASK_DEV = 24
MOST = 72
EARLY = 54
LATE = MOST - EARLY
UNUSED = 100.0
SLOT = 80
TEACH = 1.0 / 0.07
STUD = 1.0 / 0.1
LOG2E = 1.4426950408889634
F32 = jnp.float32
BF16 = jnp.bfloat16
LANES = 128
BLOCK = 2048
PIECE = 1024
LIMIT = 24 << 20
VMEM = pl.BlockSpec(memory_space=pltpu.VMEM)
SMEM = pl.BlockSpec(memory_space=pltpu.SMEM)


HBM = pl.BlockSpec(memory_space=pl.ANY)


def call(kernel, out_shape, *args, in_specs=None, scratch=(), grid=None, flops=0, moved=0):
    out_shape = [jax.ShapeDtypeStruct(*o) if isinstance(o, tuple) else o for o in out_shape]
    extra = {} if grid is None else {"grid": grid}
    return pl.pallas_call(
        kernel,
        out_shape=out_shape,
        in_specs=[VMEM] * len(args) if in_specs is None else in_specs,
        out_specs=[VMEM] * len(out_shape),
        scratch_shapes=list(scratch),
        compiler_params=pltpu.CompilerParams(vmem_limit_bytes=LIMIT),
        cost_estimate=pl.CostEstimate(flops=flops, bytes_accessed=moved, transcendentals=0),
        **extra,
    )(*args)


def fetch(far_ref, near_ref, sems):
    copies = []
    for k in range(near_ref.shape[1] // PIECE):
        piece = slice(k * PIECE, (k + 1) * PIECE)
        copies.append(pltpu.make_async_copy(far_ref.at[:, piece], near_ref.at[:, piece], sems.at[k]))
        copies[-1].start()

    def block(b):
        for copy in copies[b * BLOCK // PIECE : (b + 1) * BLOCK // PIECE]:
            copy.wait()
        return near_ref[:, b * BLOCK : (b + 1) * BLOCK]

    return block, range(near_ref.shape[1] // BLOCK)


def columns(b):
    return slice(b * BLOCK, (b + 1) * BLOCK)


def lines_of(b):
    return slice(b * BLOCK // LANES, (b + 1) * BLOCK // LANES)


def iota(shape, dim):
    return lax.broadcasted_iota(jnp.int32, shape, dim)


def eye():
    return iota((LANES, LANES), 0) == iota((LANES, LANES), 1)


def to_lanes(column):
    parts = []
    for b in range(column.shape[0] // LANES):
        part = jnp.broadcast_to(column[b * LANES : (b + 1) * LANES], (LANES, LANES))
        parts.append(jnp.sum(jnp.where(eye(), part, 0.0), axis=0, keepdims=True))
    return jnp.concatenate(parts, axis=0)


def to_column(lanes):
    parts = []
    for b in range(lanes.shape[0]):
        part = jnp.broadcast_to(lanes[b : b + 1], (LANES, LANES))
        parts.append(jnp.sum(jnp.where(eye(), part, 0.0), axis=1, keepdims=True))
    return jnp.concatenate(parts, axis=0)


def to_lines(row):
    return jnp.concatenate([row[:, b * LANES : (b + 1) * LANES] for b in range(row.shape[1] // LANES)], axis=0)


def to_row(lines):
    return jnp.concatenate([lines[b : b + 1] for b in range(lines.shape[0])], axis=1)


def merged(shares):
    top = jnp.max(shares, axis=0)
    return top + jnp.log(jnp.sum(jnp.exp(shares - top[None]), axis=0))


def pick_kernel(teacher_ref, student_ref, order_ref, count_ref, sent_ref, late_ref, picked_ref):
    patches, width = teacher_ref.shape
    order = jnp.broadcast_to(order_ref[:, :LANES], (patches, LANES))
    chosen = (iota((patches, LANES), 0) == order).astype(BF16)
    dims = (((0,), (0,)), ((), ()))
    teacher = lax.dot_general(chosen, teacher_ref[...], dims, preferred_element_type=F32)
    student = lax.dot_general(chosen, student_ref[...], dims, preferred_element_type=F32)
    teacher = jnp.where(iota((MOST, width), 0) < count_ref[0, 0], teacher[:MOST], UNUSED)
    sent_ref[...] = jnp.concatenate([teacher, student[:EARLY]], axis=0).astype(BF16)
    late = student[EARLY:MOST]
    late_ref[...] = jnp.concatenate([late[:, :LANES], late[:, LANES:]], axis=0).astype(BF16)
    picked_ref[...] = student[:SLOT].astype(BF16)


def compact(gathered, starts, counts, rows, first, length, shift):
    images, slots, width = gathered.shape
    total = images * slots
    lane, image = iota((images, total), 1), iota((images, total), 0)
    within = lane - image * slots - first
    member = jnp.logical_and(within >= 0, within < length)
    place = (within + shift).astype(F32)
    used = jnp.logical_and(member, place < counts[:, :1])
    row = jnp.sum(jnp.where(used, starts[:, :1] + place + 1.0, 0.0), axis=0, keepdims=True) - 1.0
    chosen = (iota((rows, total), 0).astype(F32) == row).astype(BF16)
    return jnp.dot(chosen, gathered.reshape(total, width), preferred_element_type=F32)


def padded(values):
    images, slots, width = values.shape
    blank = jnp.zeros((images, -slots % 8, width), F32)
    return jnp.concatenate([values, blank], axis=1).astype(BF16)


def spread(starts, counts, slots, rows):
    images = starts.shape[0]
    shape = (images, slots, rows)
    within = iota(shape, 1)
    row = (iota(shape, 2) - within).astype(F32) - starts[:, :1].reshape(images, 1, 1)
    used = jnp.logical_and(row == 0.0, within.astype(F32) < counts[:, :1].reshape(images, 1, 1))
    return used.astype(F32).astype(BF16).reshape(images * slots, rows)


def column_kernel(gathered_ref, index_ref, far_ref, share_ref, rows_ref, places_ref, near_ref, sems):
    block, blocks = fetch(far_ref, near_ref, sems)
    images = gathered_ref.shape[0]
    teacher = gathered_ref[:, :MOST]
    counts = jnp.sum((teacher[:, :, :LANES].astype(F32) < UNUSED / 2).astype(F32), axis=1)
    before = (iota((images, images), 1) < iota((images, images), 0)).astype(BF16)
    starts = jnp.dot(before, counts.astype(BF16), preferred_element_type=F32)
    half, core = images // 2, index_ref[0, 0] % 2
    place = iota((images, images), 0)
    image = jnp.where(place < half, 2 * place + core, 2 * (place - half) + 1 - core)
    other = iota((images, images), 1)
    places_ref[0] = jnp.dot((other < image).astype(BF16), counts.astype(BF16), preferred_element_type=F32)
    places_ref[1] = jnp.dot((other == image).astype(BF16), counts.astype(BF16), preferred_element_type=F32)
    places_ref[2] = starts
    places_ref[3] = counts
    rows = compact(teacher, starts, counts, rows_ref.shape[0], 0, MOST, 0).astype(BF16)
    rows_ref[...] = rows
    for b in blocks:
        products = jnp.dot(rows, block(b), preferred_element_type=F32)
        high = jnp.max(products, axis=0, keepdims=True)
        total = jnp.sum(jnp.exp2((products - high) * (TEACH * LOG2E)), axis=0, keepdims=True)
        lines = to_lines(high * TEACH + jnp.log(total))
        share_ref[:, lines_of(b)] = jnp.broadcast_to(lines[None], (share_ref.shape[0],) + lines.shape)


def split(values, parts):
    out = []
    for _ in range(parts):
        part = values.astype(BF16)
        out.append(part)
        values = values - part.astype(F32)
    return out


def fill_share(share_ref, lines):
    blank = jnp.zeros((share_ref.shape[1] - lines.shape[0], LANES), F32)
    share_ref[...] = jnp.broadcast_to(jnp.concatenate([lines, blank], axis=0)[None], share_ref.shape)


def row_kernel(shares_ref, rows_ref, protos_ref, late_ref, matrix_ref, high_ref, share_ref):
    column = merged(shares_ref[...])
    rows = rows_ref[...]
    highs, sums = [], []
    for b in range(high_ref.shape[0]):
        products = jnp.dot(rows, protos_ref[:, columns(b)], preferred_element_type=F32)
        shifted = products * (TEACH * LOG2E) - to_row(column[lines_of(b)] * LOG2E)
        high = jnp.max(shifted, axis=1, keepdims=True)
        exact = jnp.exp2(shifted - high)
        high = high * (1.0 / LOG2E)
        matrix_ref[:, columns(b)] = exact.astype(BF16)
        high_ref[b] = high
        highs.append(high)
        sums.append(jnp.sum(exact, axis=1, keepdims=True))
    top = functools.reduce(jnp.maximum, highs)
    total = sum(jnp.exp(high - top) * part for high, part in zip(highs, sums))
    own = jnp.concatenate([part.astype(F32) for part in split(to_lanes(top + jnp.log(total)), 3)], axis=0)
    blank = jnp.zeros((share_ref.shape[1] - 2 * LATE - own.shape[0], LANES), F32)
    chunk = jnp.concatenate([late_ref[...].astype(F32), own, blank], axis=0).astype(BF16)
    share_ref[...] = jnp.broadcast_to(chunk[None], share_ref.shape)


def column_sums(matrix_ref, scale, share_ref):
    for b in range(scale.shape[0]):
        sums = jnp.sum(matrix_ref[:, columns(b)].astype(F32) * scale[b], axis=0, keepdims=True)
        lines = to_lines(sums)
        shape = (share_ref.shape[0],) + lines.shape
        share_ref[:, lines_of(b)] = jnp.broadcast_to(lines[None], shape).astype(share_ref.dtype)


def first_column_kernel(shares_ref, high_ref, matrix_ref, share_ref, scale_ref):
    lines = scale_ref.shape[1] // LANES
    numbers = shares_ref[...].astype(F32)[:, 2 * LATE :]
    row_lse = merged(sum(numbers[:, k * lines : (k + 1) * lines] for k in range(3)))
    scale = jnp.exp(high_ref[...] - to_column(row_lse)[None])
    scale_ref[...] = scale
    column_sums(matrix_ref, scale, share_ref)


def later_column_kernel(shares_ref, scale_in_ref, matrix_ref, share_ref, scale_ref):
    lines = scale_in_ref.shape[1] // LANES
    total = to_column(jnp.sum(shares_ref[...][:, :lines], axis=0))
    scale = scale_in_ref[...] / total[None]
    for b in range(scale.shape[0]):
        scale_ref[b] = to_lanes(scale[b])
    column_sums(matrix_ref, scale, share_ref)


def inverse_of(shares_ref):
    return 1.0 / jnp.sum(shares_ref[...].astype(F32), axis=0)


def later_row_kernel(shares_ref, scale_ref, matrix_ref, share_ref):
    inverse = inverse_of(shares_ref)
    sums = 0.0
    for b in range(scale_ref.shape[0]):
        scaled = matrix_ref[:, columns(b)].astype(F32) * to_row(inverse[lines_of(b)])
        sums += scale_ref[b] * jnp.sum(scaled, axis=1, keepdims=True)
    fill_share(share_ref, to_lanes(sums))


def pack(sums, numbers, parts, starts, counts):
    rows, width = sums.shape
    images = starts.shape[0]
    chosen = spread(starts, counts, SLOT, rows)
    packed = jnp.dot(chosen, sums.astype(BF16), preferred_element_type=F32).astype(BF16)
    row = split(to_row(to_lanes(numbers)), parts)
    row = jnp.concatenate([part.astype(F32) for part in row] + [jnp.zeros((SLOT - MOST - parts, rows), F32)], axis=0)
    tail = lax.dot_general(row.astype(BF16), chosen, (((1,), (1,)), ((), ())), preferred_element_type=F32)
    tail = jnp.concatenate([tail, jnp.zeros((SLOT - MOST, LANES), F32)], axis=1)
    blank = jnp.zeros((SLOT - MOST, width - LANES), F32)
    tail = [jnp.concatenate([tail[:, j * SLOT : j * SLOT + LANES], blank], axis=1)[None] for j in range(images)]
    return packed.reshape(images, SLOT, width)[:, :MOST], jnp.concatenate(tail, axis=0).astype(BF16)


def join(tail, width):
    images = tail[0].shape[0]
    filler = jnp.zeros((images, 1, width - LANES), F32)
    rows = [jnp.concatenate([part.astype(F32), filler], axis=2) for part in tail]
    rows.append(jnp.zeros((images, SLOT - MOST - len(tail), width), F32))
    return jnp.concatenate(rows, axis=1).astype(BF16)


def numbers_of(chunk, parts):
    tail = chunk[:, MOST:SLOT, :LANES].astype(F32)
    return sum(tail[:, k] for k in range(parts))


def put(own_ref, other_ref, rows, tail):
    half = own_ref.shape[0]
    own_ref[:, :MOST], own_ref[:, MOST:] = rows[:half], tail[:half]
    other_ref[:, :MOST], other_ref[:, MOST:] = rows[half:], tail[half:]


def slots_of(lanes):
    images = lanes.shape[0]
    same = iota((1, MOST, LANES), 1) == iota((1, MOST, LANES), 2)
    return jnp.sum(jnp.where(same, lanes.reshape(images, 1, LANES), 0.0), axis=2, keepdims=True)


def target_kernel(shares_ref, scale_ref, matrix_ref, protos_ref, places_ref, own_ref, other_ref, sums, total):
    step = pl.program_id(0)
    scale = to_column(scale_ref[step])
    here = pl.ds(pl.multiple_of(step * BLOCK, BLOCK), BLOCK)
    weights = matrix_ref[:, here].astype(F32) * to_row(inverse_of(shares_ref))
    narrow = weights.astype(BF16)
    part = scale * lax.dot_general(narrow, protos_ref[...], (((1,), (1,)), ((), ())), preferred_element_type=F32)
    mass = scale * jnp.sum(weights, axis=1, keepdims=True)

    @pl.when(step == 0)
    def _():
        sums[...] = part
        total[...] = mass

    @pl.when(step > 0)
    def _():
        sums[...] += part
        total[...] += mass

    @pl.when(step == pl.num_programs(0) - 1)
    def _():
        put(own_ref, other_ref, *pack(sums[...], total[...], 2, places_ref[0], places_ref[1]))


def merge_kernel(own_ref, came_ref, student_own_ref, student_came_ref, out_ref):
    width = own_ref.shape[2]
    out_ref[:, :MOST] = (own_ref[:, :MOST].astype(F32) + came_ref[:, :MOST].astype(F32)).astype(BF16)
    total = numbers_of(own_ref, 2) + numbers_of(came_ref, 2)
    own, came = numbers_of(student_own_ref, 3), numbers_of(student_came_ref, 3)
    high = jnp.maximum(own, came)
    joint = high + jnp.log(jnp.exp(own - high) + jnp.exp(came - high))
    mean = student_own_ref[:, :MOST].astype(F32) * slots_of(jnp.exp(own - joint))
    mean = mean + student_came_ref[:, :MOST].astype(F32) * slots_of(jnp.exp(came - joint))
    out_ref[:, MOST : 2 * MOST] = mean.astype(BF16)
    out_ref[:, 2 * MOST :] = join([part[:, None] for part in split(total, 2) + split(joint, 3)], width)


def student_kernel(
    gathered_ref, shares_ref, places_ref, protos_ref, own_ref, other_ref, rows_ref, sums, top, total
):
    step = pl.program_id(0)

    @pl.when(step == 0)
    def _():
        starts, counts, rows = places_ref[2], places_ref[3], rows_ref.shape[0]
        late = shares_ref[...].astype(F32)
        late = jnp.concatenate([late[:, :LATE], late[:, LATE : 2 * LATE]], axis=2)
        early = gathered_ref[:, MOST:].astype(F32)
        found = compact(padded(early), starts, counts, rows, 0, EARLY, 0)
        found += compact(padded(late), starts, counts, rows, 0, LATE, EARLY)
        rows_ref[...] = found.astype(BF16)
        top[...] = jnp.full(top.shape, -1e30, F32)
        total[...] = jnp.zeros(total.shape, F32)
        sums[...] = jnp.zeros(sums.shape, F32)

    protos = protos_ref[...]
    products = jnp.dot(rows_ref[...], protos, preferred_element_type=F32)
    before = top[...]
    high = jnp.maximum(before, jnp.max(products, axis=1, keepdims=True))
    shrink = jnp.exp2((before - high) * (STUD * LOG2E))
    exact = jnp.exp2((products - high) * (STUD * LOG2E))
    total[...] = total[...] * shrink + jnp.sum(exact, axis=1, keepdims=True)
    part = lax.dot_general(exact.astype(BF16), protos, (((1,), (1,)), ((), ())), preferred_element_type=F32)
    sums[...] = sums[...] * shrink + part
    top[...] = high

    @pl.when(step == pl.num_programs(0) - 1)
    def _():
        mean, own_lse = sums[...] / total[...], top[...] * STUD + jnp.log(total[...])
        put(own_ref, other_ref, *pack(mean, own_lse, 3, places_ref[0], places_ref[1]))


def blend(chunk, lse):
    joint = merged(lse)
    weights = slots_of(jnp.exp(lse - joint[None]))
    return jnp.sum(chunk * weights, axis=0), joint


def finish_kernel(back_ref, picked_ref, order_ref, count_ref, grad_ref, loss_ref):
    patches, width = grad_ref.shape
    target = jnp.sum(back_ref[:, :MOST].astype(F32), axis=0)
    tail = back_ref[:, 2 * MOST :, :LANES].astype(F32)
    mass = to_column(jnp.sum(tail[:, 0] + tail[:, 1], axis=0, keepdims=True))[:MOST]
    soft, lse_lanes = blend(back_ref[:, MOST : 2 * MOST].astype(F32), tail[:, 2] + tail[:, 3] + tail[:, 4])
    used = iota((MOST, 1), 0) < count_ref[0, 0]
    mean = target / jnp.where(used, mass, 1.0)
    own_lse = to_column(lse_lanes.reshape(1, LANES))[:MOST]
    cross = own_lse - STUD * jnp.sum(picked_ref[:MOST].astype(F32) * mean, axis=1, keepdims=True)
    cross = jnp.sum(jnp.where(used, cross, 0.0), axis=0, keepdims=True)
    loss_ref[...] = cross / jnp.full((1, 1), count_ref[0, 0], jnp.int32).astype(F32)
    rows = jnp.where(used, STUD * (soft - mean), 0.0)
    rows = jnp.concatenate([rows, jnp.zeros((LANES - MOST, width), F32)], axis=0).astype(BF16)
    order = jnp.broadcast_to(order_ref[:, :LANES], (patches, LANES))
    chosen = (iota((patches, LANES), 0) == order).astype(BF16)
    grad_ref[...] = jnp.dot(chosen, rows, preferred_element_type=F32).astype(BF16)


def body(student_patches, teacher_patches, mask_order, counts, student_protos, teacher_protos):
    width = lax.axis_size("proto")
    groups = lax.axis_size("dp")
    rows = MASK_DEV * width
    lines = rows // LANES
    patches, bot = student_patches.shape[1:]
    protos = student_protos.shape[1]
    steps = protos // BLOCK
    depth = 8
    index = lax.axis_index("proto").astype(jnp.int32).reshape(1, 1)
    over = functools.partial(lax.all_to_all, split_axis=0, concat_axis=0, tiled=True)
    near = ((bot, protos), BF16)
    grid = (steps,)
    wide = pl.BlockSpec((bot, BLOCK), lambda k: (0, k))
    peer = pl.BlockSpec((groups, BLOCK // LANES, LANES), lambda k: (0, k, 0))
    square = pl.BlockSpec((rows, BLOCK), lambda k: (0, k))
    column = pltpu.VMEM((rows, 1), F32)
    sems = [pltpu.SemaphoreType.DMA((protos // PIECE,))]
    far = functools.partial(pltpu.with_memory_space_constraint, memory_space=pltpu.HBM)
    near_order = mask_order
    student_patches, teacher_patches, mask_order = far(student_patches[0]), far(teacher_patches[0]), far(mask_order)
    student_protos, teacher_protos = far(student_protos), far(teacher_protos)
    dot = 2 * rows * protos * bot

    sent, late, picked = call(
        pick_kernel,
        [((EARLY + MOST, bot), BF16), ((2 * LATE, LANES), BF16), pltpu.HBM((SLOT, bot), BF16)],
        teacher_patches,
        student_patches,
        mask_order,
        counts,
        in_specs=[VMEM, VMEM, VMEM, SMEM],
        moved=4 * patches * bot,
    )
    gathered = lax.all_gather(sent, "proto", axis=0, tiled=False)
    share, teacher_rows, places, near_teacher = call(
        column_kernel,
        [((groups, protos // LANES, LANES), F32), ((rows, bot), BF16), pltpu.HBM((4, width, LANES), F32), near],
        gathered,
        index,
        teacher_protos,
        in_specs=[VMEM, SMEM, HBM],
        scratch=sems,
        flops=dot,
        moved=2 * bot * protos,
    )
    shares = over(share, "dp")
    matrix, high, share = call(
        row_kernel,
        [((rows, protos), BF16), ((steps, rows, 1), F32), ((width, 48, LANES), BF16)],
        shares,
        teacher_rows,
        near_teacher,
        late,
        flops=dot,
        moved=2 * bot * protos + 2 * rows * protos,
    )
    swap = [(p, p ^ 1) for p in range(width)]
    shares = row_shares = over(share, "proto")
    share, scale = call(
        first_column_kernel,
        [
            ((groups, protos // LANES, LANES), BF16),
            ((steps, rows, 1), F32),
        ],
        shares,
        high,
        matrix,
        moved=2 * rows * protos,
    )
    shares = over(share, "dp")
    share = call(
        later_row_kernel,
        [((width, depth, LANES), F32)],
        shares,
        scale,
        matrix,
        moved=2 * rows * protos,
    )[0]
    shares = over(share, "proto")
    share, scale = call(
        later_column_kernel,
        [pltpu.HBM((groups, protos // LANES, LANES), BF16), pltpu.HBM((steps, rows // LANES, LANES), F32)],
        shares,
        scale,
        matrix,
        moved=2 * rows * protos,
    )
    packed = ((width // 2, SLOT, bot), BF16)
    student_own, student_other = call(
        student_kernel,
        [pltpu.HBM(*packed), pltpu.HBM(*packed)],
        far(gathered),
        far(row_shares),
        far(places),
        student_protos,
        grid=grid,
        in_specs=[VMEM, VMEM, VMEM, wide],
        scratch=[pltpu.VMEM((rows, bot), BF16), pltpu.VMEM((rows, bot), F32), column, column],
        flops=2 * dot,
        moved=2 * bot * protos,
    )
    student_came = lax.ppermute(student_other, "proto", swap)
    shares = over(share, "dp")
    shares, student_came = lax.optimization_barrier((shares, student_came))
    own, other = call(
        target_kernel,
        [packed, packed],
        shares,
        far(scale),
        matrix,
        student_protos,
        far(places),
        grid=grid,
        in_specs=[peer, VMEM, VMEM, wide, VMEM],
        scratch=[pltpu.VMEM((rows, bot), F32), column],
        flops=dot,
        moved=2 * rows * protos,
    )
    came = lax.ppermute(other, "proto", swap)
    sent = call(
        merge_kernel, [((width // 2, MOST + SLOT, bot), BF16)], own, came, student_own, student_came
    )[0]
    same_core = [list(range(core, width, 2)) for core in range(2)]
    back = over(sent, "proto", axis_index_groups=same_core)
    student_grad, image_loss = call(
        finish_kernel,
        [((patches, bot), BF16), ((1, 1), F32)],
        back,
        picked,
        near_order,
        counts,
        in_specs=[VMEM, VMEM, VMEM, SMEM],
        moved=2 * patches * bot,
    )
    return (student_grad[None], image_loss)


def solution(mesh):
    placed = (
        P(("dp", "proto"), None, None),
        P(("dp", "proto"), None, None),
        P(("dp", "proto"), None),
        P("dp", "proto"),
        P(None, "proto"),
        P(None, "proto"),
    )
    return jax.shard_map(
        body,
        mesh=mesh,
        in_specs=placed,
        out_specs=(P(("dp", "proto"), None, None), P("dp", "proto")),
        check_vma=False,
    )
```
